128 devices in a mesh: dp: 32 (over y, z, core), ctx: 4 (over x).
Axes of the slice: x: 4, y: 4, z: 4, core: 2. Of those that a mesh axis runs over, the one named last changes fastest.
Arguments:
- char_ids: int32 [16384, 50], P(('dp', 'ctx')), may hold values from 0 to 261
- word_lengths: int32 [16384], P(('dp', 'ctx')), may hold values from 1 to 50, as said below
- word_home: int32 [16384], P(('dp', 'ctx')), may hold values from 0 to 16383, as said below
- seq_lengths: int32 [32], P('dp'), may hold values from 385 to 512, as said below
- char_table: bfloat16 [262, 16], replicated, may hold values from -6 to 6
- conv_weight: bfloat16 [112, 2048], replicated, may hold values from -0.75 to 0.75
- conv_bias: bfloat16 [2048], replicated, may hold values from -3 to 3
- highway_weight: bfloat16 [1, 2048, 4096], replicated, may hold values from -0.125 to 0.125
- highway_bias: bfloat16 [1, 4096], replicated, may hold values from -3 to 3
- proj_weight: bfloat16 [2048, 768], replicated, may hold values from -0.125 to 0.125
- norm_gain: bfloat16 [3, 768], replicated, may hold values from 0.099609375 to 1.8984375
- norm_shift: bfloat16 [3, 768], replicated, may hold values from -2 to 2
- qkv_weight: bfloat16 [768, 2304], replicated, may hold values from -0.21875 to 0.21875
- out_weight: bfloat16 [768, 768], replicated, may hold values from -1.75 to 1.75
- up_weight: bfloat16 [768, 3072], replicated, may hold values from -0.21875 to 0.21875
- down_weight: bfloat16 [3072, 768], replicated, may hold values from -0.109375 to 0.109375
- cotangent: bfloat16 [32, 512, 768], P('dp', 'ctx'), may hold values from -6 to 6
Outputs:
- out_hidden: bfloat16 [32, 512, 768], P('dp', 'ctx')
- grad_char_table: float32 [262, 16], replicated
- grad_conv_weight: float32 [112, 2048], P(None, ('dp', 'ctx'))
- grad_conv_bias: float32 [2048], replicated
- grad_highway_weight: float32 [1, 2048, 4096], P(None, ('dp', 'ctx'))
- grad_highway_bias: float32 [1, 4096], replicated
- grad_proj_weight: float32 [2048, 768], P(('dp', 'ctx'))
- grad_norm_gain: float32 [3, 768], replicated
- grad_norm_shift: float32 [3, 768], replicated
- grad_qkv_weight: float32 [768, 2304], P(('dp', 'ctx'))
- grad_out_weight: float32 [768, 768], P(('dp', 'ctx'))
- grad_up_weight: float32 [768, 3072], P(('dp', 'ctx'))
- grad_down_weight: float32 [3072, 768], P(('dp', 'ctx'))
The draws below stay inside these ranges and needn't reach their ends.
Inputs may be any that keep to these rules, and one draw needn't show every extreme that they name: A word's characters are its first word_lengths slots; later slots hold ids that are ignored. Some word has 50 characters. word_home is a permutation. A device's block is the words that out_hidden's layout puts on it; the 128 rows of each device hold exactly 1 words of every device's block. `seq_lengths`: some sequence has length 512.
All inputs are finite; a program needn't handle non-finite values.
Results may differ from the reference program's by a relative error of at most 0.02.
Values may be sent and summed in bfloat16 or wider, within the bound.
A program may use at most 256 MiB of HBM per device.

```python
import math
import jax
import jax.numpy as jnp
import numpy as np
from jax import lax

D = 768
FF = 3072
HEADS = 12
HEAD_DIM = 64
FILTERS = 2048
CHAR_DIM = 16
CHARS = 262
WORD_CHARS = 50
TAPS = 7
HIGHWAY = 1
SEQ_LEN = 512
SEQ_DEV = 1
SEQS = 32
GROUP = 128
WORDS_DEV = 128
WORDS_TOTAL = 16384
PER_PEER = 1
N_CTX = 4


def draw_word_lengths(key, part):
    key = jax.random.fold_in(key, 12)
    exp_key, span_key, place_key = jax.random.split(key, 3)
    power_exp = jax.random.randint(exp_key, (WORDS_TOTAL,), 0, 7)
    spread = jnp.left_shift(jnp.ones_like(power_exp), power_exp)
    extra_chars = jax.random.randint(span_key, (WORDS_TOTAL,), 0, 64) % spread
    lengths = jnp.minimum(extra_chars + 1, WORD_CHARS)
    longest = jax.random.randint(place_key, (), 0, WORDS_TOTAL)
    return lengths.at[longest].set(WORD_CHARS).astype(jnp.int32)


def draw_word_home(key, part):
    key = jax.random.fold_in(key, 11)
    first_key, second_key = jax.random.split(key)
    device_count = WORDS_TOTAL // WORDS_DEV
    dest_index = jnp.arange(device_count)
    slot_index = jnp.arange(WORDS_DEV)
    seq_index = (dest_index // N_CTX)[:, None] * SEQ_DEV + (slot_index // GROUP)[None, :]
    pos_index = (dest_index % N_CTX)[:, None] * GROUP + (slot_index % GROUP)[None, :]
    word_index = (seq_index * SEQ_LEN + pos_index).astype(jnp.int32)
    word_index = jax.random.permutation(first_key, word_index, axis=1, independent=True)
    word_index = word_index.reshape(device_count, device_count, PER_PEER).transpose(1, 0, 2).reshape(device_count, WORDS_DEV)
    word_index = jax.random.permutation(second_key, word_index, axis=1, independent=True)
    return word_index.reshape(WORDS_TOTAL).astype(jnp.int32)


def draw_seq_lengths(key, part):
    key = jax.random.fold_in(key, 13)
    len_key, place_key = jax.random.split(key)
    lengths = jax.random.randint(len_key, (SEQS,), SEQ_LEN - GROUP + 1, SEQ_LEN + 1)
    fullest = jax.random.randint(place_key, (), 0, SEQS)
    return lengths.at[fullest].set(SEQ_LEN).astype(jnp.int32)


def touch_ends(result, rng, low, largest):
    longest = result.shape.index(max(result.shape))
    spots = []
    for shift in (0, 1):
        where = [jax.random.randint(jax.random.fold_in(rng, axis), (), 0, length) for axis, length in enumerate(result.shape)]
        where[longest] = (where[longest] + shift) % result.shape[longest]
        spots.append(tuple(where))
    return result.at[spots[0]].set(low).at[spots[1]].set(largest)


def steps_of(rng, dims, pieces, least, top_value):
    factor_of = 1.0
    for position, shards_of in pieces:
        draws = jax.random.uniform(jax.random.fold_in(jax.random.fold_in(rng, 6), position), (shards_of,), jnp.float32, least / len(pieces), top_value / len(pieces))
        factor_of = factor_of * jnp.repeat(jnp.exp(draws), dims[position] // shards_of).reshape((-1,) + (1,) * (len(dims) - 1 - position))
    return factor_of


def rank_bounds(count, lean):
    loads = [(1 << 20) // math.isqrt(grade ** lean) + 1 for grade in range(1, count + 1)]
    scale = 1 + sum(loads) // (1 << 30)
    return np.cumsum(np.array([max(1, weight // scale) for weight in loads]))


def skewed_ids(key, shape, amount, skew):
    listing = rank_bounds(amount, skew)
    lot = jax.random.randint(jax.random.fold_in(key, 1), shape, 0, int(listing[amount - 1]))
    grade = jnp.searchsorted(jnp.asarray(listing, jnp.int32), lot, side="right")
    return jax.random.permutation(jax.random.fold_in(key, 2), amount)[grade].astype(jnp.int32)


def normal_values(own_key, dims, scale, bound, cuts=(), held_as=jnp.bfloat16):
    drawn = jax.random.normal(own_key, dims, jnp.float32) * scale
    if len(cuts) > 0:
        drawn = steps_of(own_key, dims, cuts, -0.22, 0.18) * drawn
    return jnp.clip(drawn, min=-bound, max=bound).astype(held_as)


def setup_inputs(seed: int = 0) -> dict:
    key_list = jax.random.split(jax.random.key(seed), 18)
    return {
        "char_ids": touch_ends(skewed_ids(key_list[0], (WORDS_TOTAL, WORD_CHARS), CHARS, 2), jax.random.fold_in(key_list[0], 3), 0, CHARS - 1).astype(jnp.int32),
        "word_lengths": draw_word_lengths(jax.random.fold_in(key_list[17], 71), 0),
        "word_home": draw_word_home(jax.random.fold_in(key_list[17], 71), 0),
        "seq_lengths": draw_seq_lengths(jax.random.fold_in(key_list[17], 71), 0),
        "char_table": normal_values(key_list[4], (CHARS, CHAR_DIM), 1.0, 6.0),
        "conv_weight": normal_values(key_list[5], (TAPS * CHAR_DIM, FILTERS), 64 ** -0.5, 0.75),
        "conv_bias": normal_values(key_list[6], (FILTERS,), 0.5, 3.0),
        "highway_weight": normal_values(key_list[7], (HIGHWAY, FILTERS, 2 * FILTERS), FILTERS ** -0.5, 0.125),
        "highway_bias": normal_values(key_list[8], (HIGHWAY, 2 * FILTERS), 0.5, 3.0),
        "proj_weight": normal_values(key_list[9], (FILTERS, D), FILTERS ** -0.5, 0.125),
        "norm_gain": jnp.clip(1.0 + 0.18 * jax.random.normal(key_list[10], (3, D), jnp.float32), 0.099609375, 1.8984375).astype(jnp.bfloat16),
        "norm_shift": normal_values(key_list[11], (3, D), 0.3, 2.0),
        "qkv_weight": normal_values(key_list[12], (D, 3 * D), D ** -0.5, 0.21875),
        "out_weight": normal_values(key_list[13], (D, D), (D // 64) ** -0.5, 1.75),
        "up_weight": normal_values(key_list[14], (D, FF), D ** -0.5, 0.21875),
        "down_weight": normal_values(key_list[15], (FF, D), FF ** -0.5, 0.109375),
        "cotangent": normal_values(key_list[16], (SEQS, SEQ_LEN, D), 1.0, 6.0, ((0, 32), (1, 4))),
    }


EPSILON = 1e-05
NEG_LARGE = -1e+30
HIGHEST = lax.Precision.HIGHEST

@jax.custom_vjp
def low(v):
    return lax.optimization_barrier(v.astype(jnp.bfloat16)).astype(jnp.float32)

@jax.custom_vjp
def low_back(v):
    return v

def low_keep(v):
    return (low(v), None)

def low_pass(kept, grad):
    return (grad,)

def back_keep(v):
    return (v, None)

def back_low(kept, grad):
    return (low(grad),)
low.defvjp(low_keep, low_pass)
low_back.defvjp(back_keep, back_low)

def filter_widths():
    unit_count = FILTERS // 64
    filter_index = jnp.arange(FILTERS)
    widths = jnp.ones((FILTERS,), jnp.int32)
    for bound_units in (1, 2, 4, 8, 16, 32):
        widths = widths + (filter_index >= unit_count * bound_units).astype(jnp.int32)
    return widths

def tap_mask():
    tap_rows = jnp.arange(TAPS * CHAR_DIM) // CHAR_DIM
    return tap_rows[:, None] < filter_widths()[None, :]

def layer_norm(values_in, gain_row, shift_row):
    mean_val = lax.optimization_barrier(jnp.mean(values_in, -1, keepdims=True))
    centred = values_in - mean_val
    return centred * lax.rsqrt(lax.optimization_barrier(jnp.mean(centred * centred, -1, keepdims=True)) + EPSILON) * gain_row + shift_row

def embed_words(char_ids, word_lens, char_table, conv_masked, conv_bias, highway_weight, highway_bias, proj_weight):
    present = jnp.arange(WORD_CHARS)[None, :] < word_lens[:, None]
    char_vals = jnp.where(present[:, :, None], jnp.take(char_table, char_ids, axis=0), 0.0)
    padded = jnp.pad(char_vals, ((0, 0), (0, TAPS - 1), (0, 0)))
    unfolded = low(jnp.concatenate([padded[:, tap_index:tap_index + WORD_CHARS, :] for tap_index in range(TAPS)], axis=-1))
    conv_rows = low_back(jnp.einsum('bpc,cf->bpf', unfolded, conv_masked, precision=HIGHEST) + conv_bias)
    masked = jnp.where(present[:, :, None], conv_rows, NEG_LARGE)
    top_val = lax.optimization_barrier(jnp.max(masked, axis=1, keepdims=True))
    totals = lax.optimization_barrier(jnp.sum(jnp.where(present[:, :, None], jnp.exp(masked - top_val), 0.0), axis=1))
    pooled = top_val[:, 0, :] + jnp.log(totals)
    current = low(jax.nn.gelu(pooled))
    for depth_index in range(HIGHWAY):
        mixed_rows = low_back(jnp.dot(current, highway_weight[depth_index], precision=HIGHEST) + highway_bias[depth_index])
        carry_gate = jax.nn.sigmoid(mixed_rows[:, FILTERS:])
        current = low(carry_gate * current + (1.0 - carry_gate) * jax.nn.gelu(mixed_rows[:, :FILTERS]))
    return low(low_back(jnp.dot(current, proj_weight, precision=HIGHEST)))

def encode(word_rows, length, gain_rows, shift_rows, qkv_weight, out_weight, up_weight, down_weight):
    first_norm = low(layer_norm(word_rows, gain_rows[0], shift_rows[0]))
    joint_proj = low(low_back(jnp.dot(first_norm, qkv_weight, precision=HIGHEST)))
    queries = joint_proj[:, :D].reshape(SEQ_LEN, HEADS, HEAD_DIM)
    key_rows = joint_proj[:, D:2 * D].reshape(SEQ_LEN, HEADS, HEAD_DIM)
    value_rows = joint_proj[:, 2 * D:].reshape(SEQ_LEN, HEADS, HEAD_DIM)
    scores = low_back(jnp.einsum('qhd,khd->hqk', queries, key_rows, precision=HIGHEST) * HEAD_DIM ** (-0.5))
    key_valid = jnp.arange(SEQ_LEN) < length
    attn_probs = low(jax.nn.softmax(jnp.where(key_valid[None, None, :], scores, NEG_LARGE), axis=-1))
    context = low(low_back(jnp.einsum('hqk,khd->qhd', attn_probs, value_rows, precision=HIGHEST).reshape(SEQ_LEN, D)))
    attn_out = low_back(jnp.dot(context, out_weight, precision=HIGHEST))
    middle = low(layer_norm(first_norm + attn_out, gain_rows[1], shift_rows[1]))
    up_proj = low_back(jnp.dot(middle, up_weight, precision=HIGHEST))
    hidden_act = low(jax.nn.gelu(up_proj))
    down_proj = low_back(jnp.dot(hidden_act, down_weight, precision=HIGHEST))
    return layer_norm(middle + down_proj, gain_rows[2], shift_rows[2])

def reference(char_ids, word_lengths, word_home, seq_lengths, char_table, conv_weight, conv_bias, highway_weight, highway_bias, proj_weight, norm_gain, norm_shift, qkv_weight, out_weight, up_weight, down_weight, cotangent):
    source_row = jnp.argsort(word_home).astype(jnp.int32)
    taps_on = tap_mask().astype(jnp.float32)
    block_words = 256
    id_blocks = char_ids.reshape(WORDS_TOTAL // block_words, block_words, WORD_CHARS)
    len_blocks = word_lengths.reshape(WORDS_TOTAL // block_words, block_words)

    def forward(table_f, conv_f, conv_bias_f, high_f, high_bias_f, proj_f, gain_f, shift_f, qkv_f, out_f, up_f, down_f):
        conv_masked = conv_f * taps_on

        def embed_block(packed):
            return embed_words(packed[0], packed[1], table_f, conv_masked, conv_bias_f, high_f, high_bias_f, proj_f)
        embedded = lax.map(jax.checkpoint(embed_block), (id_blocks, len_blocks)).reshape(WORDS_TOTAL, D)
        ordered = jnp.take(embedded, source_row, axis=0).reshape(SEQS, SEQ_LEN, D)

        def encode_one(packed):
            return encode(packed[0], packed[1], gain_f, shift_f, qkv_f, out_f, up_f, down_f)
        return lax.map(jax.checkpoint(encode_one), (ordered, seq_lengths))
    output_rows, pullback = jax.vjp(forward, char_table.astype(jnp.float32), conv_weight.astype(jnp.float32), conv_bias.astype(jnp.float32), highway_weight.astype(jnp.float32), highway_bias.astype(jnp.float32), proj_weight.astype(jnp.float32), norm_gain.astype(jnp.float32), norm_shift.astype(jnp.float32), qkv_weight.astype(jnp.float32), out_weight.astype(jnp.float32), up_weight.astype(jnp.float32), down_weight.astype(jnp.float32))
    g_table, g_conv, g_conv_bias, g_high, g_high_bias, g_proj, g_gain, g_shift, g_qkv, g_out, g_up, g_down = pullback(cotangent.astype(jnp.float32))
    return (output_rows.astype(jnp.bfloat16), g_table.astype(jnp.float32), g_conv.astype(jnp.float32), g_conv_bias.astype(jnp.float32), g_high.astype(jnp.float32), g_high_bias.astype(jnp.float32), g_proj.astype(jnp.float32), g_gain.astype(jnp.float32), g_shift.astype(jnp.float32), g_qkv.astype(jnp.float32), g_out.astype(jnp.float32), g_up.astype(jnp.float32), g_down.astype(jnp.float32))
```

```python
import functools
import jax
import jax.numpy as jnp
from jax import lax
from jax.experimental import pallas as pl
from jax.experimental.pallas import tpu as pltpu
from jax.sharding import PartitionSpec as P

D = 768
FF = 3072
HEADS = 12
HEAD_DIM = 64
FILTERS = 2048
CHAR_DIM = 16
CHARS = 262
WORD_CHARS = 50
TAPS = 7
SEQ_LEN = 512
WORDS = 128

EPSILON = 1e-05
NEG_LARGE = -1e30
MESH = pl.DeviceIdType.MESH
BF16 = jnp.bfloat16
F32 = jnp.float32

BIAS_ROW = TAPS * CHAR_DIM
ABSENT_ROW = BIAS_ROW + 1
CHAR_ROWS = 272


def filter_widths():
    unit_count = FILTERS // 64
    filter_index = jnp.arange(FILTERS)
    widths = jnp.ones((FILTERS,), jnp.int32)
    for bound_units in (1, 2, 4, 8, 16, 32):
        widths = widths + (filter_index >= unit_count * bound_units).astype(jnp.int32)
    return widths


def tap_mask():
    tap_rows = jnp.arange(TAPS * CHAR_DIM) // CHAR_DIM
    return tap_rows[:, None] < filter_widths()[None, :]


def gate_mix(current, mixed_rows):
    carry_gate = jax.nn.sigmoid(mixed_rows[:, FILTERS:])
    return carry_gate * current + (1.0 - carry_gate) * jax.nn.gelu(mixed_rows[:, :FILTERS])


def norm_parts(values_in, gain_row, shift_row):
    mean_val = jnp.mean(values_in, -1, keepdims=True)
    centred = values_in - mean_val
    inverse = lax.rsqrt(jnp.mean(centred * centred, -1, keepdims=True) + EPSILON)
    normal = centred * inverse
    return (normal * gain_row + shift_row, normal, inverse)


def norm_back(grad_out, normal, inverse, gain_row):
    scaled = grad_out * gain_row
    grad_in = inverse * (
        scaled
        - jnp.mean(scaled, -1, keepdims=True)
        - normal * jnp.mean(scaled * normal, -1, keepdims=True)
    )
    return (grad_in, jnp.sum(grad_out * normal, 0), jnp.sum(grad_out, 0))


def dot(left, right):
    return jnp.dot(left, right, preferred_element_type=F32)


def back_dot(rows_in, weight_rows):
    return lax.dot_general(
        rows_in, weight_rows, (((1,), (1,)), ((), ())), preferred_element_type=F32
    )


def first_dot(left, right):
    return lax.dot_general(left, right, (((0,), (0,)), ((), ())), preferred_element_type=F32)


POOL_COLS = 256


def pool_kernel(ids_ref, table_ref, weight_ref, act_ref, pooled_ref, unfolded_ref, values, rows):
    @pl.when(pl.program_id(0) == 0)
    def _():
        lane = lax.broadcasted_iota(jnp.int32, (WORDS, 128), 1)
        code = lax.broadcasted_iota(jnp.int32, (WORDS, 384), 1)
        values[WORD_CHARS:, :, :] = jnp.zeros((TAPS - 1, WORDS, 128), F32)

        def look_up(place, ids):
            column = ids[:, :1]
            onehot = (column == code).astype(F32).astype(BF16)
            found = dot(onehot, table_ref[...])
            found = jnp.where(lane == BIAS_ROW, 1.0, found)
            absent = jnp.where(column < 0, 1.0, 0.0)
            values[place] = jnp.where(lane == ABSENT_ROW, absent, found)
            return pltpu.roll(ids, 127, 1)

        lax.fori_loop(0, WORD_CHARS, look_up, ids_ref[...])

        @pl.loop(0, WORD_CHARS)
        def _(place):
            taps = values[place]
            for tap in range(1, TAPS):
                taps = jnp.where(lane // CHAR_DIM == tap, values[place + tap], taps)
            unfolded_ref[place] = taps.astype(BF16)

    weight = weight_ref[...]

    def convolve(pair, top):
        left = unfolded_ref[pl.ds(2 * pair, 2)].reshape(2 * WORDS, 128)
        block = dot(left, weight).reshape(2, WORDS, POOL_COLS)
        rows[pl.ds(2 * pair, 2)] = block
        return jnp.maximum(top, jnp.maximum(block[0], block[1]))

    top = lax.fori_loop(
        0, WORD_CHARS // 2, convolve, jnp.full((WORDS, POOL_COLS), -3e38, F32)
    )

    def gather(pair, total):
        block = rows[pl.ds(2 * pair, 2)]
        return total + (jnp.exp(block[0] - top) + jnp.exp(block[1] - top))

    total = lax.fori_loop(0, WORD_CHARS // 2, gather, jnp.zeros((WORDS, POOL_COLS), F32))
    pooled = top + jnp.log(total)
    pooled_ref[...] = pooled
    act_ref[...] = jax.nn.gelu(pooled).astype(BF16)


def pool_words(ids_wide, table_wide, weight_wide):
    return pl.pallas_call(
        pool_kernel,
        grid=(FILTERS // POOL_COLS,),
        out_shape=(
            jax.ShapeDtypeStruct((WORDS, FILTERS), BF16),
            jax.ShapeDtypeStruct((WORDS, FILTERS), F32),
            jax.ShapeDtypeStruct((WORD_CHARS, WORDS, 128), BF16),
        ),
        in_specs=[
            pl.BlockSpec((WORDS, 128), lambda c: (0, 0)),
            pl.BlockSpec((384, 128), lambda c: (0, 0)),
            pl.BlockSpec((128, POOL_COLS), lambda c: (0, c)),
        ],
        out_specs=(
            pl.BlockSpec((WORDS, POOL_COLS), lambda c: (0, c)),
            pl.BlockSpec((WORDS, POOL_COLS), lambda c: (0, c)),
            pl.BlockSpec((WORD_CHARS, WORDS, 128), lambda c: (0, 0, 0)),
        ),
        scratch_shapes=[
            pltpu.VMEM((WORD_CHARS + TAPS - 1, WORDS, 128), F32),
            pltpu.VMEM((WORD_CHARS, WORDS, POOL_COLS), F32),
        ],
        compiler_params=pltpu.CompilerParams(
            dimension_semantics=("arbitrary",), vmem_limit_bytes=40 << 20
        ),
        cost_estimate=pl.CostEstimate(
            flops=2 * WORDS * WORD_CHARS * 128 * FILTERS,
            bytes_accessed=8 << 20,
            transcendentals=WORDS * WORD_CHARS * FILTERS,
        ),
    )(ids_wide, table_wide, weight_wide)


Y, Z, X = 0, 1, 2
ORDERS = ((Y, Z, X), (Z, X, Y), (X, Y, Z))
LEFT_COLS = {"high": 2048, "proj": 2048, "qkv": 768, "out": 768, "up": 768, "down": 3072}
RIGHT_COLS = {"high": 4096, "proj": 768, "qkv": 2304, "out": 768, "up": 3072, "down": 768}
CHUNK_ROWS = {"high": 16, "proj": 16, "qkv": 6, "out": 6, "up": 6, "down": 24}
NAMES = tuple(LEFT_COLS)
GROUPS = tuple((name, group) for name in NAMES for group in range(-(-CHUNK_ROWS[name] // 8)))
GROUP_AT = {key: at for at, key in enumerate(GROUPS)}
RIGHT_AT = {}
for _name in NAMES:
    RIGHT_AT[_name] = sum(RIGHT_COLS[n] for n in NAMES[: NAMES.index(_name)])
RIGHT_ALL = sum(RIGHT_COLS.values())

PIECES = {
    "high": (("high", 0, 0, 1, 0, 4096),),
    "proj": (("proj", 0, 0, 1, 0, 768),),
    "qkv": (("qkv", 0, 0, 0, 1152, 1152),),
    "out": (("out", 0, 0, 0, 384, 384),),
    "up": (("up", 0, 0, 0, 1536, 1536),),
    "down": (("down", 0, 0, 1, 0, 768), ("down", 2, 0, 2, 384, 384)),
}


def cut(pieces, widths):
    parts, rest = [], list(pieces)
    for width in widths:
        part, room = [], width
        while room:
            name, upper, upper_at, lower, lower_at, cols = rest.pop(0)
            used = min(cols, room)
            part.append((name, upper, upper_at, lower, lower_at, used))
            room -= used
            if used < cols:
                rest.insert(
                    0, (name, upper, upper_at + used, lower, lower_at + used, cols - used)
                )
        parts.append(tuple(part))
    assert not rest
    return tuple(parts)


def narrow(piece, most):
    name, upper, upper_at, lower, lower_at, cols = piece
    start = 0
    while start < cols:
        used = min(most, cols - start)
        yield (name, upper, upper_at + start, lower, lower_at + start, used, start)
        start += used


_HIGH = (("high", 0, 0, 1, 0, 2048), ("high", 0, 2048, 1, 2048, 2048))
STREAMS = (
    (("up", "down"), cut(PIECES["down"] + PIECES["up"], (896, 896, 896))),
    (("proj", "qkv", "out"), cut(PIECES["qkv"] + PIECES["out"] + PIECES["proj"], (768, 768, 768))),
    (("high",), cut(_HIGH[:1], (768, 640, 640))),
    ((), cut(_HIGH[1:], (640, 640, 768))),
)
PART_WIDTHS = tuple(
    tuple(sum(piece[5] for piece in part) for part in parts) for _, parts in STREAMS
)
PARTS = tuple(
    (stream, place, width)
    for stream, widths in enumerate(PART_WIDTHS)
    for place, width in enumerate(widths)
) + ((len(STREAMS), 0, 128),)
SMALL_ROWS = 72
SHARED = ((SMALL_ROWS, 128), (16, 384), (8, FILTERS))


def place_of():
    index = lax.axis_index("dp")
    return index // 8, lax.rem(index // 2, 4), lax.rem(index, 2), lax.axis_index("ctx")


def device_of(y, z, core, x):
    return ((y * 4 + z) * 2 + core, x)


def around(value, step):
    return lax.rem(value + step, 4)


def remote(source, target, sems, index, device):
    return pltpu.make_async_remote_copy(
        src_ref=source,
        dst_ref=target,
        send_sem=sems[0].at[index],
        recv_sem=sems[1].at[index],
        device_id=device,
        device_id_type=MESH,
    )


class Part:
    def __init__(self, order, refs, sems, where):
        self.tiles, self.relay1, self.last1, self.relay2, self.last2, self.last3 = refs
        self.order, self.sems, self.where = order, sems, where
        self.width = self.tiles.shape[-1]
        y, z, core, x = where
        self.here = [(y, z, x)[axis] for axis in order]
        self.copies = {}

    def peer(self, level, step):
        y, z, core, x = self.where
        spot = [y, z, x]
        spot[self.order[level]] = around(self.here[level], step)
        return device_of(spot[0], spot[1], core, spot[2])

    def start(self, index, source, target, level, step):
        copy = remote(source, target, self.sems, index, self.peer(level, step))
        copy.start()
        self.copies[index] = copy

    def slices(self, level):
        prefix = tuple(self.here[:level])
        return lambda at, half=None: self.tiles.at[
            prefix + (at,) + (() if half is None else (pl.ds(2 * half, 2),))
        ]

    def buffers(self, level):
        return (self.relay1, self.last1) if level == 0 else (self.relay2, self.last2)

    def ring_start(self, level):
        me, base, tiles = self.here[level], 6 * level, self.slices(level)
        relay, last = self.buffers(level)
        far, right, left = around(me, 2), around(me, 1), around(me, 3)
        self.start(base, tiles(far, 0), relay.at[0], level, 1)
        self.start(base + 1, tiles(far, 1), relay.at[1], level, 3)
        self.start(base + 2, tiles(right, 1), last.at[0, pl.ds(2, 2)], level, 1)
        self.start(base + 3, tiles(left, 0), last.at[1, pl.ds(0, 2)], level, 3)

    def ring_relay(self, level):
        me, base, tiles = self.here[level], 6 * level, self.slices(level)
        relay, last = self.buffers(level)
        for side in (0, 1):
            target = tiles(around(me, (1, 3)[side]), side)
            self.copies[base + side].wait_recv()
            self.add(target, (relay.at[side],), 3 - level)
            self.start(
                base + 4 + side, target, last.at[side, pl.ds(2 * side, 2)], level, (1, 3)[side]
            )

    def ring_end(self, level):
        me, base, tiles = self.here[level], 6 * level, self.slices(level)
        _, last = self.buffers(level)
        for index in range(2, 6):
            self.copies[base + index].wait_recv()
        self.add(tiles(me), (last.at[0], last.at[1]), 3 - level)

    def add(self, target, terms, dims):
        lead = target.shape[:-2]
        count = 1
        for size in lead:
            count *= size

        @pl.loop(0, count)
        def _(flat):
            at, rest = [], flat
            for size in reversed(lead):
                at.insert(0, lax.rem(rest, size))
                rest = rest // size
            at = tuple(at)
            total = target[at].astype(F32)
            for term in terms:
                total = total + term[at].astype(F32)
            target[at] = total.astype(BF16)

    def direct_start(self):
        for step in (1, 2, 3):
            source = self.tiles.at[self.here[0], self.here[1], around(self.here[2], step)]
            self.start(11 + step, source, self.last3.at[step - 1], 2, step)

    def direct_end(self):
        total = self.tiles[tuple(self.here)].astype(F32)
        for step in (1, 2, 3):
            self.copies[11 + step].wait_recv()
            total = total + self.last3[step - 1].astype(F32)
        return total

    def sent(self):
        for copy in self.copies.values():
            copy.wait_send()


class Shared:
    def __init__(self, pair, rings, sems, where):
        self.pair, self.rings, self.sems, self.where = pair, rings, sems, where
        self.copies = []

    def start(self, level, value):
        y, z, core, x = self.where
        if level == 0:
            self.pair[core] = value
            mine = self.pair.at[core]
            peers = [device_of(y, z, 1 - core, x)]
            targets = mine
        else:
            axis = level - 1
            here = (y, z, x)[axis]
            self.rings[axis, here] = value
            mine = self.rings.at[axis, here]
            peers = []
            for step in (1, 2, 3):
                spot = [y, z, x]
                spot[axis] = around(here, step)
                peers.append(device_of(spot[0], spot[1], core, spot[2]))
            targets = mine
        base = 0 if level == 0 else 3 * level - 2
        self.now = []
        for number, peer in enumerate(peers):
            copy = remote(mine, targets, self.sems, base + number, peer)
            copy.start()
            self.now.append(copy)
        self.copies += self.now

    def end(self, level):
        for copy in self.now:
            copy.wait_recv()
        if level == 0:
            return self.pair[0] + self.pair[1]
        ring = self.rings.at[level - 1]
        return (ring[0] + ring[1]) + (ring[2] + ring[3])

    def sent(self):
        for copy in self.copies:
            copy.wait_send()


def pick(rows_per_chunk, group, core, blocks, lanes):
    rows = blocks * 32
    row = lax.broadcasted_iota(jnp.int32, (rows, lanes), 0)
    lane = lax.broadcasted_iota(jnp.int32, (rows, lanes), 1)
    inner = lax.rem(row, 8) + 8 * group
    wanted = ((row // 32 * 2 + core) * 4 + lax.rem(row // 8, 4)) * rows_per_chunk + inner
    hit = jnp.logical_and(wanted == lane, inner < rows_per_chunk)
    return jnp.where(hit, 1.0, 0.0).astype(BF16)


PICK_LANES = {16: 512, 6: 384, 24: 768}


def sums_kernel(schedule, *refs):
    rest = list(refs)

    def take(count):
        taken = rest[:count]
        del rest[:count]
        return taken

    left_in = dict(zip(NAMES, take(6)))
    right_in = dict(zip(NAMES, take(6)))
    chars, unfolded, conv_w, conv_back, pooled, grad_pooled, small_in = take(7)
    outs = dict(zip(NAMES, take(6)))
    out_conv, out_small, out_table, out_bias = take(4)
    left, left_out, right = take(3)
    part_refs = [take(6) for _ in PARTS]
    part_sems = take(2)
    shared_refs = [take(2) for _ in SHARED]
    shared_sems = take(2)
    pair_left_sems, pair_right_sems, load_sems = take(3)
    conv_grad, conv_rows, conv_other, conv_sems = take(4)
    pair_left_sems, pair_right_sems, conv_sems = (
        (sems.at[0], sems.at[1]) for sems in (pair_left_sems, pair_right_sems, conv_sems)
    )
    unfolded_grad, table_grad = take(2)

    where = place_of()
    y, z, core, x = where
    partner = device_of(y, z, 1 - core, x)

    loads = {}
    for at, name in enumerate(NAMES):
        cols = pl.ds(RIGHT_AT[name], RIGHT_COLS[name])
        loads[name] = pltpu.make_async_copy(
            right_in[name], right.at[pl.ds(0, WORDS), cols], load_sems.at[at]
        )
        loads[name].start()

    barrier = pltpu.get_barrier_semaphore()
    greeted = [partner]
    for step in (1, 2, 3):
        greeted.append(device_of(around(y, step), z, core, x))
        greeted.append(device_of(y, around(z, step), core, x))
        greeted.append(device_of(y, z, core, around(x, step)))
    for device in greeted:
        pl.semaphore_signal(barrier, inc=1, device_id=device, device_id_type=MESH)
    pl.semaphore_wait(barrier, len(greeted))

    parts = [
        Part(
            ORDERS[place],
            part_refs[at],
            (part_sems[0].at[at], part_sems[1].at[at]),
            where,
        )
        for at, (_, place, _) in enumerate(PARTS)
    ]
    shared = [
        Shared(pair, rings, (shared_sems[0].at[at], shared_sems[1].at[at]), where)
        for at, (pair, rings) in enumerate(shared_refs)
    ]

    right_sent = {}
    for at, name in enumerate(("down", "up", "qkv", "out", "proj", "high")):
        cols = pl.ds(RIGHT_AT[name], RIGHT_COLS[name])
        right_sent[name] = remote(
            right_in[name],
            right.at[pl.ds(WORDS, WORDS), cols],
            pair_right_sems,
            at,
            partner,
        )
        right_sent[name].start()

    picks = {}

    def picked(rows_per_chunk, group, mine):
        key = (rows_per_chunk, group, mine)
        if key not in picks:
            lanes = PICK_LANES[rows_per_chunk]
            picks[key] = pick(
                rows_per_chunk,
                group,
                core if mine else 1 - core,
                lanes // (8 * rows_per_chunk),
                lanes,
            )
        return picks[key]

    left_sent = {}

    def prepare(stream):
        for name in STREAMS[stream][0]:
            rows_per_chunk = CHUNK_ROWS[name]
            lanes = PICK_LANES[rows_per_chunk]
            ys = lanes // (32 * rows_per_chunk)
            groups = -(-rows_per_chunk // 8)
            first = GROUP_AT[name, 0]
            for group in range(groups):
                for block in range(4 // ys):
                    source = left_in[name][:, block * lanes : (block + 1) * lanes]
                    for mine in (False, True):
                        rows = back_dot(picked(rows_per_chunk, group, mine), source)
                        rows = rows.astype(BF16).reshape(ys, 128, WORDS)
                        span = pl.ds(block * ys, ys)
                        if mine:
                            left[first + group, span, :, 0:WORDS] = rows
                        else:
                            left_out[first + group, span] = rows
            span = pl.ds(first, groups)
            left_sent[name] = remote(
                left_out.at[span],
                left.at[span, :, :, pl.ds(WORDS, WORDS)],
                pair_left_sems,
                NAMES.index(name),
                partner,
            )
            left_sent[name].start()

    def multiply(stream):
        for name in STREAMS[stream][0]:
            loads[name].wait()
            right_sent[name].wait_recv()
            left_sent[name].wait_recv()
        for at, (of, place, _) in enumerate(PARTS):
            if of != stream:
                continue
            tiles, order = part_refs[at][0], ORDERS[place]
            offset = 0
            for piece in STREAMS[stream][1][place]:
                for name, upper, upper_at, lower, lower_at, cols, start in narrow(piece, 512):
                    base, first = RIGHT_AT[name], GROUP_AT[name, 0]
                    lanes = pl.ds(offset + start, cols)

                    @pl.loop(0, 4)
                    def _(row):
                        halves = []
                        for group, column in ((upper, upper_at), (lower, lower_at)):
                            factor = right[:, base + column : base + column + cols]
                            block = dot(left[first + group, row], factor)
                            halves.append(block.reshape(16, 1, 8, cols))
                        both = jnp.concatenate(halves, axis=1).reshape(4, 4, 16, cols)
                        both = both.astype(BF16)
                        for at_z in range(4):
                            for at_x in range(4):
                                spot = tuple((row, at_z, at_x)[axis] for axis in order)
                                tiles[spot + (slice(None), lanes)] = both[at_z, at_x]

                offset += piece[5]
        ring(stream, lambda part: part.ring_start(0))

    def ring(stream, action):
        for at, (of, _, _) in enumerate(PARTS):
            if of == stream:
                action(parts[at])

    def finish(stream):
        for at, (of, place, _) in enumerate(PARTS):
            if of != stream:
                continue
            total = parts[at].direct_end()
            if stream == len(STREAMS):
                out_conv[...] = total
                continue
            offset = 0
            for name, upper, upper_at, lower, lower_at, cols in STREAMS[stream][1][place]:
                block = total[:, offset : offset + cols]
                for group, column, top in ((upper, upper_at, 0), (lower, lower_at, 8)):
                    rows = min(8, CHUNK_ROWS[name] - 8 * group)
                    outs[name][8 * group : 8 * group + rows, column : column + cols] = block[
                        top : top + rows
                    ]
                offset += cols

    lane = lax.broadcasted_iota(jnp.int32, (WORDS, 128), 1)

    def conv_start():
        unfolded_grad[0 : TAPS - 1] = jnp.zeros((TAPS - 1, WORDS, 128), F32)
        conv_grad[...] = jnp.zeros_like(conv_grad)
        table_grad[...] = jnp.zeros_like(table_grad)

    def conv_pair(pair):
        two = unfolded[pl.ds(2 * pair, 2)].reshape(2 * WORDS, 128)
        unit = jnp.where(
            lax.broadcasted_iota(jnp.int32, (128, 128), 0)
            == lax.broadcasted_iota(jnp.int32, (128, 128), 1),
            1.0,
            0.0,
        ).astype(BF16)
        turned = back_dot(unit, two).astype(BF16)
        back = jnp.zeros((2 * WORDS, 128), F32)
        for block in range(4):
            cols = slice(block * 512, (block + 1) * 512)
            conv = dot(two, conv_w[:, cols]).reshape(2, WORDS, 512)
            shares = jnp.exp(conv - pooled[:, cols][None]) * grad_pooled[:, cols][None]
            shares = shares.astype(BF16).reshape(2 * WORDS, 512)
            conv_grad[:, cols] += dot(turned, shares)
            back = back + dot(shares, conv_back[cols, :])
        unfolded_grad[pl.ds(2 * pair + TAPS - 1, 2)] = back.reshape(2, WORDS, 128)
        high_low, onehots = [], []
        for side in (0, 1):
            place = 2 * pair + side
            taps = unfolded_grad[place + TAPS - 1]
            for tap in range(1, TAPS):
                taps = jnp.where(
                    lane // CHAR_DIM == tap, unfolded_grad[place + TAPS - 1 - tap], taps
                )
            taps = jnp.where(lane < BIAS_ROW, taps, 0.0)
            high = taps.astype(BF16)
            low = (taps - high.astype(F32)).astype(BF16)
            high_low.append(jnp.concatenate([high, low], axis=1))
            code = lax.broadcasted_iota(jnp.int32, (CHAR_ROWS, WORDS), 0)
            onehots.append(jnp.where(chars[place] == code, 1.0, 0.0).astype(BF16))
        table_grad[0:CHAR_ROWS, :] += dot(
            jnp.concatenate(onehots, axis=1), jnp.concatenate(high_low, axis=0)
        )

    conv_pairs = []

    def conv_end():
        for block in range(16):
            turned = conv_grad[:, block * 128 : (block + 1) * 128].T
            conv_rows[block] = turned.reshape(2, 64, 128)
        copy = remote(conv_rows.at[:, 1 - core], conv_other, conv_sems, 0, partner)
        copy.start()
        conv_pairs.append(copy)
        table = table_grad[:, 0:128] + table_grad[:, 128:256]
        turned = jnp.concatenate(
            [table[128 * block : 128 * (block + 1)].T for block in range(3)], axis=1
        )
        folded = turned[0:CHAR_DIM]
        for tap in range(1, TAPS):
            folded = folded + turned[tap * CHAR_DIM : (tap + 1) * CHAR_DIM]
        shared[1].start(0, folded)
        shared[2].start(0, conv_grad[BIAS_ROW : BIAS_ROW + 8, :])

    def conv_ring():
        conv_pairs[0].wait_recv()
        tiles = part_refs[-1][0]

        @pl.loop(0, 4)
        def _(at):
            for inner in range(4):
                row = at * 4 + inner
                total = conv_rows[row, core] + conv_other[row]
                tiles[at, inner] = total.astype(BF16).reshape(4, 16, 128)

        ring(len(STREAMS), lambda part: part.ring_start(0))

    def shared_step(which, level):
        if level < 3:
            shared[which].start(level + 1, shared[which].end(level))
        else:
            (out_small, out_table, out_bias)[which][...] = shared[which].end(level)

    actions = {
        "prepare": prepare,
        "multiply": multiply,
        "relay1": lambda s: ring(s, lambda part: part.ring_relay(0)),
        "end1": lambda s: ring(s, lambda part: (part.ring_end(0), part.ring_start(1))),
        "relay2": lambda s: ring(s, lambda part: part.ring_relay(1)),
        "end2": lambda s: ring(s, lambda part: (part.ring_end(1), part.direct_start())),
        "finish": finish,
        "conv_start": conv_start,
        "conv": lambda first, last: lax.fori_loop(
            first, last, lambda pair, nothing: (conv_pair(pair), nothing)[1], 0
        ),
        "conv_end": conv_end,
        "conv_ring": conv_ring,
        "small": lambda: shared[0].start(0, small_in[...]),
        "shared": shared_step,
    }
    for name, *given in schedule:
        actions[name](*given)

    for part in parts:
        part.sent()
    for one in shared:
        one.sent()
    for name in NAMES:
        right_sent[name].wait_send()
        left_sent[name].wait_send()
    conv_pairs[0].wait_send()


SCHEDULE = (
    ("prepare", 0),
    ("prepare", 1),
    ("multiply", 0),
    ("prepare", 2),
    ("small",),
    ("multiply", 1),
    ("relay1", 0),
    ("shared", 0, 0),
    ("multiply", 2),
    ("relay1", 1),
    ("multiply", 3),
    ("conv_start",),
    ("conv", 0, 3),
    ("end1", 0),
    ("shared", 0, 1),
    ("conv", 3, 6),
    ("relay1", 2),
    ("relay1", 3),
    ("end1", 1),
    ("relay2", 0),
    ("shared", 0, 2),
    ("conv", 6, 11),
    ("end2", 0),
    ("relay2", 1),
    ("shared", 0, 3),
    ("conv", 11, 16),
    ("end1", 2),
    ("finish", 0),
    ("end2", 1),
    ("conv", 16, 20),
    ("end1", 3),
    ("relay2", 2),
    ("finish", 1),
    ("conv", 20, 25),
    ("conv_end",),
    ("relay2", 3),
    ("end2", 2),
    ("conv_ring",),
    ("shared", 1, 0),
    ("shared", 2, 0),
    ("end2", 3),
    ("relay1", 4),
    ("finish", 2),
    ("shared", 1, 1),
    ("shared", 2, 1),
    ("end1", 4),
    ("finish", 3),
    ("relay2", 4),
    ("shared", 1, 2),
    ("shared", 2, 2),
    ("end2", 4),
    ("shared", 1, 3),
    ("shared", 2, 3),
    ("finish", 4),
)


def sum_gradients(left, right, chars, unfolded, conv_w, conv_back, pooled, grad_pooled, small):
    part_scratch = []
    for _, _, width in PARTS:
        part_scratch += [
            pltpu.VMEM((4, 4, 4, 16, width), BF16),
            pltpu.VMEM((2, 2, 4, 16, width), BF16),
            pltpu.VMEM((2, 4, 4, 16, width), BF16),
            pltpu.VMEM((2, 2, 16, width), BF16),
            pltpu.VMEM((2, 4, 16, width), BF16),
            pltpu.VMEM((3, 16, width), BF16),
        ]
    part_scratch += [pltpu.SemaphoreType.DMA((len(PARTS), 15))] * 2
    for shape in SHARED:
        part_scratch += [pltpu.VMEM((2,) + shape, F32), pltpu.VMEM((3, 4) + shape, F32)]
    part_scratch += [pltpu.SemaphoreType.DMA((len(SHARED), 10))] * 2
    scratch = (
        [
            pltpu.VMEM((len(GROUPS), 4, 128, 2 * WORDS), BF16),
            pltpu.VMEM((len(GROUPS), 4, 128, WORDS), BF16),
            pltpu.VMEM((2 * WORDS, RIGHT_ALL), BF16),
        ]
        + part_scratch
        + [
            pltpu.SemaphoreType.DMA((2, 6)),
            pltpu.SemaphoreType.DMA((2, 6)),
            pltpu.SemaphoreType.DMA((6,)),
            pltpu.VMEM((128, FILTERS), F32),
            pltpu.VMEM((16, 2, 64, 128), F32),
            pltpu.VMEM((16, 64, 128), F32),
            pltpu.SemaphoreType.DMA((2, 1)),
            pltpu.VMEM((WORD_CHARS + TAPS - 1, WORDS, 128), F32),
            pltpu.VMEM((384, 256), F32),
        ]
    )
    whole = pl.BlockSpec(memory_space=pltpu.VMEM)
    shapes = [(CHUNK_ROWS[name], RIGHT_COLS[name]) for name in NAMES]
    shapes += [(16, 128)] + list(SHARED)
    results = pl.pallas_call(
        functools.partial(sums_kernel, SCHEDULE),
        out_shape=tuple(jax.ShapeDtypeStruct(shape, F32) for shape in shapes),
        in_specs=[whole] * 6 + [pl.BlockSpec(memory_space=pl.ANY)] * 6 + [whole] * 7,
        out_specs=tuple(whole for _ in shapes),
        scratch_shapes=scratch,
        compiler_params=pltpu.CompilerParams(
            collective_id=1, has_side_effects=True, vmem_limit_bytes=64 << 20
        ),
    )(
        *[left[name] for name in NAMES],
        *[right[name] for name in NAMES],
        chars,
        unfolded,
        conv_w,
        conv_back,
        pooled,
        grad_pooled,
        small,
    )
    return dict(zip(NAMES, results)), results[6:]


def body(
    char_ids,
    word_lengths,
    word_home,
    seq_lengths,
    char_table,
    conv_weight,
    conv_bias,
    highway_weight,
    highway_bias,
    proj_weight,
    norm_gain,
    norm_shift,
    qkv_weight,
    out_weight,
    up_weight,
    down_weight,
    cotangent,
):
    group_len = cotangent.shape[1]
    ctx_size = lax.axis_size("ctx")
    full_len = group_len * ctx_size
    head_scale = HEAD_DIM ** (-0.5)
    conv_masked = jnp.where(tap_mask(), conv_weight, jnp.zeros_like(conv_weight))
    high_shift = highway_bias.astype(F32)
    gain_rows = norm_gain.astype(F32)
    shift_rows = norm_shift.astype(F32)

    present = jnp.arange(WORD_CHARS)[None, :] < word_lengths[:, None]
    ids = jnp.where(present, char_ids, -1)
    ids_wide = jnp.pad(ids, ((0, 0), (0, 128 - WORD_CHARS)), constant_values=-1)
    chars = ids.T.reshape(WORD_CHARS, 1, WORDS)
    table_wide = jnp.pad(
        jnp.tile(char_table, (1, TAPS)), ((0, 384 - CHARS), (0, 128 - TAPS * CHAR_DIM))
    )
    conv_w = jnp.concatenate(
        [
            conv_masked,
            conv_bias[None, :],
            jnp.full((1, FILTERS), NEG_LARGE, BF16),
            jnp.zeros((128 - ABSENT_ROW - 1, FILTERS), BF16),
        ],
        axis=0,
    )
    conv_back = jnp.pad(conv_masked, ((0, 128 - TAPS * CHAR_DIM), (0, 0))).T

    act, pooled, unfolded = pool_words(ids_wide, table_wide, conv_w)
    mixed_rows = dot(act, highway_weight[0]) + high_shift[0]
    final_rows = gate_mix(act.astype(F32), mixed_rows).astype(BF16)
    embedded = dot(final_rows, proj_weight).astype(BF16)

    seq_index = word_home // SEQ_LEN
    pos_index = word_home % SEQ_LEN
    target = seq_index * ctx_size + pos_index // group_len
    slot = pos_index % group_len
    numbers = jnp.arange(WORDS)
    send_pick = (target[None, :] == numbers[:, None]).astype(BF16)
    carried = jnp.concatenate(
        [embedded, jnp.broadcast_to(slot[:, None], (WORDS, 128)).astype(BF16)], axis=1
    )
    to_send = dot(send_pick, carried).astype(BF16)
    arrived = lax.all_to_all(to_send, ("dp", "ctx"), split_axis=0, concat_axis=0, tiled=True)
    arrived_slot = arrived[:, D].astype(jnp.int32)
    place_pick = (arrived_slot[None, :] == numbers[:, None]).astype(BF16)
    word_rows = dot(place_pick, arrived[:, :D])

    first_f, first_normal, first_inv = norm_parts(word_rows, gain_rows[0], shift_rows[0])
    first_norm = first_f.astype(BF16)
    joint_proj = dot(first_norm, qkv_weight).astype(BF16)
    queries = joint_proj[:, :D].reshape(group_len, HEADS, HEAD_DIM)
    both_all = lax.all_gather(joint_proj[:, D:], "ctx", axis=0, tiled=True)
    key_heads = both_all[:, :D].reshape(full_len, HEADS, HEAD_DIM)
    value_heads = both_all[:, D:].reshape(full_len, HEADS, HEAD_DIM)
    key_valid = jnp.arange(full_len) < seq_lengths[0]
    valid_wide = key_valid[None, None, :]
    scores = (
        jnp.einsum("qhd,khd->hqk", queries, key_heads, preferred_element_type=F32) * head_scale
    )
    masked = jnp.where(valid_wide, scores, NEG_LARGE)
    top_val = jnp.max(masked, -1, keepdims=True)
    expo_val = jnp.where(valid_wide, jnp.exp(masked - top_val), 0.0)
    totals = jnp.sum(expo_val, -1, keepdims=True)
    probs = expo_val / totals
    probs_low = probs.astype(BF16)
    context = (
        jnp.einsum("hqk,khd->qhd", probs_low, value_heads, preferred_element_type=F32)
        .reshape(WORDS, D)
        .astype(BF16)
    )
    attn_out = dot(context, out_weight)
    mid_f, mid_normal, mid_inv = norm_parts(
        first_norm.astype(F32) + attn_out, gain_rows[1], shift_rows[1]
    )
    middle = mid_f.astype(BF16)
    up_proj = dot(middle, up_weight)
    hidden_act = jax.nn.gelu(up_proj).astype(BF16)
    down_proj = dot(hidden_act, down_weight)
    out_f, out_normal, out_inv = norm_parts(
        middle.astype(F32) + down_proj, gain_rows[2], shift_rows[2]
    )
    out_hidden = out_f.astype(BF16).reshape(1, group_len, D)

    grad_rows = cotangent.reshape(WORDS, D).astype(F32)
    grad_pre2, gain_two, shift_two = norm_back(grad_rows, out_normal, out_inv, gain_rows[2])
    grad_down = grad_pre2.astype(BF16)
    _, gelu_pull = jax.vjp(jax.nn.gelu, up_proj)
    grad_up = gelu_pull(back_dot(grad_down, down_weight))[0].astype(BF16)
    grad_mid = grad_pre2 + back_dot(grad_up, up_weight)
    grad_pre1, gain_one, shift_one = norm_back(grad_mid, mid_normal, mid_inv, gain_rows[1])
    grad_attn = grad_pre1.astype(BF16)
    grad_context = (
        back_dot(grad_attn, out_weight).astype(BF16).reshape(group_len, HEADS, HEAD_DIM)
    )
    grad_probs = jnp.einsum("qhd,khd->hqk", grad_context, value_heads, preferred_element_type=F32)
    delta_rows = jnp.sum(probs * grad_probs, -1, keepdims=True)
    grad_scores = (probs * (grad_probs - delta_rows)).astype(BF16)
    grad_query = (
        jnp.einsum("hqk,khd->qhd", grad_scores, key_heads, preferred_element_type=F32) * head_scale
    )
    grad_keys = (
        jnp.einsum("hqk,qhd->khd", grad_scores, queries, preferred_element_type=F32) * head_scale
    )
    grad_values = jnp.einsum("hqk,qhd->khd", probs_low, grad_context, preferred_element_type=F32)
    grad_both = jnp.concatenate(
        [grad_keys.reshape(full_len, D), grad_values.reshape(full_len, D)], axis=1
    ).astype(BF16)
    both_sum = lax.psum_scatter(grad_both, "ctx", scatter_dimension=0, tiled=True)
    grad_joint = jnp.concatenate([grad_query.reshape(WORDS, D).astype(BF16), both_sum], axis=-1)
    grad_first = back_dot(grad_joint, qkv_weight) + grad_pre1
    grad_words, gain_zero, shift_zero = norm_back(grad_first, first_normal, first_inv, gain_rows[0])

    send_back = first_dot(place_pick, grad_words.astype(BF16)).astype(BF16)
    returned = lax.all_to_all(send_back, ("dp", "ctx"), split_axis=0, concat_axis=0, tiled=True)
    grad_embedded = first_dot(send_pick, returned).astype(BF16)
    grad_act = back_dot(grad_embedded, proj_weight)
    _, mix_pull = jax.vjp(gate_mix, act.astype(F32), mixed_rows)
    grad_direct, grad_mixed = mix_pull(grad_act)
    grad_mixed = grad_mixed.astype(BF16)
    high_bias = jnp.sum(grad_mixed.astype(F32), 0)
    grad_act = grad_direct + back_dot(grad_mixed, highway_weight[0])
    _, pool_pull = jax.vjp(jax.nn.gelu, pooled)
    grad_pooled = pool_pull(grad_act)[0]

    small = jnp.concatenate(
        [high_bias, gain_zero, gain_one, gain_two, shift_zero, shift_one, shift_two]
    ).reshape(-1, 128)
    small = jnp.pad(small, ((0, SMALL_ROWS - small.shape[0]), (0, 0)))
    sums, (conv_sum, small_sum, table_sum, bias_sum) = sum_gradients(
        {
            "high": act,
            "proj": final_rows,
            "qkv": first_norm,
            "out": context,
            "up": middle,
            "down": hidden_act,
        },
        {
            "high": grad_mixed,
            "proj": grad_embedded,
            "qkv": grad_joint,
            "out": grad_attn,
            "up": grad_up,
            "down": grad_down,
        },
        chars,
        unfolded,
        conv_w,
        conv_back,
        pooled,
        grad_pooled,
        small,
    )
    small_sum = small_sum.reshape(-1)
    norm_sum = small_sum[2 * FILTERS : 2 * FILTERS + 6 * D].reshape(2, 3, D)
    conv_shard = conv_sum[:, : TAPS * CHAR_DIM].T
    me = lax.axis_index("dp") * ctx_size + lax.axis_index("ctx")
    filters = me * conv_shard.shape[1] + jnp.arange(conv_shard.shape[1])
    taps = jnp.arange(TAPS * CHAR_DIM) // CHAR_DIM
    conv_shard = jnp.where(taps[:, None] < jnp.take(filter_widths(), filters)[None, :], conv_shard, 0.0)
    return (
        out_hidden,
        table_sum[:, :CHARS].T,
        conv_shard,
        bias_sum[0],
        sums["high"][None],
        small_sum[None, : 2 * FILTERS],
        sums["proj"],
        norm_sum[0],
        norm_sum[1],
        sums["qkv"],
        sums["out"],
        sums["up"],
        sums["down"],
    )


def solution(mesh):
    placed = (
        P(("dp", "ctx"), None),
        P(("dp", "ctx")),
        P(("dp", "ctx")),
        P("dp"),
        P(),
        P(),
        P(),
        P(),
        P(),
        P(),
        P(),
        P(),
        P(),
        P(),
        P(),
        P(),
        P("dp", "ctx", None),
    )
    return jax.shard_map(
        body,
        mesh=mesh,
        in_specs=placed,
        out_specs=(
            P("dp", "ctx", None),
            P(),
            P(None, ("dp", "ctx")),
            P(),
            P(None, ("dp", "ctx"), None),
            P(),
            P(("dp", "ctx"), None),
            P(),
            P(),
            P(("dp", "ctx"), None),
            P(("dp", "ctx"), None),
            P(("dp", "ctx"), None),
            P(("dp", "ctx"), None),
        ),
        check_vma=False,
    )
```

```python
import functools
import jax
import jax.numpy as jnp
from jax import lax
from jax.experimental import pallas as pl
from jax.experimental.pallas import tpu as pltpu
from jax.sharding import PartitionSpec as P

D = 768
FF = 3072
HEADS = 12
HEAD_DIM = 64
FILTERS = 2048
CHAR_DIM = 16
CHARS = 262
WORD_CHARS = 50
TAPS = 7
SEQ_LEN = 512
WORDS = 128

EPSILON = 1e-05
NEG_LARGE = -1e30
MESH = pl.DeviceIdType.MESH
BF16 = jnp.bfloat16
F32 = jnp.float32

BIAS_ROW = TAPS * CHAR_DIM
ABSENT_ROW = BIAS_ROW + 1
CHAR_ROWS = 272


def filter_widths():
    unit_count = FILTERS // 64
    filter_index = jnp.arange(FILTERS)
    widths = jnp.ones((FILTERS,), jnp.int32)
    for bound_units in (1, 2, 4, 8, 16, 32):
        widths = widths + (filter_index >= unit_count * bound_units).astype(jnp.int32)
    return widths


def tap_mask():
    tap_rows = jnp.arange(TAPS * CHAR_DIM) // CHAR_DIM
    return tap_rows[:, None] < filter_widths()[None, :]


def gate_mix(current, mixed_rows):
    carry_gate = jax.nn.sigmoid(mixed_rows[:, FILTERS:])
    return carry_gate * current + (1.0 - carry_gate) * jax.nn.gelu(mixed_rows[:, :FILTERS])


def norm_parts(values_in, gain_row, shift_row):
    mean_val = jnp.mean(values_in, -1, keepdims=True)
    centred = values_in - mean_val
    inverse = lax.rsqrt(jnp.mean(centred * centred, -1, keepdims=True) + EPSILON)
    normal = centred * inverse
    return (normal * gain_row + shift_row, normal, inverse)


def norm_back(grad_out, normal, inverse, gain_row):
    scaled = grad_out * gain_row
    grad_in = inverse * (
        scaled
        - jnp.mean(scaled, -1, keepdims=True)
        - normal * jnp.mean(scaled * normal, -1, keepdims=True)
    )
    return (grad_in, jnp.sum(grad_out * normal, 0), jnp.sum(grad_out, 0))


def dot(left, right):
    return jnp.dot(left, right, preferred_element_type=F32)


def back_dot(rows_in, weight_rows):
    return lax.dot_general(
        rows_in, weight_rows, (((1,), (1,)), ((), ())), preferred_element_type=F32
    )


def first_dot(left, right):
    return lax.dot_general(left, right, (((0,), (0,)), ((), ())), preferred_element_type=F32)


POOL_COLS = 512
POOL_STEP = 10


def pool_kernel(ids_ref, table_ref, weight_ref, act_ref, pooled_ref, unfolded_ref, values):
    @pl.when(pl.program_id(0) == 0)
    def _():
        lane = lax.broadcasted_iota(jnp.int32, (WORDS, 128), 1)
        code = lax.broadcasted_iota(jnp.int32, (WORDS, 384), 1)
        values[WORD_CHARS:, :, :] = jnp.zeros((TAPS - 1, WORDS, 128), F32)

        def look_up(place, ids):
            column = ids[:, :1]
            onehot = (column == code).astype(F32).astype(BF16)
            found = dot(onehot, table_ref[...])
            found = jnp.where(lane == BIAS_ROW, 1.0, found)
            absent = jnp.where(column < 0, 1.0, 0.0)
            values[place] = jnp.where(lane == ABSENT_ROW, absent, found)
            return pltpu.roll(ids, 127, 1)

        lax.fori_loop(0, WORD_CHARS, look_up, ids_ref[...], unroll=5)

        @pl.loop(0, WORD_CHARS)
        def _(place):
            taps = values[place]
            for tap in range(1, TAPS):
                taps = jnp.where(lane // CHAR_DIM == tap, values[place + tap], taps)
            unfolded_ref[place] = taps.astype(BF16)

    weight = weight_ref[...]

    def convolve(step, state):
        top, total = state
        left = unfolded_ref[pl.ds(POOL_STEP * step, POOL_STEP)].reshape(POOL_STEP * WORDS, 128)
        block = dot(left, weight).reshape(POOL_STEP, WORDS, POOL_COLS)
        higher = jnp.maximum(top, jnp.max(block, axis=0))
        total = total * jnp.exp(top - higher) + jnp.sum(jnp.exp(block - higher[None]), axis=0)
        return higher, total

    top, total = lax.fori_loop(
        0,
        WORD_CHARS // POOL_STEP,
        convolve,
        (jnp.full((WORDS, POOL_COLS), -3e38, F32), jnp.zeros((WORDS, POOL_COLS), F32)),
    )
    pooled = top + jnp.log(total)
    pooled_ref[...] = pooled
    act_ref[...] = jax.nn.gelu(pooled).astype(BF16)


def pool_words(ids_wide, table_wide, weight_wide):
    return pl.pallas_call(
        pool_kernel,
        grid=(FILTERS // POOL_COLS,),
        out_shape=(
            jax.ShapeDtypeStruct((WORDS, FILTERS), BF16),
            jax.ShapeDtypeStruct((WORDS, FILTERS), F32),
            jax.ShapeDtypeStruct((WORD_CHARS, WORDS, 128), BF16),
        ),
        in_specs=[
            pl.BlockSpec((WORDS, 128), lambda c: (0, 0)),
            pl.BlockSpec((384, 128), lambda c: (0, 0)),
            pl.BlockSpec((128, POOL_COLS), lambda c: (0, c)),
        ],
        out_specs=(
            pl.BlockSpec((WORDS, POOL_COLS), lambda c: (0, c)),
            pl.BlockSpec((WORDS, POOL_COLS), lambda c: (0, c)),
            pl.BlockSpec((WORD_CHARS, WORDS, 128), lambda c: (0, 0, 0)),
        ),
        scratch_shapes=[
            pltpu.VMEM((WORD_CHARS + TAPS - 1, WORDS, 128), F32),
        ],
        compiler_params=pltpu.CompilerParams(
            dimension_semantics=("arbitrary",), vmem_limit_bytes=40 << 20
        ),
        cost_estimate=pl.CostEstimate(
            flops=2 * WORDS * WORD_CHARS * 128 * FILTERS,
            bytes_accessed=8 << 20,
            transcendentals=WORDS * WORD_CHARS * FILTERS,
        ),
    )(ids_wide, table_wide, weight_wide)


Y, Z, X = 0, 1, 2
ORDERS = ((Y, Z, X), (Z, X, Y), (X, Y, Z))
LEFT_COLS = {"high": 2048, "proj": 2048, "qkv": 768, "out": 768, "up": 768, "down": 3072}
RIGHT_COLS = {"high": 4096, "proj": 768, "qkv": 2304, "out": 768, "up": 3072, "down": 768}
CHUNK_ROWS = {"high": 16, "proj": 16, "qkv": 6, "out": 6, "up": 6, "down": 24}
NAMES = tuple(LEFT_COLS)
GROUPS = tuple((name, group) for name in NAMES for group in range(-(-CHUNK_ROWS[name] // 8)))
GROUP_AT = {key: at for at, key in enumerate(GROUPS)}
RIGHT_AT = {}
for _name in NAMES:
    RIGHT_AT[_name] = sum(RIGHT_COLS[n] for n in NAMES[: NAMES.index(_name)])
RIGHT_ALL = sum(RIGHT_COLS.values())

PIECES = {
    "high": (("high", 0, 0, 1, 0, 4096),),
    "proj": (("proj", 0, 0, 1, 0, 768),),
    "qkv": (("qkv", 0, 0, 0, 1152, 1152),),
    "out": (("out", 0, 0, 0, 384, 384),),
    "up": (("up", 0, 0, 0, 1536, 1536),),
    "down": (("down", 0, 0, 1, 0, 768), ("down", 2, 0, 2, 384, 384)),
}


def cut(pieces, widths):
    parts, rest = [], list(pieces)
    for width in widths:
        part, room = [], width
        while room:
            name, upper, upper_at, lower, lower_at, cols = rest.pop(0)
            used = min(cols, room)
            part.append((name, upper, upper_at, lower, lower_at, used))
            room -= used
            if used < cols:
                rest.insert(
                    0, (name, upper, upper_at + used, lower, lower_at + used, cols - used)
                )
        parts.append(tuple(part))
    assert not rest
    return tuple(parts)


def narrow(piece, most):
    name, upper, upper_at, lower, lower_at, cols = piece
    start = 0
    while start < cols:
        used = min(most, cols - start)
        yield (name, upper, upper_at + start, lower, lower_at + start, used, start)
        start += used


_HIGH = (("high", 0, 0, 1, 0, 2048), ("high", 0, 2048, 1, 2048, 2048))
STREAMS = (
    (("up", "down"), cut(PIECES["down"] + PIECES["up"], (896, 896, 896))),
    (("proj", "qkv", "out"), cut(PIECES["qkv"] + PIECES["out"] + PIECES["proj"], (768, 768, 768))),
    (("high",), cut(_HIGH[:1], (768, 640, 640))),
    ((), cut(_HIGH[1:], (640, 640, 768))),
)
PART_WIDTHS = tuple(
    tuple(sum(piece[5] for piece in part) for part in parts) for _, parts in STREAMS
)
PARTS = tuple(
    (stream, place, width)
    for stream, widths in enumerate(PART_WIDTHS)
    for place, width in enumerate(widths)
) + ((len(STREAMS), 0, 128),)
SMALL_ROWS = 72
SHARED = ((SMALL_ROWS, 128), (16, 384), (8, FILTERS))


def place_of():
    index = lax.axis_index("dp")
    return index // 8, lax.rem(index // 2, 4), lax.rem(index, 2), lax.axis_index("ctx")


def device_of(y, z, core, x):
    return ((y * 4 + z) * 2 + core, x)


def around(value, step):
    return lax.rem(value + step, 4)


def remote(source, target, sems, index, device):
    return pltpu.make_async_remote_copy(
        src_ref=source,
        dst_ref=target,
        send_sem=sems[0].at[index],
        recv_sem=sems[1].at[index],
        device_id=device,
        device_id_type=MESH,
    )


class Part:
    def __init__(self, order, refs, sems, where):
        self.tiles, self.relay1, self.last1, self.relay2, self.last2, self.last3 = refs
        self.order, self.sems, self.where = order, sems, where
        self.width = self.tiles.shape[-1]
        y, z, core, x = where
        self.here = [(y, z, x)[axis] for axis in order]
        self.copies = {}

    def peer(self, level, step):
        y, z, core, x = self.where
        spot = [y, z, x]
        spot[self.order[level]] = around(self.here[level], step)
        return device_of(spot[0], spot[1], core, spot[2])

    def start(self, index, source, target, level, step):
        copy = remote(source, target, self.sems, index, self.peer(level, step))
        copy.start()
        self.copies[index] = copy

    def slices(self, level):
        prefix = tuple(self.here[:level])
        return lambda at, half=None: self.tiles.at[
            prefix + (at,) + (() if half is None else (pl.ds(2 * half, 2),))
        ]

    def buffers(self, level):
        return (self.relay1, self.last1) if level == 0 else (self.relay2, self.last2)

    def ring_start(self, level):
        me, base, tiles = self.here[level], 6 * level, self.slices(level)
        relay, last = self.buffers(level)
        far, right, left = around(me, 2), around(me, 1), around(me, 3)
        self.start(base, tiles(far, 0), relay.at[0], level, 1)
        self.start(base + 1, tiles(far, 1), relay.at[1], level, 3)
        self.start(base + 2, tiles(right, 1), last.at[0, pl.ds(2, 2)], level, 1)
        self.start(base + 3, tiles(left, 0), last.at[1, pl.ds(0, 2)], level, 3)

    def ring_relay(self, level):
        me, base, tiles = self.here[level], 6 * level, self.slices(level)
        relay, last = self.buffers(level)
        for side in (0, 1):
            target = tiles(around(me, (1, 3)[side]), side)
            self.copies[base + side].wait_recv()
            self.add(target, (relay.at[side],), 3 - level)
            self.start(
                base + 4 + side, target, last.at[side, pl.ds(2 * side, 2)], level, (1, 3)[side]
            )

    def ring_end(self, level):
        me, base, tiles = self.here[level], 6 * level, self.slices(level)
        _, last = self.buffers(level)
        for index in range(2, 6):
            self.copies[base + index].wait_recv()
        self.add(tiles(me), (last.at[0], last.at[1]), 3 - level)

    def add(self, target, terms, dims):
        lead = target.shape[:-2]
        count = 1
        for size in lead:
            count *= size

        @pl.loop(0, count)
        def _(flat):
            at, rest = [], flat
            for size in reversed(lead):
                at.insert(0, lax.rem(rest, size))
                rest = rest // size
            at = tuple(at)
            total = target[at].astype(F32)
            for term in terms:
                total = total + term[at].astype(F32)
            target[at] = total.astype(BF16)

    def direct_start(self):
        for step in (1, 2, 3):
            source = self.tiles.at[self.here[0], self.here[1], around(self.here[2], step)]
            self.start(11 + step, source, self.last3.at[step - 1], 2, step)

    def direct_end(self):
        total = self.tiles[tuple(self.here)].astype(F32)
        for step in (1, 2, 3):
            self.copies[11 + step].wait_recv()
            total = total + self.last3[step - 1].astype(F32)
        return total

    def sent(self):
        for copy in self.copies.values():
            copy.wait_send()


class Shared:
    def __init__(self, pair, rings, sems, where):
        self.pair, self.rings, self.sems, self.where = pair, rings, sems, where
        self.copies = []

    def start(self, level, value):
        y, z, core, x = self.where
        if level == 0:
            self.pair[core] = value
            mine = self.pair.at[core]
            peers = [device_of(y, z, 1 - core, x)]
            targets = mine
        else:
            axis = level - 1
            here = (y, z, x)[axis]
            self.rings[axis, here] = value
            mine = self.rings.at[axis, here]
            peers = []
            for step in (1, 2, 3):
                spot = [y, z, x]
                spot[axis] = around(here, step)
                peers.append(device_of(spot[0], spot[1], core, spot[2]))
            targets = mine
        base = 0 if level == 0 else 3 * level - 2
        self.now = []
        for number, peer in enumerate(peers):
            copy = remote(mine, targets, self.sems, base + number, peer)
            copy.start()
            self.now.append(copy)
        self.copies += self.now

    def end(self, level):
        for copy in self.now:
            copy.wait_recv()
        if level == 0:
            return self.pair[0] + self.pair[1]
        ring = self.rings.at[level - 1]
        return (ring[0] + ring[1]) + (ring[2] + ring[3])

    def sent(self):
        for copy in self.copies:
            copy.wait_send()


def pick(rows_per_chunk, group, core, blocks, lanes):
    rows = blocks * 32
    row = lax.broadcasted_iota(jnp.int32, (rows, lanes), 0)
    lane = lax.broadcasted_iota(jnp.int32, (rows, lanes), 1)
    inner = lax.rem(row, 8) + 8 * group
    wanted = ((row // 32 * 2 + core) * 4 + lax.rem(row // 8, 4)) * rows_per_chunk + inner
    hit = jnp.logical_and(wanted == lane, inner < rows_per_chunk)
    return jnp.where(hit, 1.0, 0.0).astype(BF16)


PICK_LANES = {16: 512, 6: 384, 24: 768}


CONV_STEP = 10
CONV_COLS = 512


def sums_kernel(schedule, *refs):
    rest = list(refs)

    def take(count):
        taken = rest[:count]
        del rest[:count]
        return taken

    left_in = dict(zip(NAMES, take(6)))
    right_in = dict(zip(NAMES, take(6)))
    chars, unfolded, conv_w, conv_back, pooled, grad_pooled, small_in = take(7)
    outs = dict(zip(NAMES, take(6)))
    out_conv, out_small, out_table, out_bias = take(4)
    left, left_out, right = take(3)
    part_refs = [take(6) for _ in PARTS]
    part_sems = take(2)
    shared_refs = [take(2) for _ in SHARED]
    shared_sems = take(2)
    pair_left_sems, pair_right_sems, load_sems = take(3)
    conv_grad, conv_rows, conv_other, conv_sems = take(4)
    pair_left_sems, pair_right_sems, conv_sems = (
        (sems.at[0], sems.at[1]) for sems in (pair_left_sems, pair_right_sems, conv_sems)
    )
    last_grad, table_grad = take(2)

    where = place_of()
    y, z, core, x = where
    partner = device_of(y, z, 1 - core, x)

    loads = {}
    for at, name in enumerate(NAMES):
        cols = pl.ds(RIGHT_AT[name], RIGHT_COLS[name])
        loads[name] = pltpu.make_async_copy(
            right_in[name], right.at[pl.ds(0, WORDS), cols], load_sems.at[at]
        )
        loads[name].start()

    barrier = pltpu.get_barrier_semaphore()
    greeted = [partner]
    for step in (1, 2, 3):
        greeted.append(device_of(around(y, step), z, core, x))
        greeted.append(device_of(y, around(z, step), core, x))
        greeted.append(device_of(y, z, core, around(x, step)))
    for device in greeted:
        pl.semaphore_signal(barrier, inc=1, device_id=device, device_id_type=MESH)
    pl.semaphore_wait(barrier, len(greeted))

    parts = [
        Part(
            ORDERS[place],
            part_refs[at],
            (part_sems[0].at[at], part_sems[1].at[at]),
            where,
        )
        for at, (_, place, _) in enumerate(PARTS)
    ]
    shared = [
        Shared(pair, rings, (shared_sems[0].at[at], shared_sems[1].at[at]), where)
        for at, (pair, rings) in enumerate(shared_refs)
    ]

    right_sent = {}
    for at, name in enumerate(("down", "up", "qkv", "out", "proj", "high")):
        cols = pl.ds(RIGHT_AT[name], RIGHT_COLS[name])
        right_sent[name] = remote(
            right_in[name],
            right.at[pl.ds(WORDS, WORDS), cols],
            pair_right_sems,
            at,
            partner,
        )
        right_sent[name].start()

    picks = {}

    def picked(rows_per_chunk, group, mine):
        key = (rows_per_chunk, group, mine)
        if key not in picks:
            lanes = PICK_LANES[rows_per_chunk]
            picks[key] = pick(
                rows_per_chunk,
                group,
                core if mine else 1 - core,
                lanes // (8 * rows_per_chunk),
                lanes,
            )
        return picks[key]

    left_sent = {}

    def prepare(stream):
        for name in STREAMS[stream][0]:
            rows_per_chunk = CHUNK_ROWS[name]
            lanes = PICK_LANES[rows_per_chunk]
            ys = lanes // (32 * rows_per_chunk)
            groups = -(-rows_per_chunk // 8)
            first = GROUP_AT[name, 0]
            for group in range(groups):
                for block in range(4 // ys):
                    source = left_in[name][:, block * lanes : (block + 1) * lanes]
                    for mine in (False, True):
                        rows = back_dot(picked(rows_per_chunk, group, mine), source)
                        rows = rows.astype(BF16).reshape(ys, 128, WORDS)
                        span = pl.ds(block * ys, ys)
                        if mine:
                            left[first + group, span, :, 0:WORDS] = rows
                        else:
                            left_out[first + group, span] = rows
            span = pl.ds(first, groups)
            left_sent[name] = remote(
                left_out.at[span],
                left.at[span, :, :, pl.ds(WORDS, WORDS)],
                pair_left_sems,
                NAMES.index(name),
                partner,
            )
            left_sent[name].start()

    def multiply(stream):
        for name in STREAMS[stream][0]:
            loads[name].wait()
            right_sent[name].wait_recv()
            left_sent[name].wait_recv()
        for at, (of, place, _) in enumerate(PARTS):
            if of != stream:
                continue
            tiles, order = part_refs[at][0], ORDERS[place]
            offset = 0
            for piece in STREAMS[stream][1][place]:
                for name, upper, upper_at, lower, lower_at, cols, start in narrow(piece, 512):
                    base, first = RIGHT_AT[name], GROUP_AT[name, 0]
                    lanes = pl.ds(offset + start, cols)

                    @pl.loop(0, 4, unroll=4)
                    def _(row):
                        halves = []
                        for group, column in ((upper, upper_at), (lower, lower_at)):
                            factor = right[:, base + column : base + column + cols]
                            block = dot(left[first + group, row], factor)
                            halves.append(block.reshape(16, 1, 8, cols))
                        both = jnp.concatenate(halves, axis=1).reshape(4, 4, 16, cols)
                        both = both.astype(BF16)
                        for at_z in range(4):
                            for at_x in range(4):
                                spot = tuple((row, at_z, at_x)[axis] for axis in order)
                                tiles[spot + (slice(None), lanes)] = both[at_z, at_x]

                offset += piece[5]
        ring(stream, lambda part: part.ring_start(0))

    def ring(stream, action):
        for at, (of, _, _) in enumerate(PARTS):
            if of == stream:
                action(parts[at])

    def finish(stream):
        for at, (of, place, _) in enumerate(PARTS):
            if of != stream:
                continue
            total = parts[at].direct_end()
            if stream == len(STREAMS):
                out_conv[...] = total
                continue
            offset = 0
            for name, upper, upper_at, lower, lower_at, cols in STREAMS[stream][1][place]:
                block = total[:, offset : offset + cols]
                for group, column, top in ((upper, upper_at, 0), (lower, lower_at, 8)):
                    rows = min(8, CHUNK_ROWS[name] - 8 * group)
                    outs[name][8 * group : 8 * group + rows, column : column + cols] = block[
                        top : top + rows
                    ]
                offset += cols

    lane = lax.broadcasted_iota(jnp.int32, (WORDS, 128), 1)

    def conv_start():
        last_grad[...] = jnp.zeros_like(last_grad)
        conv_grad[...] = jnp.zeros_like(conv_grad)
        table_grad[...] = jnp.zeros_like(table_grad)

    def conv_block(step):
        first = CONV_STEP * step
        some = unfolded[pl.ds(first, CONV_STEP)].reshape(CONV_STEP * WORDS, 128)
        unit = jnp.where(
            lax.broadcasted_iota(jnp.int32, (128, 128), 0)
            == lax.broadcasted_iota(jnp.int32, (128, 128), 1),
            1.0,
            0.0,
        ).astype(BF16)
        turned = back_dot(unit, some).astype(BF16)
        back = jnp.zeros((CONV_STEP * WORDS, 128), F32)
        for block in range(FILTERS // CONV_COLS):
            cols = slice(block * CONV_COLS, (block + 1) * CONV_COLS)
            conv = dot(some, conv_w[:, cols]).reshape(CONV_STEP, WORDS, CONV_COLS)
            shares = jnp.exp(conv - pooled[:, cols][None]) * grad_pooled[:, cols][None]
            shares = shares.astype(BF16).reshape(CONV_STEP * WORDS, CONV_COLS)
            conv_grad[:, cols] += dot(turned, shares)
            back = back + dot(shares, conv_back[cols, :])
        back = back.reshape(CONV_STEP, WORDS, 128)
        before = last_grad[...]
        last_grad[...] = back[CONV_STEP - TAPS + 1 :]
        high_low, onehots = [], []
        for side in range(CONV_STEP):
            place = first + side
            taps = back[side]
            for tap in range(1, TAPS):
                from_tap = back[side - tap] if side >= tap else before[TAPS - 1 + side - tap]
                taps = jnp.where(lane // CHAR_DIM == tap, from_tap, taps)
            taps = jnp.where(lane < BIAS_ROW, taps, 0.0)
            high = taps.astype(BF16)
            low = (taps - high.astype(F32)).astype(BF16)
            high_low.append(jnp.concatenate([high, low], axis=1))
            code = lax.broadcasted_iota(jnp.int32, (CHAR_ROWS, WORDS), 0)
            onehots.append(jnp.where(chars[place] == code, 1.0, 0.0).astype(BF16))
        table_grad[0:CHAR_ROWS, :] += dot(
            jnp.concatenate(onehots, axis=1), jnp.concatenate(high_low, axis=0)
        )

    conv_pairs = []

    def conv_end():
        for block in range(16):
            turned = conv_grad[:, block * 128 : (block + 1) * 128].T
            conv_rows[block] = turned.reshape(2, 64, 128)
        copy = remote(conv_rows.at[:, 1 - core], conv_other, conv_sems, 0, partner)
        copy.start()
        conv_pairs.append(copy)
        table = table_grad[:, 0:128] + table_grad[:, 128:256]
        turned = jnp.concatenate(
            [table[128 * block : 128 * (block + 1)].T for block in range(3)], axis=1
        )
        folded = turned[0:CHAR_DIM]
        for tap in range(1, TAPS):
            folded = folded + turned[tap * CHAR_DIM : (tap + 1) * CHAR_DIM]
        shared[1].start(0, folded)
        shared[2].start(0, conv_grad[BIAS_ROW : BIAS_ROW + 8, :])

    def conv_ring():
        conv_pairs[0].wait_recv()
        tiles = part_refs[-1][0]

        @pl.loop(0, 4)
        def _(at):
            for inner in range(4):
                row = at * 4 + inner
                total = conv_rows[row, core] + conv_other[row]
                tiles[at, inner] = total.astype(BF16).reshape(4, 16, 128)

        ring(len(STREAMS), lambda part: part.ring_start(0))

    def shared_step(which, level):
        if level < 3:
            shared[which].start(level + 1, shared[which].end(level))
        else:
            (out_small, out_table, out_bias)[which][...] = shared[which].end(level)

    actions = {
        "prepare": prepare,
        "multiply": multiply,
        "relay1": lambda s: ring(s, lambda part: part.ring_relay(0)),
        "end1": lambda s: ring(s, lambda part: (part.ring_end(0), part.ring_start(1))),
        "relay2": lambda s: ring(s, lambda part: part.ring_relay(1)),
        "end2": lambda s: ring(s, lambda part: (part.ring_end(1), part.direct_start())),
        "finish": finish,
        "conv_start": conv_start,
        "conv": lambda first, last: lax.fori_loop(
            first, last, lambda step, nothing: (conv_block(step), nothing)[1], 0
        ),
        "conv_end": conv_end,
        "conv_ring": conv_ring,
        "small": lambda: shared[0].start(0, small_in[...]),
        "shared": shared_step,
    }
    for name, *given in schedule:
        actions[name](*given)

    for part in parts:
        part.sent()
    for one in shared:
        one.sent()
    for name in NAMES:
        right_sent[name].wait_send()
        left_sent[name].wait_send()
    conv_pairs[0].wait_send()


SCHEDULE = (
    ("prepare", 0),
    ("multiply", 0),
    ("prepare", 1),
    ("multiply", 1),
    ("prepare", 2),
    ("multiply", 2),
    ("multiply", 3),
    ("small",),
    ("conv_start",),
    ("conv", 0, 5),
    ("conv_end",),
    ("shared", 0, 0),
    ("relay1", 0),
    ("conv_ring",),
    ("relay1", 1),
    ("shared", 0, 1),
    ("shared", 1, 0),
    ("shared", 2, 0),
    ("relay1", 2),
    ("relay1", 4),
    ("relay1", 3),
    ("end1", 0),
    ("shared", 0, 2),
    ("shared", 1, 1),
    ("shared", 2, 1),
    ("end1", 4),
    ("end1", 1),
    ("relay2", 0),
    ("end1", 2),
    ("shared", 0, 3),
    ("shared", 1, 2),
    ("shared", 2, 2),
    ("relay2", 4),
    ("relay2", 1),
    ("end2", 0),
    ("end1", 3),
    ("relay2", 2),
    ("shared", 1, 3),
    ("shared", 2, 3),
    ("end2", 4),
    ("end2", 1),
    ("finish", 0),
    ("relay2", 3),
    ("end2", 2),
    ("finish", 1),
    ("finish", 4),
    ("end2", 3),
    ("finish", 2),
    ("finish", 3),
)


def sum_gradients(left, right, chars, unfolded, conv_w, conv_back, pooled, grad_pooled, small):
    part_scratch = []
    for _, _, width in PARTS:
        part_scratch += [
            pltpu.VMEM((4, 4, 4, 16, width), BF16),
            pltpu.VMEM((2, 2, 4, 16, width), BF16),
            pltpu.VMEM((2, 4, 4, 16, width), BF16),
            pltpu.VMEM((2, 2, 16, width), BF16),
            pltpu.VMEM((2, 4, 16, width), BF16),
            pltpu.VMEM((3, 16, width), BF16),
        ]
    part_scratch += [pltpu.SemaphoreType.DMA((len(PARTS), 15))] * 2
    for shape in SHARED:
        part_scratch += [pltpu.VMEM((2,) + shape, F32), pltpu.VMEM((3, 4) + shape, F32)]
    part_scratch += [pltpu.SemaphoreType.DMA((len(SHARED), 10))] * 2
    scratch = (
        [
            pltpu.VMEM((len(GROUPS), 4, 128, 2 * WORDS), BF16),
            pltpu.VMEM((len(GROUPS), 4, 128, WORDS), BF16),
            pltpu.VMEM((2 * WORDS, RIGHT_ALL), BF16),
        ]
        + part_scratch
        + [
            pltpu.SemaphoreType.DMA((2, 6)),
            pltpu.SemaphoreType.DMA((2, 6)),
            pltpu.SemaphoreType.DMA((6,)),
            pltpu.VMEM((128, FILTERS), F32),
            pltpu.VMEM((16, 2, 64, 128), F32),
            pltpu.VMEM((16, 64, 128), F32),
            pltpu.SemaphoreType.DMA((2, 1)),
            pltpu.VMEM((TAPS - 1, WORDS, 128), F32),
            pltpu.VMEM((384, 256), F32),
        ]
    )
    whole = pl.BlockSpec(memory_space=pltpu.VMEM)
    shapes = [(CHUNK_ROWS[name], RIGHT_COLS[name]) for name in NAMES]
    shapes += [(16, 128)] + list(SHARED)
    results = pl.pallas_call(
        functools.partial(sums_kernel, SCHEDULE),
        out_shape=tuple(jax.ShapeDtypeStruct(shape, F32) for shape in shapes),
        in_specs=[whole] * 6 + [pl.BlockSpec(memory_space=pl.ANY)] * 6 + [whole] * 7,
        out_specs=tuple(whole for _ in shapes),
        scratch_shapes=scratch,
        compiler_params=pltpu.CompilerParams(
            collective_id=1, has_side_effects=True, vmem_limit_bytes=64 << 20
        ),
    )(
        *[left[name] for name in NAMES],
        *[right[name] for name in NAMES],
        chars,
        unfolded,
        conv_w,
        conv_back,
        pooled,
        grad_pooled,
        small,
    )
    return dict(zip(NAMES, results)), results[6:]


PAIRS = HEADS // 2
SENT = 1024
GELU_SCALE = 0.7978845608028654
GELU_CUBE = 0.044715
FF_COLS = 512


def gelu_both(value):
    square = value * value
    bend = jnp.tanh(GELU_SCALE * value * (1.0 + GELU_CUBE * square))
    half = 0.5 * (1.0 + bend)
    slope = half + 0.5 * GELU_SCALE * value * (1.0 - bend * bend) * (
        1.0 + 3.0 * GELU_CUBE * square
    )
    return value * half, slope


def encoder_kernel(*refs):
    rest = list(refs)

    def take(count):
        taken = rest[:count]
        del rest[:count]
        return taken

    rows_in, slot_in, order_in, valid_in, gains, shifts, cotangent = take(7)
    weights_in = take(4)
    out_hidden, out_first, out_context, out_middle, out_hidden_act = take(5)
    out_joint, out_attn, out_up, out_down, out_rows, out_norms = take(6)
    weights = take(4)
    load_sems, go_sems, back_sems, keys_sems, sums_sems = take(5)
    go_near, near, go_far, far = take(4)
    back_far, home_far, back_near, home_near = take(4)
    joint, both, probs, probs_low, slopes = take(5)
    grads, relay, last = take(3)
    go_near_sems, go_far_sems = (go_sems.at[0], go_sems.at[1]), (go_sems.at[2], go_sems.at[3])
    back_near_sems, back_far_sems = (
        (back_sems.at[0], back_sems.at[1]),
        (back_sems.at[2], back_sems.at[3]),
    )
    keys_sems = (keys_sems.at[0], keys_sems.at[1])
    sums_sems = (sums_sems.at[0], sums_sems.at[1])

    y, z, core, x = place_of()
    loads = []
    for at in range(4):
        loads.append(pltpu.make_async_copy(weights_in[at], weights[at], load_sems.at[at]))
        loads[at].start()
    qkv_w, out_w, up_w, down_w = weights

    near_peers, far_peers = [], []
    for number in range(1, 8):
        their_core, their_x = lax.rem(core + number // 4, 2), around(x, number % 4)
        near_peers.append((number, their_core * 4 + their_x, device_of(y, z, their_core, their_x)))
    for number in range(1, 16):
        their_y, their_z = around(y, number // 4), around(z, number % 4)
        far_peers.append((number, their_y * 4 + their_z, device_of(their_y, their_z, core, x)))
    near_me, far_me = core * 4 + x, y * 4 + z
    right = device_of(y, z, core, around(x, 1))
    left = device_of(y, z, core, around(x, 3))

    barrier = pltpu.get_barrier_semaphore()
    for _, _, device in near_peers + far_peers:
        pl.semaphore_signal(barrier, inc=1, device_id=device, device_id_type=MESH)

    lane = lax.broadcasted_iota(jnp.int32, (WORDS, WORDS), 1)
    row = lax.broadcasted_iota(jnp.int32, (WORDS, WORDS), 0)
    one_hot = lambda hit: jnp.where(hit, 1.0, 0.0).astype(BF16)
    send_pick = one_hot(order_in[...] == row)
    turn_pick = one_hot(lane == lax.rem(row, 8) * 16 + row // 8)

    def exchange(peers, mine, sems, source, target):
        copies = []
        for number, index, device in peers:
            copy = remote(source.at[index], target.at[mine], sems, number, device)
            copy.start()
            copies.append(copy)
        target[mine] = source[mine]
        for copy in copies:
            copy.wait_recv()
        return copies

    carried = dot(send_pick, rows_in[...]).astype(BF16)
    slots = dot(send_pick, slot_in[...]).astype(BF16)
    go_near[:, :, 0:D] = carried.reshape(8, 16, D)
    go_near[:, :, D : D + 128] = slots.reshape(8, 16, 128)
    go_near[:, :, D + 128 :] = jnp.zeros((8, 16, SENT - D - 128), BF16)
    pl.semaphore_wait(barrier, len(near_peers) + len(far_peers))
    sent = exchange(near_peers, near_me, go_near_sems, go_near, near)
    turned = dot(turn_pick, near[...].reshape(WORDS, SENT)).reshape(16, 8, SENT)
    halves = [turned[:, :, : SENT // 2], turned[:, :, SENT // 2 :]]
    go_far[...] = jnp.concatenate(halves, axis=1).astype(BF16)
    sent += exchange(far_peers, far_me, go_far_sems, go_far, far)
    arrived = far[...].astype(F32)
    arrived = jnp.concatenate([arrived[:, :8], arrived[:, 8:]], axis=2).reshape(WORDS, SENT)
    place_pick = one_hot(arrived[:, D : D + 128] == lane.astype(F32))
    word_rows = first_dot(place_pick, arrived[:, :D].astype(BF16))

    gain = [gains[at : at + 1, :] for at in range(3)]
    shift = [shifts[at : at + 1, :] for at in range(3)]
    first_f, first_normal, first_inv = norm_parts(word_rows, gain[0], shift[0])
    first_norm = first_f.astype(BF16)
    out_first[...] = first_norm
    loads[0].wait()
    for start in (D, 2 * D, 0):
        cols = slice(start, start + D)
        joint[:, cols] = dot(first_norm, qkv_w[:, cols]).astype(BF16)
        if start:
            half = pl.ds(start - D, D)
            both[x, :, start - D : start] = joint[:, cols]
            for side, device in ((0, right), (1, left)):
                copy = remote(
                    both.at[x, :, half], both.at[x, :, half], keys_sems, start // D * 2 + side, device
                )
                copy.start()
                sent.append(copy)
    key_right, key_left, value_right, value_left = sent[-4:]
    key_right.wait_recv()
    behind, ahead = around(x, 3), around(x, 1)
    pass_key = remote(
        both.at[behind, :, pl.ds(0, D)], both.at[behind, :, pl.ds(0, D)], keys_sems, 0, right
    )
    pass_key.start()
    value_left.wait_recv()
    pass_value = remote(
        both.at[ahead, :, pl.ds(D, D)], both.at[ahead, :, pl.ds(D, D)], keys_sems, 1, left
    )
    pass_value.start()
    sent += [pass_key, pass_value]
    for copy in (key_left, value_right, pass_key, pass_value):
        copy.wait_recv()

    scale = HEAD_DIM ** (-0.5)
    low_lanes = one_hot(lane < HEAD_DIM)
    high_lanes = one_hot(lane >= HEAD_DIM)
    valid = valid_in[...] > 0

    def stacked(rows):
        return jnp.concatenate([rows * low_lanes, rows * high_lanes], axis=0)

    def unstacked(rows):
        return jnp.where(lane < HEAD_DIM, rows[:WORDS], rows[WORDS:])

    for pair in range(PAIRS):
        cols = slice(pair * 128, pair * 128 + 128)
        keys = both[:, :, cols].reshape(SEQ_LEN, 128)
        values = both[:, :, D + pair * 128 : D + pair * 128 + 128].reshape(SEQ_LEN, 128)
        scores = back_dot(stacked(joint[:, cols]), keys) * scale
        masked = jnp.where(valid, scores, NEG_LARGE)
        top = jnp.max(masked, -1, keepdims=True)
        expo = jnp.where(valid, jnp.exp(masked - top), 0.0)
        share = expo / jnp.sum(expo, -1, keepdims=True)
        probs[pair] = share
        share = share.astype(BF16)
        probs_low[pair] = share
        out_context[:, cols] = unstacked(dot(share, values)).astype(BF16)
    loads[1].wait()
    attn_out = dot(out_context[...], out_w[...])
    mid_f, mid_normal, mid_inv = norm_parts(first_norm.astype(F32) + attn_out, gain[1], shift[1])
    middle = mid_f.astype(BF16)
    out_middle[...] = middle
    loads[2].wait()
    loads[3].wait()

    down_proj = jnp.zeros((WORDS, D), F32)
    for block in range(FF // FF_COLS):
        cols = slice(block * FF_COLS, (block + 1) * FF_COLS)
        act, slope = gelu_both(dot(middle, up_w[:, cols]))
        act = act.astype(BF16)
        slopes[:, cols] = slope
        out_hidden_act[:, cols] = act
        down_proj = down_proj + dot(act, down_w[cols, :])
    out_f, out_normal, out_inv = norm_parts(middle.astype(F32) + down_proj, gain[2], shift[2])
    out_hidden[...] = out_f.astype(BF16)

    def note(which, gain_row, shift_row):
        out_norms[which : which + 1, :] = gain_row[None]
        out_norms[3 + which : 4 + which, :] = shift_row[None]

    grad_pre2, gain_row, shift_row = norm_back(
        cotangent[...].astype(F32), out_normal, out_inv, gain[2]
    )
    note(2, gain_row, shift_row)
    grad_down = grad_pre2.astype(BF16)
    out_down[...] = grad_down
    grad_mid = grad_pre2
    for block in range(FF // FF_COLS):
        cols = slice(block * FF_COLS, (block + 1) * FF_COLS)
        grad_up = (slopes[:, cols] * back_dot(grad_down, down_w[cols, :])).astype(BF16)
        out_up[:, cols] = grad_up
        grad_mid = grad_mid + back_dot(grad_up, up_w[:, cols])
    grad_pre1, gain_row, shift_row = norm_back(grad_mid, mid_normal, mid_inv, gain[1])
    note(1, gain_row, shift_row)
    grad_attn = grad_pre1.astype(BF16)
    out_attn[...] = grad_attn
    grad_context = back_dot(grad_attn, out_w[...]).astype(BF16)

    for pair in range(PAIRS):
        cols = slice(pair * 128, pair * 128 + 128)
        value_cols = slice(D + pair * 128, D + pair * 128 + 128)
        keys = both[:, :, cols].reshape(SEQ_LEN, 128)
        values = both[:, :, value_cols].reshape(SEQ_LEN, 128)
        grad_rows = stacked(grad_context[:, cols])
        share = probs[pair]
        grad_probs = back_dot(grad_rows, values)
        delta = jnp.sum(share * grad_probs, -1, keepdims=True)
        grad_scores = (share * (grad_probs - delta)).astype(BF16)
        grad_query = unstacked(dot(grad_scores, keys)) * scale
        out_joint[:, cols] = grad_query.astype(BF16)
        grad_keys = first_dot(grad_scores, stacked(joint[:, cols])) * scale
        grads[:, :, cols] = grad_keys.astype(BF16).reshape(4, WORDS, 128)
        grad_values = first_dot(probs_low[pair], grad_rows)
        grads[:, :, value_cols] = grad_values.astype(BF16).reshape(4, WORDS, 128)

    key_half, value_half = pl.ds(0, D), pl.ds(D, D)
    opposite = around(x, 2)
    steps = [
        remote(grads.at[opposite, :, key_half], relay.at[0], sums_sems, 0, right),
        remote(grads.at[opposite, :, value_half], relay.at[1], sums_sems, 1, left),
        remote(grads.at[ahead, :, value_half], last.at[0, :, value_half], sums_sems, 2, right),
        remote(grads.at[behind, :, key_half], last.at[1, :, key_half], sums_sems, 3, left),
    ]
    for copy in steps:
        copy.start()
    steps[0].wait_recv()
    grads[ahead, :, 0:D] = (grads[ahead, :, 0:D].astype(F32) + relay[0].astype(F32)).astype(BF16)
    steps.append(
        remote(grads.at[ahead, :, key_half], last.at[0, :, key_half], sums_sems, 4, right)
    )
    steps[4].start()
    steps[1].wait_recv()
    grads[behind, :, D:] = (grads[behind, :, D:].astype(F32) + relay[1].astype(F32)).astype(BF16)
    steps.append(
        remote(grads.at[behind, :, value_half], last.at[1, :, value_half], sums_sems, 5, left)
    )
    steps[5].start()
    sent += steps
    for copy in steps[2:]:
        copy.wait_recv()
    total = grads[x].astype(F32) + last[0].astype(F32) + last[1].astype(F32)
    out_joint[:, D:] = total.astype(BF16)

    grad_first = grad_pre1
    for start in range(0, 3 * D, D):
        cols = slice(start, start + D)
        grad_first = grad_first + back_dot(out_joint[:, cols], qkv_w[:, cols])
    grad_words, gain_row, shift_row = norm_back(grad_first, first_normal, first_inv, gain[0])
    note(0, gain_row, shift_row)

    turned = dot(place_pick, grad_words.astype(BF16)).reshape(16, 8, D)
    halves = [turned[:, :, : D // 2], turned[:, :, D // 2 :]]
    back_far[...] = jnp.concatenate(halves, axis=1).astype(BF16)
    sent += exchange(far_peers, far_me, back_far_sems, back_far, home_far)
    arrived = home_far[...].astype(F32)
    arrived = jnp.concatenate([arrived[:, :8], arrived[:, 8:]], axis=2).reshape(WORDS, D)
    arrived = first_dot(turn_pick, arrived.astype(BF16)).astype(BF16)
    back_near[...] = arrived.reshape(8, 16, D)
    sent += exchange(near_peers, near_me, back_near_sems, back_near, home_near)
    out_rows[...] = first_dot(send_pick, home_near[...].reshape(WORDS, D)).astype(BF16)
    for copy in sent:
        copy.wait_send()


def encode(rows, slots, order, valid, gains, shifts, cotangent, weights):
    whole = pl.BlockSpec(memory_space=pltpu.VMEM)
    shapes = [(WORDS, D)] * 4 + [(WORDS, FF), (WORDS, 3 * D), (WORDS, D), (WORDS, FF)]
    shapes += [(WORDS, D)] * 2
    out_shapes = [jax.ShapeDtypeStruct(shape, BF16) for shape in shapes]
    out_shapes.append(jax.ShapeDtypeStruct((6, D), F32))
    dma = pltpu.SemaphoreType.DMA
    return pl.pallas_call(
        encoder_kernel,
        out_shape=tuple(out_shapes),
        in_specs=[whole] * 7 + [pl.BlockSpec(memory_space=pl.ANY)] * 4,
        out_specs=tuple(whole for _ in out_shapes),
        scratch_shapes=[
            *(pltpu.VMEM(weight.shape, BF16) for weight in weights),
            dma((4,)),
            dma((4, 16)),
            dma((4, 16)),
            dma((2, 6)),
            dma((2, 6)),
            pltpu.VMEM((8, 16, SENT), BF16),
            pltpu.VMEM((8, 16, SENT), BF16),
            pltpu.VMEM((16, 16, SENT // 2), BF16),
            pltpu.VMEM((16, 16, SENT // 2), BF16),
            pltpu.VMEM((16, 16, D // 2), BF16),
            pltpu.VMEM((16, 16, D // 2), BF16),
            pltpu.VMEM((8, 16, D), BF16),
            pltpu.VMEM((8, 16, D), BF16),
            pltpu.VMEM((WORDS, 3 * D), BF16),
            pltpu.VMEM((4, WORDS, 2 * D), BF16),
            pltpu.VMEM((PAIRS, 2 * WORDS, SEQ_LEN), F32),
            pltpu.VMEM((PAIRS, 2 * WORDS, SEQ_LEN), BF16),
            pltpu.VMEM((WORDS, FF), F32),
            pltpu.VMEM((4, WORDS, 2 * D), BF16),
            pltpu.VMEM((2, WORDS, D), BF16),
            pltpu.VMEM((2, WORDS, 2 * D), BF16),
        ],
        compiler_params=pltpu.CompilerParams(
            collective_id=2, has_side_effects=True, vmem_limit_bytes=60 << 20
        ),
    )(rows, slots, order, valid, gains, shifts, cotangent, *weights)


def body(
    char_ids,
    word_lengths,
    word_home,
    seq_lengths,
    char_table,
    conv_weight,
    conv_bias,
    highway_weight,
    highway_bias,
    proj_weight,
    norm_gain,
    norm_shift,
    qkv_weight,
    out_weight,
    up_weight,
    down_weight,
    cotangent,
):
    group_len = cotangent.shape[1]
    ctx_size = lax.axis_size("ctx")
    full_len = group_len * ctx_size
    conv_masked = jnp.where(tap_mask(), conv_weight, jnp.zeros_like(conv_weight))
    high_shift = highway_bias.astype(F32)
    gain_rows = norm_gain.astype(F32)
    shift_rows = norm_shift.astype(F32)

    present = jnp.arange(WORD_CHARS)[None, :] < word_lengths[:, None]
    ids = jnp.where(present, char_ids, -1)
    ids_wide = jnp.pad(ids, ((0, 0), (0, 128 - WORD_CHARS)), constant_values=-1)
    chars = ids.T.reshape(WORD_CHARS, 1, WORDS)
    table_wide = jnp.pad(
        jnp.tile(char_table, (1, TAPS)), ((0, 384 - CHARS), (0, 128 - TAPS * CHAR_DIM))
    )
    conv_w = jnp.concatenate(
        [
            conv_masked,
            conv_bias[None, :],
            jnp.full((1, FILTERS), NEG_LARGE, BF16),
            jnp.zeros((128 - ABSENT_ROW - 1, FILTERS), BF16),
        ],
        axis=0,
    )
    conv_back = jnp.pad(conv_masked, ((0, 128 - TAPS * CHAR_DIM), (0, 0))).T

    act, pooled, unfolded = pool_words(ids_wide, table_wide, conv_w)
    mixed_rows = dot(act, highway_weight[0]) + high_shift[0]
    final_rows = gate_mix(act.astype(F32), mixed_rows).astype(BF16)
    embedded = dot(final_rows, proj_weight).astype(BF16)

    seq_index = word_home // SEQ_LEN
    pos_index = word_home % SEQ_LEN
    slot = pos_index % group_len
    near = seq_index % 2 * ctx_size + pos_index // group_len
    order = near * 16 + seq_index // 2
    slots = jnp.broadcast_to(slot[:, None], (WORDS, 128)).astype(BF16)
    valid = (jnp.arange(full_len) < seq_lengths[0]).astype(jnp.int32)
    (
        out_hidden,
        first_norm,
        context,
        middle,
        hidden_act,
        grad_joint,
        grad_attn,
        grad_up,
        grad_down,
        grad_embedded,
        norm_grads,
    ) = encode(
        embedded,
        slots,
        order[None, :],
        valid[None, :],
        gain_rows,
        shift_rows,
        cotangent.reshape(WORDS, D),
        (qkv_weight, out_weight, up_weight, down_weight),
    )
    out_hidden = out_hidden.reshape(1, group_len, D)
    grad_act = back_dot(grad_embedded, proj_weight)
    _, mix_pull = jax.vjp(gate_mix, act.astype(F32), mixed_rows)
    grad_direct, grad_mixed = mix_pull(grad_act)
    grad_mixed = grad_mixed.astype(BF16)
    high_bias = jnp.sum(grad_mixed.astype(F32), 0)
    grad_act = grad_direct + back_dot(grad_mixed, highway_weight[0])
    _, pool_pull = jax.vjp(jax.nn.gelu, pooled)
    grad_pooled = pool_pull(grad_act)[0]

    small = jnp.concatenate([high_bias, norm_grads.reshape(-1)]).reshape(-1, 128)
    small = jnp.pad(small, ((0, SMALL_ROWS - small.shape[0]), (0, 0)))
    sums, (conv_sum, small_sum, table_sum, bias_sum) = sum_gradients(
        {
            "high": act,
            "proj": final_rows,
            "qkv": first_norm,
            "out": context,
            "up": middle,
            "down": hidden_act,
        },
        {
            "high": grad_mixed,
            "proj": grad_embedded,
            "qkv": grad_joint,
            "out": grad_attn,
            "up": grad_up,
            "down": grad_down,
        },
        chars,
        unfolded,
        conv_w,
        conv_back,
        pooled,
        grad_pooled,
        small,
    )
    small_sum = small_sum.reshape(-1)
    norm_sum = small_sum[2 * FILTERS : 2 * FILTERS + 6 * D].reshape(2, 3, D)
    conv_shard = conv_sum[:, : TAPS * CHAR_DIM].T
    me = lax.axis_index("dp") * ctx_size + lax.axis_index("ctx")
    filters = me * conv_shard.shape[1] + jnp.arange(conv_shard.shape[1])
    taps = jnp.arange(TAPS * CHAR_DIM) // CHAR_DIM
    conv_shard = jnp.where(taps[:, None] < jnp.take(filter_widths(), filters)[None, :], conv_shard, 0.0)
    return (
        out_hidden,
        table_sum[:, :CHARS].T,
        conv_shard,
        bias_sum[0],
        sums["high"][None],
        small_sum[None, : 2 * FILTERS],
        sums["proj"],
        norm_sum[0],
        norm_sum[1],
        sums["qkv"],
        sums["out"],
        sums["up"],
        sums["down"],
    )


def solution(mesh):
    placed = (
        P(("dp", "ctx"), None),
        P(("dp", "ctx")),
        P(("dp", "ctx")),
        P("dp"),
        P(),
        P(),
        P(),
        P(),
        P(),
        P(),
        P(),
        P(),
        P(),
        P(),
        P(),
        P(),
        P("dp", "ctx", None),
    )
    return jax.shard_map(
        body,
        mesh=mesh,
        in_specs=placed,
        out_specs=(
            P("dp", "ctx", None),
            P(),
            P(None, ("dp", "ctx")),
            P(),
            P(None, ("dp", "ctx"), None),
            P(),
            P(("dp", "ctx"), None),
            P(),
            P(),
            P(("dp", "ctx"), None),
            P(("dp", "ctx"), None),
            P(("dp", "ctx"), None),
            P(("dp", "ctx"), None),
        ),
        check_vma=False,
    )
```

```python
import functools
import jax
import jax.numpy as jnp
from jax import lax
from jax.experimental import pallas as pl
from jax.experimental.pallas import tpu as pltpu
from jax.sharding import PartitionSpec as P

D = 768
FF = 3072
HEADS = 12
HEAD_DIM = 64
FILTERS = 2048
CHAR_DIM = 16
CHARS = 262
WORD_CHARS = 50
TAPS = 7
SEQ_LEN = 512
WORDS = 128

EPSILON = 1e-05
NEG_LARGE = -1e30
MESH = pl.DeviceIdType.MESH
BF16 = jnp.bfloat16
F32 = jnp.float32

BIAS_ROW = TAPS * CHAR_DIM
ABSENT_ROW = BIAS_ROW + 1
CHAR_ROWS = 272


def norm_parts(values_in, gain_row, shift_row):
    mean_val = jnp.mean(values_in, -1, keepdims=True)
    centred = values_in - mean_val
    inverse = lax.rsqrt(jnp.mean(centred * centred, -1, keepdims=True) + EPSILON)
    normal = centred * inverse
    return (normal * gain_row + shift_row, normal, inverse)


def norm_back(grad_out, normal, inverse, gain_row):
    scaled = grad_out * gain_row
    grad_in = inverse * (
        scaled
        - jnp.mean(scaled, -1, keepdims=True)
        - normal * jnp.mean(scaled * normal, -1, keepdims=True)
    )
    return (grad_in, jnp.sum(grad_out * normal, 0), jnp.sum(grad_out, 0))


def dot(left, right):
    return jnp.dot(left, right, preferred_element_type=F32)


def back_dot(rows_in, weight_rows):
    return lax.dot_general(
        rows_in, weight_rows, (((1,), (1,)), ((), ())), preferred_element_type=F32
    )


def first_dot(left, right):
    return lax.dot_general(left, right, (((0,), (0,)), ((), ())), preferred_element_type=F32)


def place_of():
    index = lax.axis_index("dp")
    return index // 8, lax.rem(index // 2, 4), lax.rem(index, 2), lax.axis_index("ctx")


def device_of(y, z, core, x):
    return ((y * 4 + z) * 2 + core, x)


def around(value, step):
    return lax.rem(value + step, 4)


def remote(source, target, sems, index, device):
    return pltpu.make_async_remote_copy(
        src_ref=source,
        dst_ref=target,
        send_sem=sems[0].at[index],
        recv_sem=sems[1].at[index],
        device_id=device,
        device_id_type=MESH,
    )


def near_peers_of(where):
    y, z, core, x = where
    peers = []
    for number in range(1, 8):
        their_core, their_x = lax.rem(core + number // 4, 2), around(x, number % 4)
        peers.append((number, their_core * 4 + their_x, device_of(y, z, their_core, their_x)))
    return peers


def far_peers_of(where):
    y, z, core, x = where
    peers = []
    for number in range(1, 16):
        their_y, their_z = around(y, number // 4), around(z, number % 4)
        peers.append((number, their_y * 4 + their_z, device_of(their_y, their_z, core, x)))
    return peers


def exchange(peers, mine, sems, source, target):
    copies = []
    for number, index, device in peers:
        copy = remote(source.at[index], target.at[mine], sems, number, device)
        copy.start()
        copies.append(copy)
    target[mine] = source[mine]
    for copy in copies:
        copy.wait_recv()
    return copies


def exact_dot(left, right):
    return jnp.dot(left, right, preferred_element_type=F32, precision=lax.Precision.HIGHEST)


POOL_COLS = 512
POOL_STEP = 10
HIGH_PARTS = 4


def embed_kernel(
    ids_ref,
    lengths_ref,
    home_ref,
    table_ref,
    conv_ref,
    conv_bias_ref,
    high_in,
    high_bias_ref,
    proj_in,
    act_ref,
    pooled_ref,
    unfolded_ref,
    weight_ref,
    chars_ref,
    mixed_ref,
    final_ref,
    embedded_ref,
    values,
    ids_turned,
    ids_wide,
    table_wide,
    high,
    proj,
    sems,
    near_sems,
    far_sems,
    go_near,
    near,
    go_far,
    far,
):
    where = place_of()
    y, z, core, x = where
    rows_each = FILTERS // HIGH_PARTS
    loads = []
    for part in range(HIGH_PARTS):
        rows = pl.ds(part * rows_each, rows_each)
        loads.append(pltpu.make_async_copy(high_in.at[0, rows], high.at[rows], sems.at[part]))
    loads.append(pltpu.make_async_copy(proj_in, proj, sems.at[HIGH_PARTS]))
    for load in loads:
        load.start()

    near_peers, far_peers = near_peers_of(where), far_peers_of(where)
    barrier = pltpu.get_barrier_semaphore()
    for _, _, device in near_peers + far_peers:
        pl.semaphore_signal(barrier, inc=1, device_id=device, device_id_type=MESH)

    lane = lax.broadcasted_iota(jnp.int32, (WORDS, 128), 1)
    row = lax.broadcasted_iota(jnp.int32, (WORDS, 128), 0)
    home = home_ref[...]
    seat, spot = home // SEQ_LEN, lax.rem(home, SEQ_LEN)
    order = (lax.rem(seat, 2) * 4 + spot // WORDS) * 16 + seat // 2
    ids_turned[...] = jnp.full((128, WORDS), -1.0, F32)
    place = lax.broadcasted_iota(jnp.int32, (WORD_CHARS, WORDS), 0)
    ids_turned[0:WORD_CHARS, :] = jnp.where(place < lengths_ref[...], ids_ref[...], -1).astype(F32)
    carried = jnp.where(row == 127, lax.rem(spot, WORDS).astype(F32), ids_turned[...]).T
    carried = exact_dot(jnp.where(order == row, 1.0, 0.0), carried)
    go_near[...] = carried.reshape(8, 16, 128)
    pl.semaphore_wait(barrier, len(near_peers) + len(far_peers))
    sent = exchange(near_peers, core * 4 + x, (near_sems.at[0], near_sems.at[1]), go_near, near)
    turn = jnp.where(lane == lax.rem(row, 8) * 16 + row // 8, 1.0, 0.0)
    go_far[...] = exact_dot(turn, near[...].reshape(WORDS, 128)).reshape(16, 8, 128)
    sent += exchange(far_peers, y * 4 + z, (far_sems.at[0], far_sems.at[1]), go_far, far)
    arrived = far[...].reshape(WORDS, 128)
    slots = jnp.sum(jnp.where(lane == 127, arrived, 0.0), -1, keepdims=True)
    placed = jnp.where(slots == lane.astype(F32), 1.0, 0.0).T
    placed = jnp.where(lane < WORD_CHARS, exact_dot(placed, arrived), -1.0)
    ids_wide[...] = placed.astype(jnp.int32)
    chars_ref[...] = placed.T.astype(jnp.int32)

    code = lax.broadcasted_iota(jnp.int32, (WORDS, 384), 1)
    spread_lane = lax.broadcasted_iota(jnp.int32, (CHAR_DIM, 128), 1)
    spread_row = lax.broadcasted_iota(jnp.int32, (CHAR_DIM, 128), 0)
    spread = jnp.logical_and(lax.rem(spread_lane, CHAR_DIM) == spread_row, spread_lane < BIAS_ROW)
    spread = jnp.where(spread, 1.0, 0.0).astype(BF16)
    table_wide[...] = jnp.zeros((384, 128), BF16)
    table_wide[0:CHARS, :] = first_dot(table_ref[...], spread).astype(BF16)
    values[WORD_CHARS:, :, :] = jnp.zeros((TAPS - 1, WORDS, 128), F32)

    def look_up(place, ids):
        column = ids[:, :1]
        onehot = (column == code).astype(F32).astype(BF16)
        found = dot(onehot, table_wide[...])
        found = jnp.where(lane == BIAS_ROW, 1.0, found)
        absent = jnp.where(column < 0, 1.0, 0.0)
        values[place] = jnp.where(lane == ABSENT_ROW, absent, found)
        return pltpu.roll(ids, 127, 1)

    lax.fori_loop(0, WORD_CHARS, look_up, ids_wide[...], unroll=5)

    @pl.loop(0, WORD_CHARS)
    def _(place):
        taps = values[place]
        for tap in range(1, TAPS):
            taps = jnp.where(lane // CHAR_DIM == tap, values[place + tap], taps)
        unfolded_ref[place] = taps.astype(BF16)

    @pl.loop(0, FILTERS // POOL_COLS)
    def _(block):
        cols = pl.ds(pl.multiple_of(block * POOL_COLS, POOL_COLS), POOL_COLS)
        filters = lax.broadcasted_iota(jnp.int32, (BIAS_ROW, POOL_COLS), 1) + block * POOL_COLS
        tap_rows = lax.broadcasted_iota(jnp.int32, (BIAS_ROW, POOL_COLS), 0) // CHAR_DIM
        widths = jnp.ones((BIAS_ROW, POOL_COLS), jnp.int32)
        for bound in (1, 2, 4, 8, 16, 32):
            widths = widths + (filters >= FILTERS // 64 * bound).astype(jnp.int32)
        masked = jnp.where(tap_rows < widths, conv_ref[:, cols].astype(F32), 0.0)
        rest_row = lax.broadcasted_iota(jnp.int32, (128 - BIAS_ROW, POOL_COLS), 0)
        rest = jnp.where(rest_row == 0, conv_bias_ref[:, cols].astype(F32), 0.0)
        rest = jnp.where(rest_row == ABSENT_ROW - BIAS_ROW, NEG_LARGE, rest)
        weight = jnp.concatenate([masked, rest], axis=0).astype(BF16)
        weight_ref[:, cols] = weight

        def convolve(step, state):
            top, total = state
            left = unfolded_ref[pl.ds(POOL_STEP * step, POOL_STEP)]
            rows = dot(left.reshape(POOL_STEP * WORDS, 128), weight)
            rows = rows.reshape(POOL_STEP, WORDS, POOL_COLS)
            higher = jnp.maximum(top, jnp.max(rows, axis=0))
            more = jnp.sum(jnp.exp(rows - higher[None]), axis=0)
            return higher, total * jnp.exp(top - higher) + more

        top, total = lax.fori_loop(
            0,
            WORD_CHARS // POOL_STEP,
            convolve,
            (jnp.full((WORDS, POOL_COLS), -3e38, F32), jnp.zeros((WORDS, POOL_COLS), F32)),
        )
        pooled = top + jnp.log(total)
        pooled_ref[:, cols] = pooled
        act_ref[:, cols] = jax.nn.gelu(pooled).astype(BF16)

    for load in loads:
        load.wait()
    act = act_ref[...]
    for start in range(0, FILTERS, 512):
        near_cols, far_cols = slice(start, start + 512), slice(FILTERS + start, FILTERS + start + 512)
        mixed = dot(act, high[:, near_cols]) + high_bias_ref[:, near_cols].astype(F32)
        gates = dot(act, high[:, far_cols]) + high_bias_ref[:, far_cols].astype(F32)
        mixed_ref[:, near_cols] = mixed
        mixed_ref[:, far_cols] = gates
        carry = jax.nn.sigmoid(gates)
        final = carry * act[:, near_cols].astype(F32) + (1.0 - carry) * jax.nn.gelu(mixed)
        final_ref[:, near_cols] = final.astype(BF16)
    embedded_ref[...] = dot(final_ref[...], proj[...]).astype(BF16)
    for copy in sent:
        copy.wait_send()


def embed_words(ids, lengths, home, table, conv, conv_bias, high, high_bias, proj):
    whole = pl.BlockSpec(memory_space=pltpu.VMEM)
    outside = pl.BlockSpec(memory_space=pl.ANY)
    shapes = [
        ((WORDS, FILTERS), BF16),
        ((WORDS, FILTERS), F32),
        ((WORD_CHARS, WORDS, 128), BF16),
        ((128, FILTERS), BF16),
        ((128, WORDS), jnp.int32),
        ((WORDS, 2 * FILTERS), F32),
        ((WORDS, FILTERS), BF16),
        ((WORDS, D), BF16),
    ]
    dma = pltpu.SemaphoreType.DMA
    return pl.pallas_call(
        embed_kernel,
        out_shape=tuple(jax.ShapeDtypeStruct(*shape) for shape in shapes),
        in_specs=[whole] * 6 + [outside, whole, outside],
        out_specs=tuple(whole for _ in shapes),
        scratch_shapes=[
            pltpu.VMEM((WORD_CHARS + TAPS - 1, WORDS, 128), F32),
            pltpu.VMEM((128, WORDS), F32),
            pltpu.VMEM((WORDS, 128), jnp.int32),
            pltpu.VMEM((384, 128), BF16),
            pltpu.VMEM((FILTERS, 2 * FILTERS), BF16),
            pltpu.VMEM((FILTERS, D), BF16),
            dma((HIGH_PARTS + 1,)),
            dma((2, 8)),
            dma((2, 16)),
            pltpu.VMEM((8, 16, 128), F32),
            pltpu.VMEM((8, 16, 128), F32),
            pltpu.VMEM((16, 8, 128), F32),
            pltpu.VMEM((16, 8, 128), F32),
        ],
        compiler_params=pltpu.CompilerParams(
            collective_id=3, has_side_effects=True, vmem_limit_bytes=60 << 20
        ),
    )(ids, lengths, home, table, conv, conv_bias, high, high_bias, proj)


Y, Z, X = 0, 1, 2
LEFT_COLS = {"high": 2048, "proj": 2048, "qkv": 768, "out": 768, "up": 768, "down": 3072}
RIGHT_COLS = {"high": 4096, "proj": 768, "qkv": 2304, "out": 768, "up": 3072, "down": 768}
CHUNK_ROWS = {"high": 16, "proj": 16, "qkv": 6, "out": 6, "up": 6, "down": 24}

PIECES = {
    "high": (("high", 0, 0, 1, 0, 2048), ("high", 0, 2048, 1, 2048, 2048)),
    "proj": (("proj", 0, 0, 1, 0, 768),),
    "qkv": (("qkv", 0, 0, 0, 1152, 1152),),
    "out": (("out", 0, 0, 0, 384, 384),),
    "up": (("up", 0, 0, 0, 1536, 1536),),
    "down": (("down", 0, 0, 1, 0, 768), ("down", 2, 0, 2, 384, 384)),
}


def cut(pieces, widths):
    parts, rest = [], list(pieces)
    for width in widths:
        part, room = [], width
        while room:
            name, upper, upper_at, lower, lower_at, cols = rest.pop(0)
            used = min(cols, room)
            part.append((name, upper, upper_at, lower, lower_at, used))
            room -= used
            if used < cols:
                rest.insert(
                    0, (name, upper, upper_at + used, lower, lower_at + used, cols - used)
                )
        parts.append(tuple(part))
    assert not rest
    return tuple(parts)


def narrow(piece, most):
    name, upper, upper_at, lower, lower_at, cols = piece
    start = 0
    while start < cols:
        used = min(most, cols - start)
        yield (name, upper, upper_at + start, lower, lower_at + start, used, start)
        start += used


class Plan:
    def __init__(self, names, streams, plain=()):
        self.names = names
        self.stream_names, self.parts = [], []
        self.groups, self.group_at, self.right_at = 0, {}, {}
        self.right_cols = 0
        for name in names:
            self.group_at[name] = self.groups
            self.groups += -(-CHUNK_ROWS[name] // 8)
            self.right_at[name] = self.right_cols
            self.right_cols += RIGHT_COLS[name]
        for stream, (of, pieces, orders, widths) in enumerate(streams):
            self.stream_names.append(of)
            for order, part, width in zip(orders, cut(pieces, widths), widths, strict=True):
                self.parts.append((stream, order, part, width))
        for stream, order, width in plain:
            self.parts.append((stream, order, (), width))

    def scratch(self):
        dma = pltpu.SemaphoreType.DMA
        shapes = [
            pltpu.VMEM((self.groups, 4, 128, 2 * WORDS), BF16),
            pltpu.VMEM((self.groups, 4, 128, WORDS), BF16),
            pltpu.VMEM((2 * WORDS, self.right_cols), BF16),
            dma((2, len(self.names))),
            dma((2, len(self.names))),
            dma((2, len(self.parts), 15)),
        ]
        for _, _, _, width in self.parts:
            shapes += [
                pltpu.VMEM((4, 4, 4, 16, width), BF16),
                pltpu.VMEM((2, 2, 4, 16, width), BF16),
                pltpu.VMEM((2, 4, 4, 16, width), BF16),
                pltpu.VMEM((2, 2, 16, width), BF16),
                pltpu.VMEM((2, 4, 16, width), BF16),
                pltpu.VMEM((3, 16, width), BF16),
            ]
        return shapes


ORDERS = ((Y, Z, X), (Z, X, Y), (X, Y, Z))
DOWN_PLAN = Plan(("down",), ((("down",), PIECES["down"], ((Y, Z, X), (Z, Y, X)), (640, 512)),))
LATE_PLAN = Plan(
    ("proj", "qkv", "out", "up"),
    (
        (("up",), PIECES["up"], ORDERS, (512, 512, 512)),
        (
            ("proj", "qkv", "out"),
            PIECES["qkv"] + PIECES["out"] + PIECES["proj"],
            ORDERS,
            (768, 768, 768),
        ),
    ),
    plain=(
        (2, (Y, Z, X), 128),
        (3, (Z, X, Y), 384),
        (3, (X, Z, Y), 128),
        (4, (Y, X, Z), 384),
        (4, (X, Y, Z), 128),
    ),
)
CONV, DEALT = 2, {Y: 3, Z: 4}
RING_WORDS = 8 * WORDS
DEAL_COLS = 512
SHARED = ((16, D), (16, 384), (8, FILTERS))


class Part:
    def __init__(self, order, refs, sems, where):
        self.tiles, self.relay1, self.last1, self.relay2, self.last2, self.last3 = refs
        self.order, self.sems, self.where = order, sems, where
        self.width = self.tiles.shape[-1]
        y, z, core, x = where
        self.here = [(y, z, x)[axis] for axis in order]
        self.copies = {}

    def peer(self, level, step):
        y, z, core, x = self.where
        spot = [y, z, x]
        spot[self.order[level]] = around(self.here[level], step)
        return device_of(spot[0], spot[1], core, spot[2])

    def start(self, index, source, target, level, step):
        copy = remote(source, target, self.sems, index, self.peer(level, step))
        copy.start()
        self.copies[index] = copy

    def slices(self, level):
        prefix = tuple(self.here[:level])
        return lambda at, half=None: self.tiles.at[
            prefix + (at,) + (() if half is None else (pl.ds(2 * half, 2),))
        ]

    def buffers(self, level):
        return (self.relay1, self.last1) if level == 0 else (self.relay2, self.last2)

    def ring_start(self, level):
        me, base, tiles = self.here[level], 6 * level, self.slices(level)
        relay, last = self.buffers(level)
        far, right, left = around(me, 2), around(me, 1), around(me, 3)
        self.start(base, tiles(far, 0), relay.at[0], level, 1)
        self.start(base + 1, tiles(far, 1), relay.at[1], level, 3)
        self.start(base + 2, tiles(right, 1), last.at[0, pl.ds(2, 2)], level, 1)
        self.start(base + 3, tiles(left, 0), last.at[1, pl.ds(0, 2)], level, 3)

    def ring_relay(self, level):
        me, base, tiles = self.here[level], 6 * level, self.slices(level)
        relay, last = self.buffers(level)
        for side in (0, 1):
            target = tiles(around(me, (1, 3)[side]), side)
            self.copies[base + side].wait_recv()
            self.add(target, (relay.at[side],), 3 - level)
            self.start(
                base + 4 + side, target, last.at[side, pl.ds(2 * side, 2)], level, (1, 3)[side]
            )

    def ring_end(self, level):
        me, base, tiles = self.here[level], 6 * level, self.slices(level)
        _, last = self.buffers(level)
        for index in range(2, 6):
            self.copies[base + index].wait_recv()
        self.add(tiles(me), (last.at[0], last.at[1]), 3 - level)

    def add(self, target, terms, dims):
        lead = target.shape[:-2]
        count = 1
        for size in lead:
            count *= size

        @pl.loop(0, count)
        def _(flat):
            at, rest = [], flat
            for size in reversed(lead):
                at.insert(0, lax.rem(rest, size))
                rest = rest // size
            at = tuple(at)
            total = target[at].astype(F32)
            for term in terms:
                total = total + term[at].astype(F32)
            target[at] = total.astype(BF16)

    def direct_start(self):
        for step in (1, 2, 3):
            source = self.tiles.at[self.here[0], self.here[1], around(self.here[2], step)]
            self.start(11 + step, source, self.last3.at[step - 1], 2, step)

    def dealt_end(self, out, start):
        for step in (0, 1, 2, 3):
            if step:
                self.copies[11 + step].wait_recv()
                block = self.last3[step - 1]
            else:
                block = self.tiles[tuple(self.here)]
            column = around(self.here[2], 4 - step) * DEAL_COLS + start
            out[:, pl.ds(pl.multiple_of(column, 128), self.width)] = block.astype(F32)

    def direct_end(self):
        total = self.tiles[tuple(self.here)].astype(F32)
        for step in (1, 2, 3):
            self.copies[11 + step].wait_recv()
            total = total + self.last3[step - 1].astype(F32)
        return total

    def sent(self):
        for copy in self.copies.values():
            copy.wait_send()


class Shared:
    def __init__(self, pair, rings, sems, where):
        self.pair, self.rings, self.sems, self.where = pair, rings, sems, where
        self.copies = []

    def start(self, level, value):
        y, z, core, x = self.where
        if level == 0:
            self.pair[core] = value
            mine = self.pair.at[core]
            peers = [device_of(y, z, 1 - core, x)]
            targets = mine
        else:
            axis = level - 1
            here = (y, z, x)[axis]
            self.rings[axis, here] = value
            mine = self.rings.at[axis, here]
            peers = []
            for step in (1, 2, 3):
                spot = [y, z, x]
                spot[axis] = around(here, step)
                peers.append(device_of(spot[0], spot[1], core, spot[2]))
            targets = mine
        base = 0 if level == 0 else 3 * level - 2
        self.now = []
        for number, peer in enumerate(peers):
            copy = remote(mine, targets, self.sems, base + number, peer)
            copy.start()
            self.now.append(copy)
        self.copies += self.now

    def end(self, level):
        for copy in self.now:
            copy.wait_recv()
        if level == 0:
            return self.pair[0] + self.pair[1]
        ring = self.rings.at[level - 1]
        return (ring[0] + ring[1]) + (ring[2] + ring[3])

    def sent(self):
        for copy in self.copies:
            copy.wait_send()


def pick(rows_per_chunk, group, core, blocks, lanes):
    rows = blocks * 32
    row = lax.broadcasted_iota(jnp.int32, (rows, lanes), 0)
    lane = lax.broadcasted_iota(jnp.int32, (rows, lanes), 1)
    inner = lax.rem(row, 8) + 8 * group
    wanted = ((row // 32 * 2 + core) * 4 + lax.rem(row // 8, 4)) * rows_per_chunk + inner
    hit = jnp.logical_and(wanted == lane, inner < rows_per_chunk)
    return jnp.where(hit, 1.0, 0.0).astype(BF16)


PICK_LANES = {16: 512, 6: 384, 24: 768}


class Sums:
    def __init__(self, plan, refs, where):
        self.plan, self.where = plan, where
        y, z, core, x = where
        self.partner = device_of(y, z, 1 - core, x)
        self.left, self.left_out, self.right, left_sems, right_sems, part_sems = refs[:6]
        self.left_sems = (left_sems.at[0], left_sems.at[1])
        self.right_sems = (right_sems.at[0], right_sems.at[1])
        self.parts = []
        for at, (_, order, _, _) in enumerate(plan.parts):
            sems = (part_sems.at[0, at], part_sems.at[1, at])
            self.parts.append(Part(order, refs[6 + 6 * at : 12 + 6 * at], sems, where))
        self.picks, self.copies = {}, {}

    def right_part(self, name, mine):
        cols = pl.ds(self.plan.right_at[name], RIGHT_COLS[name])
        return self.right.at[pl.ds(0 if mine else WORDS, WORDS), cols]

    def send_right(self, name, source):
        copy = remote(
            source,
            self.right_part(name, False),
            self.right_sems,
            self.plan.names.index(name),
            self.partner,
        )
        copy.start()
        self.copies["right", name] = copy

    def picked(self, rows_per_chunk, group, mine):
        key = (rows_per_chunk, group, mine)
        if key not in self.picks:
            lanes = PICK_LANES[rows_per_chunk]
            core = self.where[2] if mine else 1 - self.where[2]
            self.picks[key] = pick(
                rows_per_chunk, group, core, lanes // (8 * rows_per_chunk), lanes
            )
        return self.picks[key]

    def send_left(self, name, source):
        rows_per_chunk = CHUNK_ROWS[name]
        lanes = PICK_LANES[rows_per_chunk]
        ys = lanes // (32 * rows_per_chunk)
        groups = -(-rows_per_chunk // 8)
        first = self.plan.group_at[name]
        for mine in (False, True):
            for group in range(groups):
                for block in range(4 // ys):
                    columns = source[:, block * lanes : (block + 1) * lanes]
                    rows = back_dot(self.picked(rows_per_chunk, group, mine), columns)
                    rows = rows.astype(BF16).reshape(ys, 128, WORDS)
                    span = pl.ds(block * ys, ys)
                    if mine:
                        self.left[first + group, span, :, 0:WORDS] = rows
                    else:
                        self.left_out[first + group, span] = rows
            if not mine:
                span = pl.ds(first, groups)
                copy = remote(
                    self.left_out.at[span],
                    self.left.at[span, :, :, pl.ds(WORDS, WORDS)],
                    self.left_sems,
                    self.plan.names.index(name),
                    self.partner,
                )
                copy.start()
                self.copies["left", name] = copy

    def multiply(self, stream):
        for name in self.plan.stream_names[stream]:
            self.copies["right", name].wait_recv()
            self.copies["left", name].wait_recv()
        for at, (of, order, pieces, _) in enumerate(self.plan.parts):
            if of != stream:
                continue
            tiles = self.parts[at].tiles
            offset = 0
            for piece in pieces:
                for name, upper, upper_at, lower, lower_at, cols, start in narrow(piece, 512):
                    base, first = self.plan.right_at[name], self.plan.group_at[name]
                    lanes = pl.ds(offset + start, cols)

                    @pl.loop(0, 4, unroll=4)
                    def _(row):
                        halves = []
                        for group, column in ((upper, upper_at), (lower, lower_at)):
                            factor = self.right[:, base + column : base + column + cols]
                            block = dot(self.left[first + group, row], factor)
                            halves.append(block.reshape(16, 1, 8, cols))
                        both = jnp.concatenate(halves, axis=1).reshape(4, 4, 16, cols)
                        both = both.astype(BF16)
                        for at_z in range(4):
                            for at_x in range(4):
                                spot = tuple((row, at_z, at_x)[axis] for axis in order)
                                tiles[spot + (slice(None), lanes)] = both[at_z, at_x]

                offset += piece[5]
        self.each(stream, lambda part: part.ring_start(0))

    def each(self, stream, action):
        for at, (of, _, _, _) in enumerate(self.plan.parts):
            if of == stream:
                action(self.parts[at])

    def relay1(self, stream):
        self.each(stream, lambda part: part.ring_relay(0))

    def end1(self, stream):
        self.each(stream, lambda part: (part.ring_end(0), part.ring_start(1)))

    def relay2(self, stream):
        self.each(stream, lambda part: part.ring_relay(1))

    def end2(self, stream):
        self.each(stream, lambda part: (part.ring_end(1), part.direct_start()))

    def finish(self, stream, outs):
        for at, (of, _, pieces, _) in enumerate(self.plan.parts):
            if of != stream:
                continue
            total = self.parts[at].direct_end()
            if not pieces:
                outs[...] = total
            offset = 0
            for name, upper, upper_at, lower, lower_at, cols in pieces:
                block = total[:, offset : offset + cols]
                for group, column, top in ((upper, upper_at, 0), (lower, lower_at, 8)):
                    rows = min(8, CHUNK_ROWS[name] - 8 * group)
                    outs[name][8 * group : 8 * group + rows, column : column + cols] = block[
                        top : top + rows
                    ]
                offset += cols

    def sent(self):
        for part in self.parts:
            part.sent()
        for copy in self.copies.values():
            copy.wait_send()


def sums_peers(where):
    y, z, core, x = where
    peers = [device_of(y, z, 1 - core, x)]
    for step in (1, 2, 3):
        peers.append(device_of(around(y, step), z, core, x))
        peers.append(device_of(y, around(z, step), core, x))
        peers.append(device_of(y, z, core, around(x, step)))
    return peers


PAIRS = HEADS // 2
GELU_SCALE = 0.7978845608028654
GELU_CUBE = 0.044715
FF_COLS = 512


def gelu_both(value):
    square = value * value
    bend = jnp.tanh(GELU_SCALE * value * (1.0 + GELU_CUBE * square))
    half = 0.5 * (1.0 + bend)
    slope = half + 0.5 * GELU_SCALE * value * (1.0 - bend * bend) * (
        1.0 + 3.0 * GELU_CUBE * square
    )
    return value * half, slope


def encoder_kernel(*refs):
    rest = list(refs)

    def take(count):
        taken = rest[:count]
        del rest[:count]
        return taken

    rows_in, act, length_in, gains, shifts, cotangent = take(6)
    weights_in = take(4)
    out_hidden, out_first, out_context, out_joint, out_attn, out_rows = take(6)
    out_middle, out_up, out_norms, out_down = take(4)
    out_rings = dict(zip((Y, Z), take(2)))
    sums_refs = take(6 + 6 * len(DOWN_PLAN.parts))
    weights = take(4)
    (hidden_rows,) = take(1)
    high_out, high_sems, ring_sems, store_sems = take(4)
    rings = dict(zip((Y, Z), take(2)))
    load_sems, keys_sems, sums_sems = take(3)
    joint, both, probs, probs_low, slopes = take(5)
    grads, relay, last = take(3)
    keys_sems = (keys_sems.at[0], keys_sems.at[1])
    sums_sems = (sums_sems.at[0], sums_sems.at[1])

    where = place_of()
    y, z, core, x = where
    sums = Sums(DOWN_PLAN, sums_refs, where)
    loads = []
    for at in range(4):
        loads.append(pltpu.make_async_copy(weights_in[at], weights[at], load_sems.at[at]))
        loads[at].start()
    qkv_w, out_w, up_w, down_w = weights

    right = device_of(y, z, core, around(x, 1))
    left = device_of(y, z, core, around(x, 3))

    barrier = pltpu.get_barrier_semaphore()
    greeted = sums_peers(where)
    for device in greeted:
        pl.semaphore_signal(barrier, inc=1, device_id=device, device_id_type=MESH)

    lane = lax.broadcasted_iota(jnp.int32, (WORDS, WORDS), 1)
    one_hot = lambda hit: jnp.where(hit, 1.0, 0.0).astype(BF16)
    sent = []
    word_rows = rows_in[...].astype(F32)
    gain = [gains[at : at + 1, :].astype(F32) for at in range(3)]
    shift = [shifts[at : at + 1, :].astype(F32) for at in range(3)]
    first_f, first_normal, first_inv = norm_parts(word_rows, gain[0], shift[0])
    first_norm = first_f.astype(BF16)
    out_first[...] = first_norm
    loads[0].wait()
    pl.semaphore_wait(barrier, len(greeted))
    for start in (D, 2 * D, 0):
        cols = slice(start, start + D)
        joint[:, cols] = dot(first_norm, qkv_w[:, cols]).astype(BF16)
        if start:
            half = pl.ds(start - D, D)
            both[x, :, start - D : start] = joint[:, cols]
            for side, device in ((0, right), (1, left)):
                copy = remote(
                    both.at[x, :, half], both.at[x, :, half], keys_sems, start // D * 2 + side, device
                )
                copy.start()
                sent.append(copy)
    key_right, key_left, value_right, value_left = sent[-4:]

    span = lambda at: pl.ds(pl.multiple_of(at * 2 * WORDS, 128), 2 * WORDS)
    mine = lambda at: pl.ds(pl.multiple_of(at * 2 * WORDS, 128), WORDS)
    theirs = lambda at: pl.ds(pl.multiple_of(at * 2 * WORDS + WORDS, 128), WORDS)
    spots = {Y: y, Z: z}
    partner = device_of(y, z, 1 - core, x)
    for keep in (False, True):
        for group in range(2):
            chosen = sums.picked(16, group, keep)
            for block in range(4):
                rows = back_dot(chosen, act[:, block * 512 : (block + 1) * 512]).astype(BF16)
                if not keep:
                    high_out[group, block] = rows
                    continue
                for axis, spot in spots.items():
                    rings[axis][group, block, :, mine(spot)] = rows
        if not keep:
            for axis, spot in spots.items():
                copy = remote(
                    high_out,
                    rings[axis].at[:, :, :, theirs(spot)],
                    (high_sems.at[0], high_sems.at[1]),
                    axis,
                    partner,
                )
                copy.start()
                sent.append(copy)
    for copy in sent[-2:]:
        copy.wait_recv()
    gathers = {}

    def gather(axis, index, source, group, step):
        place = [y, z, x]
        place[axis] = around(spots[axis], step)
        view = rings[axis].at[:, :, :, span(source)]
        if group is not None:
            view = rings[axis].at[group, :, :, span(source)]
        copy = remote(
            view,
            view,
            (ring_sems.at[0, axis], ring_sems.at[1, axis]),
            index,
            device_of(place[0], place[1], core, place[2]),
        )
        copy.start()
        sent.append(copy)
        gathers[axis, index] = copy

    for axis, spot in spots.items():
        gather(axis, 0, spot, None, 1)
        gather(axis, 1, spot, None, 3)
    key_right.wait_recv()
    behind, ahead = around(x, 3), around(x, 1)
    pass_key = remote(
        both.at[behind, :, pl.ds(0, D)], both.at[behind, :, pl.ds(0, D)], keys_sems, 0, right
    )
    pass_key.start()
    value_left.wait_recv()
    pass_value = remote(
        both.at[ahead, :, pl.ds(D, D)], both.at[ahead, :, pl.ds(D, D)], keys_sems, 1, left
    )
    pass_value.start()
    sent += [pass_key, pass_value]
    for copy in (key_left, value_right, pass_key, pass_value):
        copy.wait_recv()

    scale = HEAD_DIM ** (-0.5)
    low_lanes = one_hot(lane < HEAD_DIM)
    high_lanes = one_hot(lane >= HEAD_DIM)
    valid = lax.broadcasted_iota(jnp.int32, (1, SEQ_LEN), 1) < length_in[...]

    def stacked(rows):
        return jnp.concatenate([rows * low_lanes, rows * high_lanes], axis=0)

    def unstacked(rows):
        return jnp.where(lane < HEAD_DIM, rows[:WORDS], rows[WORDS:])

    for pair in range(PAIRS):
        cols = slice(pair * 128, pair * 128 + 128)
        keys = both[:, :, cols].reshape(SEQ_LEN, 128)
        values = both[:, :, D + pair * 128 : D + pair * 128 + 128].reshape(SEQ_LEN, 128)
        scores = back_dot(stacked(joint[:, cols]), keys) * scale
        masked = jnp.where(valid, scores, NEG_LARGE)
        top = jnp.max(masked, -1, keepdims=True)
        expo = jnp.where(valid, jnp.exp(masked - top), 0.0)
        share = expo / jnp.sum(expo, -1, keepdims=True)
        probs[pair] = share
        share = share.astype(BF16)
        probs_low[pair] = share
        out_context[:, cols] = unstacked(dot(share, values)).astype(BF16)
    for axis, spot in spots.items():
        for index, step in ((0, 1), (1, 3)):
            gathers[axis, index].wait_recv()
            gather(axis, 2 + index, around(spot, 4 - step), index, step)
    loads[1].wait()
    attn_out = dot(out_context[...], out_w[...])
    mid_f, mid_normal, mid_inv = norm_parts(first_norm.astype(F32) + attn_out, gain[1], shift[1])
    middle = mid_f.astype(BF16)
    out_middle[...] = middle
    loads[2].wait()
    loads[3].wait()

    down_proj = jnp.zeros((WORDS, D), F32)
    for block in range(FF // FF_COLS):
        cols = slice(block * FF_COLS, (block + 1) * FF_COLS)
        act, slope = gelu_both(dot(middle, up_w[:, cols]))
        act = act.astype(BF16)
        slopes[:, cols] = slope
        hidden_rows[:, cols] = act
        down_proj = down_proj + dot(act, down_w[cols, :])
    out_f, out_normal, out_inv = norm_parts(middle.astype(F32) + down_proj, gain[2], shift[2])
    out_hidden[...] = out_f.astype(BF16)

    def note(which, gain_row, shift_row):
        out_norms[which : which + 1, :] = gain_row[None]
        out_norms[3 + which : 4 + which, :] = shift_row[None]

    grad_pre2, gain_row, shift_row = norm_back(
        cotangent[...].astype(F32), out_normal, out_inv, gain[2]
    )
    note(2, gain_row, shift_row)
    grad_down = grad_pre2.astype(BF16)
    sums.right_part("down", True)[...] = grad_down
    sums.send_right("down", sums.right_part("down", True))
    sums.send_left("down", hidden_rows)
    grad_mid = grad_pre2
    for block in range(FF // FF_COLS):
        cols = slice(block * FF_COLS, (block + 1) * FF_COLS)
        grad_up = (slopes[:, cols] * back_dot(grad_down, down_w[cols, :])).astype(BF16)
        out_up[:, cols] = grad_up
        grad_mid = grad_mid + back_dot(grad_up, up_w[:, cols])
    grad_pre1, gain_row, shift_row = norm_back(grad_mid, mid_normal, mid_inv, gain[1])
    note(1, gain_row, shift_row)
    grad_attn = grad_pre1.astype(BF16)
    out_attn[...] = grad_attn
    grad_context = back_dot(grad_attn, out_w[...]).astype(BF16)
    stores = []
    for axis in spots:
        for index in (2, 3):
            gathers[axis, index].wait_recv()
        stores.append(pltpu.make_async_copy(rings[axis], out_rings[axis], store_sems.at[axis]))
        stores[-1].start()
    sums.multiply(0)

    for pair in range(PAIRS):
        cols = slice(pair * 128, pair * 128 + 128)
        value_cols = slice(D + pair * 128, D + pair * 128 + 128)
        keys = both[:, :, cols].reshape(SEQ_LEN, 128)
        values = both[:, :, value_cols].reshape(SEQ_LEN, 128)
        grad_rows = stacked(grad_context[:, cols])
        share = probs[pair]
        grad_probs = back_dot(grad_rows, values)
        delta = jnp.sum(share * grad_probs, -1, keepdims=True)
        grad_scores = (share * (grad_probs - delta)).astype(BF16)
        grad_query = unstacked(dot(grad_scores, keys)) * scale
        out_joint[:, cols] = grad_query.astype(BF16)
        grad_keys = first_dot(grad_scores, stacked(joint[:, cols])) * scale
        grads[:, :, cols] = grad_keys.astype(BF16).reshape(4, WORDS, 128)
        grad_values = first_dot(probs_low[pair], grad_rows)
        grads[:, :, value_cols] = grad_values.astype(BF16).reshape(4, WORDS, 128)

    key_half, value_half = pl.ds(0, D), pl.ds(D, D)
    opposite = around(x, 2)
    steps = [
        remote(grads.at[opposite, :, key_half], relay.at[0], sums_sems, 0, right),
        remote(grads.at[opposite, :, value_half], relay.at[1], sums_sems, 1, left),
        remote(grads.at[ahead, :, value_half], last.at[0, :, value_half], sums_sems, 2, right),
        remote(grads.at[behind, :, key_half], last.at[1, :, key_half], sums_sems, 3, left),
    ]
    for copy in steps:
        copy.start()
    sums.relay1(0)
    steps[0].wait_recv()
    grads[ahead, :, 0:D] = (grads[ahead, :, 0:D].astype(F32) + relay[0].astype(F32)).astype(BF16)
    steps.append(
        remote(grads.at[ahead, :, key_half], last.at[0, :, key_half], sums_sems, 4, right)
    )
    steps[4].start()
    steps[1].wait_recv()
    grads[behind, :, D:] = (grads[behind, :, D:].astype(F32) + relay[1].astype(F32)).astype(BF16)
    steps.append(
        remote(grads.at[behind, :, value_half], last.at[1, :, value_half], sums_sems, 5, left)
    )
    steps[5].start()
    sent += steps
    sums.end1(0)
    for copy in steps[2:]:
        copy.wait_recv()
    total = grads[x].astype(F32) + last[0].astype(F32) + last[1].astype(F32)
    out_joint[:, D:] = total.astype(BF16)

    grad_first = grad_pre1
    for start in range(0, 3 * D, D):
        cols = slice(start, start + D)
        grad_first = grad_first + back_dot(out_joint[:, cols], qkv_w[:, cols])
    grad_words, gain_row, shift_row = norm_back(grad_first, first_normal, first_inv, gain[0])
    note(0, gain_row, shift_row)

    out_rows[...] = grad_words.astype(BF16)
    sums.relay2(0)
    sums.end2(0)
    sums.finish(0, {"down": out_down})
    for copy in sent:
        copy.wait_send()
    for store in stores:
        store.wait()
    sums.sent()


def encode(rows, act, length, gains, shifts, cotangent, weights):
    whole = pl.BlockSpec(memory_space=pltpu.VMEM)
    shapes = [(WORDS, D)] * 3 + [(WORDS, 3 * D)] + [(WORDS, D)] * 3 + [(WORDS, FF)]
    out_shapes = [jax.ShapeDtypeStruct(shape, BF16) for shape in shapes]
    for shape in ((6, D), (CHUNK_ROWS["down"], D)):
        out_shapes.append(jax.ShapeDtypeStruct(shape, F32))
    ring_shape = (2, 4, 128, RING_WORDS)
    out_shapes += [jax.ShapeDtypeStruct(ring_shape, BF16)] * 2
    dma = pltpu.SemaphoreType.DMA
    return pl.pallas_call(
        encoder_kernel,
        out_shape=tuple(out_shapes),
        in_specs=[whole] * 6 + [pl.BlockSpec(memory_space=pl.ANY)] * 4,
        out_specs=(whole,) * (len(out_shapes) - 2) + (pl.BlockSpec(memory_space=pl.ANY),) * 2,
        scratch_shapes=[
            *DOWN_PLAN.scratch(),
            *(pltpu.VMEM(weight.shape, BF16) for weight in weights),
            pltpu.VMEM((WORDS, FF), BF16),
            pltpu.VMEM((2, 4, 128, WORDS), BF16),
            dma((2, 2)),
            dma((2, 2, 4)),
            dma((2,)),
            pltpu.VMEM(ring_shape, BF16),
            pltpu.VMEM(ring_shape, BF16),
            dma((4,)),
            dma((2, 6)),
            dma((2, 6)),
            pltpu.VMEM((WORDS, 3 * D), BF16),
            pltpu.VMEM((4, WORDS, 2 * D), BF16),
            pltpu.VMEM((PAIRS, 2 * WORDS, SEQ_LEN), F32),
            pltpu.VMEM((PAIRS, 2 * WORDS, SEQ_LEN), BF16),
            pltpu.VMEM((WORDS, FF), F32),
            pltpu.VMEM((4, WORDS, 2 * D), BF16),
            pltpu.VMEM((2, WORDS, D), BF16),
            pltpu.VMEM((2, WORDS, 2 * D), BF16),
        ],
        compiler_params=pltpu.CompilerParams(
            collective_id=2, has_side_effects=True, vmem_limit_bytes=62 << 20
        ),
    )(rows, act, length, gains, shifts, cotangent, *weights)


CONV_STEP = 10
CONV_COLS = 512
HIGH_ROWS = 256
HIGH_SLOTS = 3


def late_kernel(schedule, *refs):
    rest = list(refs)

    def take(count):
        taken = rest[:count]
        del rest[:count]
        return taken

    act, final_rows, first_norm, context, middle = take(5)
    chars, unfolded, conv_w, pooled, mixed, norms = take(6)
    right_in = dict(zip(("proj", "qkv", "out", "up"), take(4)))
    high_in, proj_in = take(2)
    rings_in = dict(zip((Y, Z), take(2)))
    outs = dict(zip(("high", "proj", "qkv", "out", "up"), take(5)))
    (out_conv,) = take(1)
    out_shared = take(3)
    sums_refs = take(6 + 6 * len(LATE_PLAN.parts))
    shared_refs = [take(2) for _ in SHARED]
    shared_sems, load_sems, high_sems = take(3)
    conv_back, conv_grad, conv_rows, conv_other, conv_sems = take(5)
    last_grad, table_grad, high_slots, proj, grad_pooled, small = take(6)
    grad_mixed, ring_sems, deal_sems, pair_sems = take(4)
    rings = dict(zip((Y, Z), take(2)))
    dealt = dict(zip((Y, Z), take(2)))
    conv_sems = (conv_sems.at[0], conv_sems.at[1])

    where = place_of()
    y, z, core, x = where
    partner = device_of(y, z, 1 - core, x)
    sums = Sums(LATE_PLAN, sums_refs, where)
    shared = [
        Shared(pair, rings, (shared_sems.at[0, at], shared_sems.at[1, at]), where)
        for at, (pair, rings) in enumerate(shared_refs)
    ]

    loads = {"proj_w": pltpu.make_async_copy(proj_in, proj, load_sems.at[4])}
    for at, name in enumerate(right_in):
        loads[name] = pltpu.make_async_copy(
            right_in[name], sums.right_part(name, True), load_sems.at[at]
        )
    for axis in (Y, Z):
        loads[axis] = pltpu.make_async_copy(rings_in[axis], rings[axis], ring_sems.at[axis])
    for load in loads.values():
        load.start()
    high_loads = [
        pltpu.make_async_copy(
            high_in.at[0, pl.ds(at * HIGH_ROWS, HIGH_ROWS)],
            high_slots.at[at % HIGH_SLOTS],
            high_sems.at[at],
        )
        for at in range(FILTERS // HIGH_ROWS)
    ]
    for at in range(HIGH_SLOTS):
        high_loads[at].start()

    barrier = pltpu.get_barrier_semaphore()
    peers = sums_peers(where)
    for device in peers:
        pl.semaphore_signal(barrier, inc=1, device_id=device, device_id_type=MESH)
    small[...] = jnp.zeros_like(small)
    small[0:6, :] = norms[...]
    pl.semaphore_wait(barrier, len(peers))
    for name in right_in:
        sums.send_right(name, right_in[name])

    def prepare(*names):
        for name in names:
            lefts = {"proj": final_rows, "qkv": first_norm, "out": context, "up": middle}
            sums.send_left(name, lefts[name])

    def multiply(stream):
        for name in LATE_PLAN.stream_names[stream]:
            if name in loads and name != "proj":
                loads[name].wait()
        sums.multiply(stream)

    def gates():
        loads["proj_w"].wait()
        loads["proj"].wait()
        grad_rows = sums.right_part("proj", True)[...]
        for start in range(0, FILTERS, 512):
            near, far = slice(start, start + 512), slice(FILTERS + start, FILTERS + start + 512)
            grad = back_dot(grad_rows, proj[near, :])
            carry = jax.nn.sigmoid(mixed[:, far])
            value, slope = gelu_both(mixed[:, near])
            grad_near = ((1.0 - carry) * slope * grad).astype(BF16)
            grad_far = (act[:, near].astype(F32) - value) * carry * (1.0 - carry) * grad
            grad_far = grad_far.astype(BF16)
            grad_mixed[:, near] = grad_near
            grad_mixed[:, far] = grad_far
            grad_pooled[:, near] = carry * grad
            for grads, at in ((grad_near, start), (grad_far, FILTERS + start)):
                total = jnp.sum(grads.astype(F32), 0, keepdims=True)
                for block in range(0, 512, 256):
                    line, lane_at = divmod(at + block, D)
                    small[6 + line : 7 + line, lane_at : lane_at + 256] = total[
                        :, block : block + 256
                    ]
        for axis, here in spots.items():
            share = lambda at: pl.ds(pl.multiple_of(axis * FILTERS + at * DEAL_COLS, 128), DEAL_COLS)
            rows = pl.ds(pl.multiple_of(here * 2 * WORDS, 128), WORDS)
            for step in (1, 2, 3):
                place = [y, z, x]
                place[axis] = around(here, step)
                copy = remote(
                    grad_mixed.at[:, share(place[axis])],
                    dealt[axis].at[rows, :],
                    (deal_sems.at[0, axis], deal_sems.at[1, axis]),
                    step,
                    device_of(place[0], place[1], core, place[2]),
                )
                copy.start()
                deals[axis, step] = copy
            dealt[axis][rows, :] = grad_mixed[:, share(here)]
            pass_on(axis, 0)

    spots = {Y: y, Z: z}
    deals, passes = {}, {}

    def pass_on(axis, step):
        source = around(spots[axis], 4 - step) * 2 * WORDS
        copy = remote(
            dealt[axis].at[pl.ds(pl.multiple_of(source, 128), WORDS), :],
            dealt[axis].at[pl.ds(pl.multiple_of(source + WORDS, 128), WORDS), :],
            (pair_sems.at[0, axis], pair_sems.at[1, axis]),
            step,
            partner,
        )
        copy.start()
        passes[axis, step] = copy

    def pass_all():
        for step in (1, 3, 2):
            for axis in spots:
                deals[axis, step].wait_recv()
                pass_on(axis, step)

    def multiply_high(axis):
        loads[axis].wait()
        for step in (0, 1, 2, 3):
            passes[axis, step].wait_recv()
        stream = DEALT[axis]
        chosen = [at for at, part in enumerate(LATE_PLAN.parts) if part[0] == stream]

        @pl.loop(0, 4, unroll=4)
        def _(row):
            halves = []
            for group in range(2):
                block = dot(rings[axis][group, row], dealt[axis][...])
                halves.append(block.reshape(16, 1, 8, DEAL_COLS))
            both = jnp.concatenate(halves, axis=1).reshape(4, 4, 16, DEAL_COLS).astype(BF16)
            start = 0
            for at in chosen:
                _, order, _, width = LATE_PLAN.parts[at]
                for at_z in range(4):
                    for at_x in range(4):
                        spot = tuple((row, at_z, at_x)[one] for one in order)
                        sums.parts[at].tiles[spot] = both[at_z, at_x][:, start : start + width]
                start += width

        sums.each(stream, lambda part: part.ring_start(0))

    def finish(stream):
        if stream == CONV:
            sums.finish(stream, out_conv)
        elif stream in (DEALT[Y], DEALT[Z]):
            axis = Y if stream == DEALT[Y] else Z
            start = [axis * FILTERS]

            def end(part):
                part.dealt_end(outs["high"], start[0])
                start[0] += part.width

            sums.each(stream, end)
        else:
            sums.finish(stream, outs)

    def highway(first, last):
        for at in range(first, last):
            cols = slice(at * HIGH_ROWS, (at + 1) * HIGH_ROWS)
            high_loads[at].wait()
            weight = high_slots.at[at % HIGH_SLOTS]
            grad = grad_pooled[:, cols]
            grad = grad + back_dot(grad_mixed[:, 0:FILTERS], weight[:, 0:FILTERS])
            grad = grad + back_dot(grad_mixed[:, FILTERS:], weight[:, FILTERS:])
            _, slope = gelu_both(pooled[:, cols])
            grad_pooled[:, cols] = slope * grad
            if at + HIGH_SLOTS < len(high_loads):
                high_loads[at + HIGH_SLOTS].start()

    lane = lax.broadcasted_iota(jnp.int32, (WORDS, 128), 1)

    def conv_start():
        last_grad[...] = jnp.zeros_like(last_grad)
        conv_grad[...] = jnp.zeros_like(conv_grad)
        table_grad[...] = jnp.zeros_like(table_grad)
        tap_row = lax.broadcasted_iota(jnp.int32, (128, 128), 0)
        for block in range(FILTERS // 128):
            weight = conv_w[:, block * 128 : (block + 1) * 128].astype(F32)
            weight = jnp.where(tap_row < BIAS_ROW, weight, 0.0)
            conv_back[block * 128 : (block + 1) * 128, :] = weight.T.astype(BF16)

    def conv_block(step):
        first = CONV_STEP * step
        some = unfolded[pl.ds(first, CONV_STEP)].reshape(CONV_STEP * WORDS, 128)
        unit = jnp.where(
            lax.broadcasted_iota(jnp.int32, (128, 128), 0)
            == lax.broadcasted_iota(jnp.int32, (128, 128), 1),
            1.0,
            0.0,
        ).astype(BF16)
        turned = back_dot(unit, some).astype(BF16)
        back = jnp.zeros((CONV_STEP * WORDS, 128), F32)
        for block in range(FILTERS // CONV_COLS):
            cols = slice(block * CONV_COLS, (block + 1) * CONV_COLS)
            conv = dot(some, conv_w[:, cols]).reshape(CONV_STEP, WORDS, CONV_COLS)
            shares = jnp.exp(conv - pooled[:, cols][None]) * grad_pooled[:, cols][None]
            shares = shares.astype(BF16).reshape(CONV_STEP * WORDS, CONV_COLS)
            conv_grad[:, cols] += dot(turned, shares)
            back = back + dot(shares, conv_back[cols, :])
        back = back.reshape(CONV_STEP, WORDS, 128)
        before = last_grad[...]
        last_grad[...] = back[CONV_STEP - TAPS + 1 :]
        high_low, onehots = [], []
        for side in range(CONV_STEP):
            taps = back[side]
            for tap in range(1, TAPS):
                from_tap = back[side - tap] if side >= tap else before[TAPS - 1 + side - tap]
                taps = jnp.where(lane // CHAR_DIM == tap, from_tap, taps)
            taps = jnp.where(lane < BIAS_ROW, taps, 0.0)
            high = taps.astype(BF16)
            low = (taps - high.astype(F32)).astype(BF16)
            high_low.append(jnp.concatenate([high, low], axis=1))
            code = lax.broadcasted_iota(jnp.int32, (CHAR_ROWS, WORDS), 0)
            ids = chars[pl.ds(first + side, 1), :]
            onehots.append(jnp.where(ids == code, 1.0, 0.0).astype(BF16))
        table_grad[0:CHAR_ROWS, :] += dot(
            jnp.concatenate(onehots, axis=1), jnp.concatenate(high_low, axis=0)
        )

    conv_pairs = []

    def conv_end():
        for block in range(16):
            turned = conv_grad[:, block * 128 : (block + 1) * 128].T
            conv_rows[block] = turned.reshape(2, 64, 128)
        copy = remote(conv_rows.at[:, 1 - core], conv_other, conv_sems, 0, partner)
        copy.start()
        conv_pairs.append(copy)
        table = table_grad[:, 0:128] + table_grad[:, 128:256]
        turned = jnp.concatenate(
            [table[128 * block : 128 * (block + 1)].T for block in range(3)], axis=1
        )
        folded = turned[0:CHAR_DIM]
        for tap in range(1, TAPS):
            folded = folded + turned[tap * CHAR_DIM : (tap + 1) * CHAR_DIM]
        shared[1].start(0, folded)
        shared[2].start(0, conv_grad[BIAS_ROW : BIAS_ROW + 8, :])

    def conv_ring():
        conv_pairs[0].wait_recv()
        tiles = [
            part.tiles for part, of in zip(sums.parts, LATE_PLAN.parts) if of[0] == CONV
        ][0]

        @pl.loop(0, 4)
        def _(at):
            for inner in range(4):
                row = at * 4 + inner
                total = conv_rows[row, core] + conv_other[row]
                tiles[at, inner] = total.astype(BF16).reshape(4, 16, 128)

        sums.each(CONV, lambda part: part.ring_start(0))

    def shared_step(level, *which):
        for one in which:
            if level < 3:
                shared[one].start(level + 1, shared[one].end(level))
            else:
                out_shared[one][...] = shared[one].end(level)

    actions = {
        "prepare": prepare,
        "gates": gates,
        "highway": highway,
        "multiply": multiply,
        "relay1": sums.relay1,
        "end1": sums.end1,
        "relay2": sums.relay2,
        "end2": sums.end2,
        "finish": finish,
        "pass_all": pass_all,
        "multiply_high": multiply_high,
        "conv_start": conv_start,
        "conv": lambda first, last: lax.fori_loop(
            first, last, lambda step, nothing: (conv_block(step), nothing)[1], 0
        ),
        "conv_end": conv_end,
        "conv_ring": conv_ring,
        "small": lambda: shared[0].start(0, small[...]),
        "shared": shared_step,
    }
    for name, *given in schedule:
        actions[name](*given)

    sums.sent()
    for one in shared:
        one.sent()
    conv_pairs[0].wait_send()
    for copy in (*deals.values(), *passes.values()):
        copy.wait_send()


LATE_SCHEDULE = (
    ("prepare", "up"),
    ("multiply", 0),
    ("prepare", "proj", "qkv", "out"),
    ("gates",),
    ("multiply", 1),
    ("small",),
    ("highway", 0, 3),
    ("pass_all",),
    ("highway", 3, 5),
    ("multiply_high", 0),
    ("multiply_high", 1),
    ("relay1", 0),
    ("highway", 5, 8),
    ("conv_start",),
    ("conv", 0, 1),
    ("relay1", 1),
    ("shared", 0, 0),
    ("conv", 1, 2),
    ("relay1", 3),
    ("relay1", 4),
    ("end1", 0),
    ("conv", 2, 3),
    ("end1", 1),
    ("conv", 3, 4),
    ("end1", 3),
    ("end1", 4),
    ("relay2", 0),
    ("conv", 4, 5),
    ("conv_end",),
    ("relay2", 1),
    ("shared", 1, 0),
    ("conv_ring",),
    ("end2", 0),
    ("relay2", 3),
    ("relay2", 4),
    ("shared", 0, 1, 2),
    ("relay1", 2),
    ("end2", 1),
    ("shared", 2, 0),
    ("shared", 1, 1, 2),
    ("end1", 2),
    ("end2", 3),
    ("end2", 4),
    ("finish", 0),
    ("relay2", 2),
    ("shared", 3, 0),
    ("shared", 2, 1, 2),
    ("finish", 1),
    ("end2", 2),
    ("shared", 3, 1, 2),
    ("finish", 3),
    ("finish", 4),
    ("finish", 2),
)


def late_sums(vmem_in, right, high_weight, proj_weight, rings):
    dma = pltpu.SemaphoreType.DMA
    scratch = LATE_PLAN.scratch()
    for shape in SHARED:
        scratch += [pltpu.VMEM((2,) + shape, F32), pltpu.VMEM((3, 4) + shape, F32)]
    scratch += [
        dma((2, len(SHARED), 10)),
        dma((5,)),
        dma((FILTERS // HIGH_ROWS,)),
        pltpu.VMEM((FILTERS, 128), BF16),
        pltpu.VMEM((128, FILTERS), F32),
        pltpu.VMEM((16, 2, 64, 128), F32),
        pltpu.VMEM((16, 64, 128), F32),
        dma((2, 1)),
        pltpu.VMEM((TAPS - 1, WORDS, 128), F32),
        pltpu.VMEM((384, 256), F32),
        pltpu.VMEM((HIGH_SLOTS, HIGH_ROWS, 2 * FILTERS), BF16),
        pltpu.VMEM((FILTERS, D), BF16),
        pltpu.VMEM((WORDS, FILTERS), F32),
        pltpu.VMEM(SHARED[0], F32),
        pltpu.VMEM((WORDS, 2 * FILTERS), BF16),
        dma((2,)),
        dma((2, 2, 4)),
        dma((2, 2, 4)),
        pltpu.VMEM((2, 4, 128, RING_WORDS), BF16),
        pltpu.VMEM((2, 4, 128, RING_WORDS), BF16),
        pltpu.VMEM((RING_WORDS, DEAL_COLS), BF16),
        pltpu.VMEM((RING_WORDS, DEAL_COLS), BF16),
    ]
    whole = pl.BlockSpec(memory_space=pltpu.VMEM)
    outside = pl.BlockSpec(memory_space=pl.ANY)
    names = ("high", "proj", "qkv", "out", "up")
    shapes = [(CHUNK_ROWS[name], RIGHT_COLS[name]) for name in names]
    shapes += [(16, 128)] + list(SHARED)
    return pl.pallas_call(
        functools.partial(late_kernel, LATE_SCHEDULE),
        out_shape=tuple(jax.ShapeDtypeStruct(shape, F32) for shape in shapes),
        in_specs=[whole] * len(vmem_in) + [outside] * 8,
        out_specs=tuple(whole for _ in shapes),
        scratch_shapes=scratch,
        compiler_params=pltpu.CompilerParams(
            collective_id=1, has_side_effects=True, vmem_limit_bytes=64 << 20
        ),
    )(*vmem_in, *right, high_weight, proj_weight, *rings)


def results_kernel(*refs):
    hidden, high, proj, qkv, out, up, down, conv, small, table, bias = refs[:11]
    (
        to_hidden,
        to_table,
        to_conv,
        to_conv_bias,
        to_high,
        to_high_bias,
        to_proj,
        to_gain,
        to_shift,
        to_qkv,
        to_out,
        to_up,
        to_down,
    ) = refs[11:]
    to_hidden[0] = hidden[...]
    to_high[0] = high[...]
    for source, target in ((proj, to_proj), (qkv, to_qkv), (out, to_out), (up, to_up), (down, to_down)):
        target[...] = source[...]
    to_gain[...] = small[0:3, :]
    to_shift[...] = small[3:6, :]
    for line in range(0, 2 * FILTERS, D):
        used = min(D, 2 * FILTERS - line)
        to_high_bias[:, line : line + used] = small[6 + line // D : 7 + line // D, 0:used]
    to_conv_bias[...] = bias[0:1, :]
    to_table[...] = table[:, 0:CHARS]
    me = lax.axis_index("dp") * 4 + lax.axis_index("ctx")
    filters = me * 16 + lax.broadcasted_iota(jnp.int32, (16, BIAS_ROW), 0)
    widths = jnp.ones((16, BIAS_ROW), jnp.int32)
    for bound in (1, 2, 4, 8, 16, 32):
        widths = widths + (filters >= FILTERS // 64 * bound).astype(jnp.int32)
    taps = lax.broadcasted_iota(jnp.int32, (16, BIAS_ROW), 1) // CHAR_DIM
    to_conv[...] = jnp.where(taps < widths, conv[:, 0:BIAS_ROW], 0.0)


def results(*arrays):
    shapes = [
        ((1, WORDS, D), BF16),
        ((CHAR_DIM, CHARS), F32),
        ((16, BIAS_ROW), F32),
        ((1, FILTERS), F32),
        ((1, 16, 2 * FILTERS), F32),
        ((1, 2 * FILTERS), F32),
        ((16, D), F32),
        ((3, D), F32),
        ((3, D), F32),
        ((6, 3 * D), F32),
        ((6, D), F32),
        ((6, FF), F32),
        ((24, D), F32),
    ]
    whole = pl.BlockSpec(memory_space=pltpu.VMEM)
    return pl.pallas_call(
        results_kernel,
        out_shape=tuple(jax.ShapeDtypeStruct(*shape) for shape in shapes),
        in_specs=[whole] * len(arrays),
        out_specs=tuple(whole for _ in shapes),
    )(*arrays)


def body(
    char_ids,
    word_lengths,
    word_home,
    seq_lengths,
    char_table,
    conv_weight,
    conv_bias,
    highway_weight,
    highway_bias,
    proj_weight,
    norm_gain,
    norm_shift,
    qkv_weight,
    out_weight,
    up_weight,
    down_weight,
    cotangent,
):
    act, pooled, unfolded, conv_w, chars, mixed, final_rows, embedded = embed_words(
        char_ids.T,
        word_lengths[None, :],
        word_home[None, :],
        char_table.T,
        conv_weight,
        conv_bias[None, :],
        highway_weight,
        highway_bias,
        proj_weight,
    )
    (
        out_hidden,
        first_norm,
        context,
        grad_joint,
        grad_attn,
        grad_embedded,
        middle,
        grad_up,
        norms,
        grad_down_weight,
        *rings,
    ) = encode(
        embedded,
        act,
        seq_lengths[None, :],
        norm_gain,
        norm_shift,
        cotangent.reshape(WORDS, D),
        (qkv_weight, out_weight, up_weight, down_weight),
    )
    high, proj, qkv, out, grad_up_weight, conv, small, table, bias = late_sums(
        (
            act,
            final_rows,
            first_norm,
            context,
            middle,
            chars,
            unfolded,
            conv_w,
            pooled,
            mixed,
            norms,
        ),
        (grad_embedded, grad_joint, grad_attn, grad_up),
        highway_weight,
        proj_weight,
        rings,
    )
    outs = list(
        results(
            out_hidden,
            high,
            proj,
            qkv,
            out,
            grad_up_weight,
            grad_down_weight,
            conv,
            small,
            table,
            bias,
        )
    )
    outs[1], outs[2] = outs[1].T, outs[2].T
    outs[3] = outs[3].reshape(-1)
    return tuple(outs)


def solution(mesh):
    placed = (
        P(("dp", "ctx"), None),
        P(("dp", "ctx")),
        P(("dp", "ctx")),
        P("dp"),
        P(),
        P(),
        P(),
        P(),
        P(),
        P(),
        P(),
        P(),
        P(),
        P(),
        P(),
        P(),
        P("dp", "ctx", None),
    )
    return jax.shard_map(
        body,
        mesh=mesh,
        in_specs=placed,
        out_specs=(
            P("dp", "ctx", None),
            P(),
            P(None, ("dp", "ctx")),
            P(),
            P(None, ("dp", "ctx"), None),
            P(),
            P(("dp", "ctx"), None),
            P(),
            P(),
            P(("dp", "ctx"), None),
            P(("dp", "ctx"), None),
            P(("dp", "ctx"), None),
            P(("dp", "ctx"), None),
        ),
        check_vma=False,
    )
```

```python
import functools
import jax
import jax.numpy as jnp
from jax import lax
from jax.experimental import pallas as pl
from jax.experimental.pallas import tpu as pltpu
from jax.sharding import PartitionSpec as P

D = 768
FF = 3072
HEADS = 12
HEAD_DIM = 64
FILTERS = 2048
CHAR_DIM = 16
CHARS = 262
WORD_CHARS = 50
TAPS = 7
SEQ_LEN = 512
WORDS = 128

EPSILON = 1e-05
NEG_LARGE = -1e30
MESH = pl.DeviceIdType.MESH
BF16 = jnp.bfloat16
F32 = jnp.float32

BIAS_ROW = TAPS * CHAR_DIM
ABSENT_ROW = BIAS_ROW + 1
CHAR_ROWS = 272


def norm_parts(values_in, gain_row, shift_row):
    mean_val = jnp.mean(values_in, -1, keepdims=True)
    centred = values_in - mean_val
    inverse = lax.rsqrt(jnp.mean(centred * centred, -1, keepdims=True) + EPSILON)
    normal = centred * inverse
    return (normal * gain_row + shift_row, normal, inverse)


def norm_back(grad_out, normal, inverse, gain_row):
    scaled = grad_out * gain_row
    grad_in = inverse * (
        scaled
        - jnp.mean(scaled, -1, keepdims=True)
        - normal * jnp.mean(scaled * normal, -1, keepdims=True)
    )
    return (grad_in, jnp.sum(grad_out * normal, 0), jnp.sum(grad_out, 0))


def dot(left, right):
    return jnp.dot(left, right, preferred_element_type=F32)


def back_dot(rows_in, weight_rows):
    return lax.dot_general(
        rows_in, weight_rows, (((1,), (1,)), ((), ())), preferred_element_type=F32
    )


def first_dot(left, right):
    return lax.dot_general(left, right, (((0,), (0,)), ((), ())), preferred_element_type=F32)


def place_of():
    index = lax.axis_index("dp")
    return index // 8, lax.rem(index // 2, 4), lax.rem(index, 2), lax.axis_index("ctx")


def device_of(y, z, core, x):
    return ((y * 4 + z) * 2 + core, x)


def around(value, step):
    return lax.rem(value + step, 4)


def remote(source, target, sems, index, device):
    return pltpu.make_async_remote_copy(
        src_ref=source,
        dst_ref=target,
        send_sem=sems[0].at[index],
        recv_sem=sems[1].at[index],
        device_id=device,
        device_id_type=MESH,
    )


def near_peers_of(where):
    y, z, core, x = where
    peers = []
    for number in range(1, 8):
        their_core, their_x = lax.rem(core + number // 4, 2), around(x, number % 4)
        peers.append((number, their_core * 4 + their_x, device_of(y, z, their_core, their_x)))
    return peers


def far_peers_of(where):
    y, z, core, x = where
    peers = []
    for number in range(1, 16):
        their_y, their_z = around(y, number // 4), around(z, number % 4)
        peers.append((number, their_y * 4 + their_z, device_of(their_y, their_z, core, x)))
    return peers


def exchange(peers, mine, sems, source, target):
    copies = []
    for number, index, device in peers:
        copy = remote(source.at[index], target.at[mine], sems, number, device)
        copy.start()
        copies.append(copy)
    target[mine] = source[mine]
    for copy in copies:
        copy.wait_recv()
    return copies


def exact_dot(left, right):
    return jnp.dot(left, right, preferred_element_type=F32, precision=lax.Precision.HIGHEST)


POOL_COLS = 512
POOL_STEP = 10
HIGH_PARTS = 4


def embed_kernel(
    ids_ref,
    lengths_ref,
    home_ref,
    table_ref,
    conv_ref,
    conv_bias_ref,
    high_in,
    high_bias_ref,
    proj_in,
    act_ref,
    pooled_ref,
    unfolded_ref,
    weight_ref,
    chars_ref,
    mixed_ref,
    final_ref,
    embedded_ref,
    values,
    ids_turned,
    ids_wide,
    table_wide,
    high,
    proj,
    sems,
    near_sems,
    far_sems,
    go_near,
    near,
    go_far,
    far,
    conv_rows,
):
    where = place_of()
    y, z, core, x = where
    rows_each = FILTERS // HIGH_PARTS
    loads = []
    for part in range(HIGH_PARTS):
        rows = pl.ds(part * rows_each, rows_each)
        loads.append(pltpu.make_async_copy(high_in.at[0, rows], high.at[rows], sems.at[part]))
    loads.append(pltpu.make_async_copy(proj_in, proj, sems.at[HIGH_PARTS]))
    for load in loads:
        load.start()

    near_peers, far_peers = near_peers_of(where), far_peers_of(where)
    barrier = pltpu.get_barrier_semaphore()
    for _, _, device in near_peers + far_peers:
        pl.semaphore_signal(barrier, inc=1, device_id=device, device_id_type=MESH)

    lane = lax.broadcasted_iota(jnp.int32, (WORDS, 128), 1)
    row = lax.broadcasted_iota(jnp.int32, (WORDS, 128), 0)
    home = home_ref[...]
    seat, spot = home // SEQ_LEN, lax.rem(home, SEQ_LEN)
    order = (lax.rem(seat, 2) * 4 + spot // WORDS) * 16 + seat // 2
    ids_turned[...] = jnp.full((128, WORDS), -1.0, F32)
    place = lax.broadcasted_iota(jnp.int32, (WORD_CHARS, WORDS), 0)
    ids_turned[0:WORD_CHARS, :] = jnp.where(place < lengths_ref[...], ids_ref[...], -1).astype(F32)
    carried = jnp.where(row == 127, lax.rem(spot, WORDS).astype(F32), ids_turned[...]).T
    carried = exact_dot(jnp.where(order == row, 1.0, 0.0), carried)
    go_near[...] = carried.reshape(8, 16, 128)
    pl.semaphore_wait(barrier, len(near_peers) + len(far_peers))
    sent = exchange(near_peers, core * 4 + x, (near_sems.at[0], near_sems.at[1]), go_near, near)
    for number in range(8):
        go_far[:, number : number + 1, :] = near[number].reshape(16, 1, 128)
    sent += exchange(far_peers, y * 4 + z, (far_sems.at[0], far_sems.at[1]), go_far, far)
    arrived = far[...].reshape(WORDS, 128)
    slots = jnp.sum(jnp.where(lane == 127, arrived, 0.0), -1, keepdims=True)
    placed = jnp.where(slots == lane.astype(F32), 1.0, 0.0).T
    placed = jnp.where(lane < WORD_CHARS, exact_dot(placed, arrived), -1.0)
    ids_wide[...] = placed.astype(jnp.int32)
    chars_ref[...] = placed.T.astype(jnp.int32)

    code = lax.broadcasted_iota(jnp.int32, (WORDS, 384), 1)
    spread_lane = lax.broadcasted_iota(jnp.int32, (CHAR_DIM, 128), 1)
    spread_row = lax.broadcasted_iota(jnp.int32, (CHAR_DIM, 128), 0)
    spread = jnp.logical_and(lax.rem(spread_lane, CHAR_DIM) == spread_row, spread_lane < BIAS_ROW)
    spread = jnp.where(spread, 1.0, 0.0).astype(BF16)
    table_wide[...] = jnp.zeros((384, 128), BF16)
    table_wide[0:CHARS, :] = first_dot(table_ref[...], spread).astype(BF16)
    values[WORD_CHARS:, :, :] = jnp.zeros((TAPS - 1, WORDS, 128), F32)

    def look_up(step, ids):
        onehots, absents = [], []
        for side in range(POOL_STEP):
            column = ids[:, side : side + 1]
            onehots.append((column == code).astype(F32).astype(BF16))
            absents.append(jnp.where(column < 0, 1.0, 0.0))
        found = dot(jnp.concatenate(onehots, axis=0), table_wide[...])
        found = found.reshape(POOL_STEP, WORDS, 128)
        for side in range(POOL_STEP):
            taps = jnp.where(lane == BIAS_ROW, 1.0, found[side])
            values[POOL_STEP * step + side] = jnp.where(lane == ABSENT_ROW, absents[side], taps)
        return pltpu.roll(ids, 128 - POOL_STEP, 1)

    lax.fori_loop(0, WORD_CHARS // POOL_STEP, look_up, ids_wide[...])

    @pl.loop(0, WORD_CHARS, unroll=5)
    def _(place):
        taps = values[place]
        for tap in range(1, TAPS):
            taps = jnp.where(lane // CHAR_DIM == tap, values[place + tap], taps)
        unfolded_ref[place] = taps.astype(BF16)

    @pl.loop(0, FILTERS // POOL_COLS)
    def _(block):
        cols = pl.ds(pl.multiple_of(block * POOL_COLS, POOL_COLS), POOL_COLS)
        filters = lax.broadcasted_iota(jnp.int32, (BIAS_ROW, POOL_COLS), 1) + block * POOL_COLS
        tap_rows = lax.broadcasted_iota(jnp.int32, (BIAS_ROW, POOL_COLS), 0) // CHAR_DIM
        widths = jnp.ones((BIAS_ROW, POOL_COLS), jnp.int32)
        for bound in (1, 2, 4, 8, 16, 32):
            widths = widths + (filters >= FILTERS // 64 * bound).astype(jnp.int32)
        masked = jnp.where(tap_rows < widths, conv_ref[:, cols].astype(F32), 0.0)
        rest_row = lax.broadcasted_iota(jnp.int32, (128 - BIAS_ROW, POOL_COLS), 0)
        rest = jnp.where(rest_row == 0, conv_bias_ref[cols].astype(F32)[None], 0.0)
        rest = jnp.where(rest_row == ABSENT_ROW - BIAS_ROW, NEG_LARGE, rest)
        weight = jnp.concatenate([masked, rest], axis=0).astype(BF16)
        weight_ref[:, cols] = weight

        def convolve(step):
            left = unfolded_ref[POOL_STEP * step : POOL_STEP * (step + 1)]
            rows = dot(left.reshape(POOL_STEP * WORDS, 128), weight)
            return rows.reshape(POOL_STEP, WORDS, POOL_COLS)

        steps = WORD_CHARS // POOL_STEP
        conv_rows[0] = convolve(0)
        top = jnp.full((WORDS, POOL_COLS), -3e38, F32)
        total = jnp.zeros((WORDS, POOL_COLS), F32)
        for step in range(steps):
            if step + 1 < steps:
                conv_rows[(step + 1) % 2] = convolve(step + 1)
            rows = conv_rows[step % 2]
            higher = jnp.maximum(top, jnp.max(rows, axis=0))
            more = jnp.sum(jnp.exp(rows - higher[None]), axis=0)
            total = total * jnp.exp(top - higher) + more
            top = higher
        pooled = top + jnp.log(total)
        pooled_ref[:, cols] = pooled
        act_ref[:, cols] = jax.nn.gelu(pooled).astype(BF16)

    for load in loads:
        load.wait()
    act = act_ref[...]
    for start in range(0, FILTERS, 512):
        near_cols, far_cols = slice(start, start + 512), slice(FILTERS + start, FILTERS + start + 512)
        mixed = dot(act, high[:, near_cols]) + high_bias_ref[:, near_cols].astype(F32)
        gates = dot(act, high[:, far_cols]) + high_bias_ref[:, far_cols].astype(F32)
        mixed_ref[:, near_cols] = mixed
        mixed_ref[:, far_cols] = gates
        carry = jax.nn.sigmoid(gates)
        final = carry * act[:, near_cols].astype(F32) + (1.0 - carry) * jax.nn.gelu(mixed)
        final_ref[:, near_cols] = final.astype(BF16)
    embedded_ref[...] = dot(final_ref[...], proj[...]).astype(BF16)
    for copy in sent:
        copy.wait_send()


def embed_words(ids, lengths, home, table, conv, conv_bias, high, high_bias, proj):
    whole = pl.BlockSpec(memory_space=pltpu.VMEM)
    outside = pl.BlockSpec(memory_space=pl.ANY)
    shapes = [
        ((WORDS, FILTERS), BF16),
        ((WORDS, FILTERS), F32),
        ((WORD_CHARS, WORDS, 128), BF16),
        ((128, FILTERS), BF16),
        ((128, WORDS), jnp.int32),
        ((WORDS, 2 * FILTERS), F32),
        ((WORDS, FILTERS), BF16),
        ((WORDS, D), BF16),
    ]
    dma = pltpu.SemaphoreType.DMA
    return pl.pallas_call(
        embed_kernel,
        out_shape=tuple(jax.ShapeDtypeStruct(*shape) for shape in shapes),
        in_specs=[whole] * 6 + [outside, whole, outside],
        out_specs=tuple(whole for _ in shapes),
        scratch_shapes=[
            pltpu.VMEM((WORD_CHARS + TAPS - 1, WORDS, 128), F32),
            pltpu.VMEM((128, WORDS), F32),
            pltpu.VMEM((WORDS, 128), jnp.int32),
            pltpu.VMEM((384, 128), BF16),
            pltpu.VMEM((FILTERS, 2 * FILTERS), BF16),
            pltpu.VMEM((FILTERS, D), BF16),
            dma((HIGH_PARTS + 1,)),
            dma((2, 8)),
            dma((2, 16)),
            pltpu.VMEM((8, 16, 128), F32),
            pltpu.VMEM((8, 16, 128), F32),
            pltpu.VMEM((16, 8, 128), F32),
            pltpu.VMEM((16, 8, 128), F32),
            pltpu.VMEM((2, POOL_STEP, WORDS, POOL_COLS), F32),
        ],
        compiler_params=pltpu.CompilerParams(
            collective_id=3, has_side_effects=True, vmem_limit_bytes=60 << 20
        ),
    )(ids, lengths, home, table, conv, conv_bias, high, high_bias, proj)


Y, Z, X = 0, 1, 2
LEFT_COLS = {"high": 2048, "proj": 2048, "qkv": 768, "out": 768, "up": 768, "down": 3072}
RIGHT_COLS = {"high": 4096, "proj": 768, "qkv": 2304, "out": 768, "up": 3072, "down": 768}
CHUNK_ROWS = {"high": 16, "proj": 16, "qkv": 6, "out": 6, "up": 6, "down": 24}

PIECES = {
    "high": (("high", 0, 0, 1, 0, 2048), ("high", 0, 2048, 1, 2048, 2048)),
    "proj": (("proj", 0, 0, 1, 0, 768),),
    "qkv": (("qkv", 0, 0, 0, 1152, 1152),),
    "out": (("out", 0, 0, 0, 384, 384),),
    "up": (("up", 0, 0, 0, 1536, 1536),),
    "down": (("down", 0, 0, 1, 0, 768), ("down", 2, 0, 2, 384, 384)),
}


def cut(pieces, widths):
    parts, rest = [], list(pieces)
    for width in widths:
        part, room = [], width
        while room:
            name, upper, upper_at, lower, lower_at, cols = rest.pop(0)
            used = min(cols, room)
            part.append((name, upper, upper_at, lower, lower_at, used))
            room -= used
            if used < cols:
                rest.insert(
                    0, (name, upper, upper_at + used, lower, lower_at + used, cols - used)
                )
        parts.append(tuple(part))
    assert not rest
    return tuple(parts)


def narrow(piece, most):
    name, upper, upper_at, lower, lower_at, cols = piece
    start = 0
    while start < cols:
        used = min(most, cols - start)
        yield (name, upper, upper_at + start, lower, lower_at + start, used, start)
        start += used


class Plan:
    def __init__(self, names, streams, plain=()):
        self.names = names
        self.stream_names, self.parts = [], []
        self.groups, self.group_at, self.right_at = 0, {}, {}
        self.right_cols = 0
        for name in names:
            self.group_at[name] = self.groups
            self.groups += -(-CHUNK_ROWS[name] // 8)
            self.right_at[name] = self.right_cols
            self.right_cols += RIGHT_COLS[name]
        for stream, (of, pieces, orders, widths) in enumerate(streams):
            self.stream_names.append(of)
            for order, part, width in zip(orders, cut(pieces, widths), widths, strict=True):
                self.parts.append((stream, order, part, width))
        for stream, order, width in plain:
            self.parts.append((stream, order, (), width))

    def scratch(self):
        dma = pltpu.SemaphoreType.DMA
        shapes = [
            pltpu.VMEM((self.groups, 4, 128, 2 * WORDS), BF16),
            pltpu.VMEM((self.groups, 4, 128, WORDS), BF16),
            pltpu.VMEM((2 * WORDS, self.right_cols), BF16),
            dma((2, len(self.names))),
            dma((2, len(self.names))),
            dma((2, len(self.parts), 15)),
        ]
        for _, _, _, width in self.parts:
            shapes += [
                pltpu.VMEM((4, 4, 4, 16, width), BF16),
                pltpu.VMEM((2, 2, 4, 16, width), BF16),
                pltpu.VMEM((2, 4, 4, 16, width), BF16),
                pltpu.VMEM((2, 2, 16, width), BF16),
                pltpu.VMEM((2, 4, 16, width), BF16),
                pltpu.VMEM((3, 16, width), BF16),
            ]
        return shapes


ORDERS = ((Y, Z, X), (Z, X, Y), (X, Y, Z))
DOWN_PLAN = Plan(("down",), ((("down",), PIECES["down"], ((Y, Z, X), (Z, Y, X)), (640, 512)),))
LATE_PLAN = Plan(
    ("proj", "qkv", "out", "up"),
    (
        (("up",), PIECES["up"], ORDERS, (512, 512, 512)),
        (
            ("proj", "qkv", "out"),
            PIECES["qkv"] + PIECES["out"] + PIECES["proj"],
            ORDERS,
            (768, 768, 768),
        ),
    ),
    plain=(
        (2, (Z, X, Y), 384),
        (2, (X, Z, Y), 128),
        (3, (Y, X, Z), 384),
        (3, (X, Y, Z), 128),
    ),
)
DEALT = {Y: 2, Z: 3}
RING_WORDS = 8 * WORDS
DEAL_COLS = 512
SHARED = ((16, D), (16, 512))


class Part:
    def __init__(self, order, refs, sems, where):
        self.tiles, self.relay1, self.last1, self.relay2, self.last2, self.last3 = refs
        self.order, self.sems, self.where = order, sems, where
        self.width = self.tiles.shape[-1]
        y, z, core, x = where
        self.here = [(y, z, x)[axis] for axis in order]
        self.copies = {}

    def peer(self, level, step):
        y, z, core, x = self.where
        spot = [y, z, x]
        spot[self.order[level]] = around(self.here[level], step)
        return device_of(spot[0], spot[1], core, spot[2])

    def start(self, index, source, target, level, step):
        copy = remote(source, target, self.sems, index, self.peer(level, step))
        copy.start()
        self.copies[index] = copy

    def slices(self, level):
        prefix = tuple(self.here[:level])
        return lambda at, half=None: self.tiles.at[
            prefix + (at,) + (() if half is None else (pl.ds(2 * half, 2),))
        ]

    def buffers(self, level):
        return (self.relay1, self.last1) if level == 0 else (self.relay2, self.last2)

    def ring_start(self, level):
        me, base, tiles = self.here[level], 6 * level, self.slices(level)
        relay, last = self.buffers(level)
        far, right, left = around(me, 2), around(me, 1), around(me, 3)
        self.start(base, tiles(far, 0), relay.at[0], level, 1)
        self.start(base + 1, tiles(far, 1), relay.at[1], level, 3)
        self.start(base + 2, tiles(right, 1), last.at[0, pl.ds(2, 2)], level, 1)
        self.start(base + 3, tiles(left, 0), last.at[1, pl.ds(0, 2)], level, 3)

    def ring_relay(self, level):
        me, base, tiles = self.here[level], 6 * level, self.slices(level)
        relay, last = self.buffers(level)
        for side in (0, 1):
            target = tiles(around(me, (1, 3)[side]), side)
            self.copies[base + side].wait_recv()
            self.add(target, (relay.at[side],), 3 - level)
            self.start(
                base + 4 + side, target, last.at[side, pl.ds(2 * side, 2)], level, (1, 3)[side]
            )

    def ring_end(self, level):
        me, base, tiles = self.here[level], 6 * level, self.slices(level)
        _, last = self.buffers(level)
        for index in range(2, 6):
            self.copies[base + index].wait_recv()
        self.add(tiles(me), (last.at[0], last.at[1]), 3 - level)

    def add(self, target, terms, dims):
        lead = target.shape[:-2]
        count = 1
        for size in lead:
            count *= size

        @pl.loop(0, count)
        def _(flat):
            at, rest = [], flat
            for size in reversed(lead):
                at.insert(0, lax.rem(rest, size))
                rest = rest // size
            at = tuple(at)
            total = target[at].astype(F32)
            for term in terms:
                total = total + term[at].astype(F32)
            target[at] = total.astype(BF16)

    def direct_start(self):
        for step in (1, 2, 3):
            source = self.tiles.at[self.here[0], self.here[1], around(self.here[2], step)]
            self.start(11 + step, source, self.last3.at[step - 1], 2, step)

    def dealt_end(self, out, start):
        for step in (0, 1, 2, 3):
            if step:
                self.copies[11 + step].wait_recv()
                block = self.last3[step - 1]
            else:
                block = self.tiles[tuple(self.here)]
            column = around(self.here[2], 4 - step) * DEAL_COLS + start
            out[:, pl.ds(pl.multiple_of(column, 128), self.width)] = block.astype(F32)

    def direct_end(self):
        total = self.tiles[tuple(self.here)].astype(F32)
        for step in (1, 2, 3):
            self.copies[11 + step].wait_recv()
            total = total + self.last3[step - 1].astype(F32)
        return total

    def sent(self):
        for copy in self.copies.values():
            copy.wait_send()


class Shared:
    def __init__(self, pair, rings, sems, where):
        self.pair, self.rings, self.sems, self.where = pair, rings, sems, where
        self.copies = []

    def start(self, level, value):
        y, z, core, x = self.where
        if level == 0:
            self.pair[core] = value
            mine = self.pair.at[core]
            peers = [device_of(y, z, 1 - core, x)]
            targets = mine
        else:
            axis = level - 1
            here = (y, z, x)[axis]
            self.rings[axis, here] = value
            mine = self.rings.at[axis, here]
            peers = []
            for step in (1, 2, 3):
                spot = [y, z, x]
                spot[axis] = around(here, step)
                peers.append(device_of(spot[0], spot[1], core, spot[2]))
            targets = mine
        base = 0 if level == 0 else 3 * level - 2
        self.now = []
        for number, peer in enumerate(peers):
            copy = remote(mine, targets, self.sems, base + number, peer)
            copy.start()
            self.now.append(copy)
        self.copies += self.now

    def end(self, level):
        for copy in self.now:
            copy.wait_recv()
        if level == 0:
            return self.pair[0] + self.pair[1]
        ring = self.rings.at[level - 1]
        return (ring[0] + ring[1]) + (ring[2] + ring[3])

    def sent(self):
        for copy in self.copies:
            copy.wait_send()


def pick(rows_per_chunk, group, core, blocks, lanes):
    rows = blocks * 32
    row = lax.broadcasted_iota(jnp.int32, (rows, lanes), 0)
    lane = lax.broadcasted_iota(jnp.int32, (rows, lanes), 1)
    inner = lax.rem(row, 8) + 8 * group
    wanted = ((row // 32 * 2 + core) * 4 + lax.rem(row // 8, 4)) * rows_per_chunk + inner
    hit = jnp.logical_and(wanted == lane, inner < rows_per_chunk)
    return jnp.where(hit, 1.0, 0.0).astype(BF16)


PICK_LANES = {16: 512, 6: 384, 24: 768}


class Sums:
    def __init__(self, plan, refs, where):
        self.plan, self.where = plan, where
        y, z, core, x = where
        self.partner = device_of(y, z, 1 - core, x)
        self.left, self.left_out, self.right, left_sems, right_sems, part_sems = refs[:6]
        self.left_sems = (left_sems.at[0], left_sems.at[1])
        self.right_sems = (right_sems.at[0], right_sems.at[1])
        self.parts = []
        for at, (_, order, _, _) in enumerate(plan.parts):
            sems = (part_sems.at[0, at], part_sems.at[1, at])
            self.parts.append(Part(order, refs[6 + 6 * at : 12 + 6 * at], sems, where))
        self.picks, self.copies = {}, {}

    def right_part(self, name, mine):
        cols = pl.ds(self.plan.right_at[name], RIGHT_COLS[name])
        return self.right.at[pl.ds(0 if mine else WORDS, WORDS), cols]

    def send_right(self, name, source):
        copy = remote(
            source,
            self.right_part(name, False),
            self.right_sems,
            self.plan.names.index(name),
            self.partner,
        )
        copy.start()
        self.copies["right", name] = copy

    def picked(self, rows_per_chunk, group, mine):
        key = (rows_per_chunk, group, mine)
        if key not in self.picks:
            lanes = PICK_LANES[rows_per_chunk]
            core = self.where[2] if mine else 1 - self.where[2]
            self.picks[key] = pick(
                rows_per_chunk, group, core, lanes // (8 * rows_per_chunk), lanes
            )
        return self.picks[key]

    def make_left(self, name, source):
        rows_per_chunk = CHUNK_ROWS[name]
        lanes = PICK_LANES[rows_per_chunk]
        ys = lanes // (32 * rows_per_chunk)
        groups = -(-rows_per_chunk // 8)
        first = self.plan.group_at[name]
        for mine in (False, True):
            for group in range(groups):
                for block in range(4 // ys):
                    columns = source[:, block * lanes : (block + 1) * lanes]
                    rows = back_dot(self.picked(rows_per_chunk, group, mine), columns)
                    rows = rows.astype(BF16).reshape(ys, 128, WORDS)
                    span = pl.ds(block * ys, ys)
                    if mine:
                        self.left[first + group, span, :, 0:WORDS] = rows
                    else:
                        self.left_out[first + group, span] = rows

    def send_left(self, name):
        span = pl.ds(self.plan.group_at[name], -(-CHUNK_ROWS[name] // 8))
        copy = remote(
            self.left_out.at[span],
            self.left.at[span, :, :, pl.ds(WORDS, WORDS)],
            self.left_sems,
            self.plan.names.index(name),
            self.partner,
        )
        copy.start()
        self.copies["left", name] = copy

    def multiply(self, stream):
        for name in self.plan.stream_names[stream]:
            self.copies["right", name].wait_recv()
            self.copies["left", name].wait_recv()
        for at, (of, order, pieces, _) in enumerate(self.plan.parts):
            if of != stream:
                continue
            tiles = self.parts[at].tiles
            offset = 0
            for piece in pieces:
                for name, upper, upper_at, lower, lower_at, cols, start in narrow(piece, 512):
                    base, first = self.plan.right_at[name], self.plan.group_at[name]
                    lanes = pl.ds(offset + start, cols)

                    @pl.loop(0, 4, unroll=4)
                    def _(row):
                        halves = []
                        for group, column in ((upper, upper_at), (lower, lower_at)):
                            factor = self.right[:, base + column : base + column + cols]
                            block = dot(self.left[first + group, row], factor)
                            halves.append(block.reshape(16, 1, 8, cols))
                        both = jnp.concatenate(halves, axis=1).reshape(4, 4, 16, cols)
                        both = both.astype(BF16)
                        for at_z in range(4):
                            for at_x in range(4):
                                spot = tuple((row, at_z, at_x)[axis] for axis in order)
                                tiles[spot + (slice(None), lanes)] = both[at_z, at_x]

                offset += piece[5]
        self.each(stream, lambda part: part.ring_start(0))

    def each(self, stream, action):
        for at, (of, _, _, _) in enumerate(self.plan.parts):
            if of == stream:
                action(self.parts[at])

    def relay1(self, stream):
        self.each(stream, lambda part: part.ring_relay(0))

    def end1(self, stream):
        self.each(stream, lambda part: (part.ring_end(0), part.ring_start(1)))

    def relay2(self, stream):
        self.each(stream, lambda part: part.ring_relay(1))

    def end2(self, stream):
        self.each(stream, lambda part: (part.ring_end(1), part.direct_start()))

    def finish(self, stream, outs):
        for at, (of, _, pieces, _) in enumerate(self.plan.parts):
            if of != stream:
                continue
            total = self.parts[at].direct_end()
            offset = 0
            for name, upper, upper_at, lower, lower_at, cols in pieces:
                block = total[:, offset : offset + cols]
                for group, column, top in ((upper, upper_at, 0), (lower, lower_at, 8)):
                    rows = min(8, CHUNK_ROWS[name] - 8 * group)
                    outs[name][8 * group : 8 * group + rows, column : column + cols] = block[
                        top : top + rows
                    ]
                offset += cols

    def sent(self):
        for part in self.parts:
            part.sent()
        for copy in self.copies.values():
            copy.wait_send()


def sums_peers(where):
    y, z, core, x = where
    peers = [device_of(y, z, 1 - core, x)]
    for step in (1, 2, 3):
        peers.append(device_of(around(y, step), z, core, x))
        peers.append(device_of(y, around(z, step), core, x))
        peers.append(device_of(y, z, core, around(x, step)))
    return peers


PAIRS = HEADS // 2
GELU_SCALE = 0.7978845608028654
GELU_CUBE = 0.044715
FF_COLS = 512


def gelu_both(value):
    square = value * value
    bend = jnp.tanh(GELU_SCALE * value * (1.0 + GELU_CUBE * square))
    half = 0.5 * (1.0 + bend)
    slope = half + 0.5 * GELU_SCALE * value * (1.0 - bend * bend) * (
        1.0 + 3.0 * GELU_CUBE * square
    )
    return value * half, slope


def encoder_kernel(*refs):
    rest = list(refs)

    def take(count):
        taken = rest[:count]
        del rest[:count]
        return taken

    rows_in, act, length_in, gains, shifts, cotangent = take(6)
    weights_in = take(4)
    out_hidden, out_first, out_context, out_joint, out_attn, out_rows = take(6)
    out_middle, out_up, out_norms, out_down = take(4)
    out_rings = dict(zip((Y, Z), take(2)))
    sums_refs = take(6 + 6 * len(DOWN_PLAN.parts))
    weights = take(4)
    (hidden_rows,) = take(1)
    high_out, high_sems, ring_sems, store_sems = take(4)
    rings = dict(zip((Y, Z), take(2)))
    load_sems, keys_sems, sums_sems = take(3)
    joint, both, probs, probs_low, slopes = take(5)
    grads, relay, last = take(3)
    keys_sems = (keys_sems.at[0], keys_sems.at[1])
    sums_sems = (sums_sems.at[0], sums_sems.at[1])

    where = place_of()
    y, z, core, x = where
    sums = Sums(DOWN_PLAN, sums_refs, where)
    loads = []
    for at in range(4):
        loads.append(pltpu.make_async_copy(weights_in[at], weights[at], load_sems.at[at]))
        loads[at].start()
    qkv_w, out_w, up_w, down_w = weights

    right = device_of(y, z, core, around(x, 1))
    left = device_of(y, z, core, around(x, 3))

    barrier = pltpu.get_barrier_semaphore()
    greeted = sums_peers(where)
    for device in greeted:
        pl.semaphore_signal(barrier, inc=1, device_id=device, device_id_type=MESH)

    lane = lax.broadcasted_iota(jnp.int32, (WORDS, WORDS), 1)
    one_hot = lambda hit: jnp.where(hit, 1.0, 0.0).astype(BF16)
    sent = []
    word_rows = rows_in[...].astype(F32)
    gain = [gains[at : at + 1, :].astype(F32) for at in range(3)]
    shift = [shifts[at : at + 1, :].astype(F32) for at in range(3)]
    first_f, first_normal, first_inv = norm_parts(word_rows, gain[0], shift[0])
    first_norm = first_f.astype(BF16)
    out_first[...] = first_norm
    loads[0].wait()
    pl.semaphore_wait(barrier, len(greeted))
    for start in (D, 2 * D, 0):
        cols = slice(start, start + D)
        joint[:, cols] = dot(first_norm, qkv_w[:, cols]).astype(BF16)
        if start:
            half = pl.ds(start - D, D)
            both[x, :, start - D : start] = joint[:, cols]
            for side, device in ((0, right), (1, left)):
                copy = remote(
                    both.at[x, :, half], both.at[x, :, half], keys_sems, start // D * 2 + side, device
                )
                copy.start()
                sent.append(copy)
    key_right, key_left, value_right, value_left = sent[-4:]

    span = lambda at: pl.ds(pl.multiple_of(at * 2 * WORDS, 128), 2 * WORDS)
    mine = lambda at: pl.ds(pl.multiple_of(at * 2 * WORDS, 128), WORDS)
    theirs = lambda at: pl.ds(pl.multiple_of(at * 2 * WORDS + WORDS, 128), WORDS)
    spots = {Y: y, Z: z}
    partner = device_of(y, z, 1 - core, x)
    for keep in (False, True):
        for group in range(2):
            chosen = sums.picked(16, group, keep)
            for block in range(4):
                rows = back_dot(chosen, act[:, block * 512 : (block + 1) * 512]).astype(BF16)
                if not keep:
                    high_out[group, block] = rows
                    continue
                for axis, spot in spots.items():
                    rings[axis][group, block, :, mine(spot)] = rows
        if not keep:
            for axis, spot in spots.items():
                copy = remote(
                    high_out,
                    rings[axis].at[:, :, :, theirs(spot)],
                    (high_sems.at[0], high_sems.at[1]),
                    axis,
                    partner,
                )
                copy.start()
                sent.append(copy)
    for copy in sent[-2:]:
        copy.wait_recv()
    gathers = {}

    def gather(axis, index, source, group, step):
        place = [y, z, x]
        place[axis] = around(spots[axis], step)
        view = rings[axis].at[:, :, :, span(source)]
        if group is not None:
            view = rings[axis].at[group, :, :, span(source)]
        copy = remote(
            view,
            view,
            (ring_sems.at[0, axis], ring_sems.at[1, axis]),
            index,
            device_of(place[0], place[1], core, place[2]),
        )
        copy.start()
        sent.append(copy)
        gathers[axis, index] = copy

    for axis, spot in spots.items():
        gather(axis, 0, spot, None, 1)
        gather(axis, 1, spot, None, 3)
    key_right.wait_recv()
    behind, ahead = around(x, 3), around(x, 1)
    pass_key = remote(
        both.at[behind, :, pl.ds(0, D)], both.at[behind, :, pl.ds(0, D)], keys_sems, 0, right
    )
    pass_key.start()
    value_left.wait_recv()
    pass_value = remote(
        both.at[ahead, :, pl.ds(D, D)], both.at[ahead, :, pl.ds(D, D)], keys_sems, 1, left
    )
    pass_value.start()
    sent += [pass_key, pass_value]
    for copy in (key_left, value_right, pass_key, pass_value):
        copy.wait_recv()

    scale = HEAD_DIM ** (-0.5)
    low_lanes = one_hot(lane < HEAD_DIM)
    high_lanes = one_hot(lane >= HEAD_DIM)
    valid = lax.broadcasted_iota(jnp.int32, (1, SEQ_LEN), 1) < length_in[...]

    def stacked(rows):
        return jnp.concatenate([rows * low_lanes, rows * high_lanes], axis=0)

    def unstacked(rows):
        return jnp.where(lane < HEAD_DIM, rows[:WORDS], rows[WORDS:])

    for pair in range(PAIRS):
        cols = slice(pair * 128, pair * 128 + 128)
        keys = both[:, :, cols].reshape(SEQ_LEN, 128)
        values = both[:, :, D + pair * 128 : D + pair * 128 + 128].reshape(SEQ_LEN, 128)
        scores = back_dot(stacked(joint[:, cols]), keys) * scale
        masked = jnp.where(valid, scores, NEG_LARGE)
        top = jnp.max(masked, -1, keepdims=True)
        expo = jnp.where(valid, jnp.exp(masked - top), 0.0)
        share = expo / jnp.sum(expo, -1, keepdims=True)
        probs[pair] = share
        share = share.astype(BF16)
        probs_low[pair] = share
        out_context[:, cols] = unstacked(dot(share, values)).astype(BF16)
    for axis, spot in spots.items():
        for index, step in ((0, 1), (1, 3)):
            gathers[axis, index].wait_recv()
            gather(axis, 2 + index, around(spot, 4 - step), index, step)
    loads[1].wait()
    attn_out = dot(out_context[...], out_w[...])
    mid_f, mid_normal, mid_inv = norm_parts(first_norm.astype(F32) + attn_out, gain[1], shift[1])
    middle = mid_f.astype(BF16)
    out_middle[...] = middle
    loads[2].wait()
    loads[3].wait()

    down_proj = jnp.zeros((WORDS, D), F32)
    for block in range(FF // FF_COLS):
        cols = slice(block * FF_COLS, (block + 1) * FF_COLS)
        act, slope = gelu_both(dot(middle, up_w[:, cols]))
        act = act.astype(BF16)
        slopes[:, cols] = slope
        hidden_rows[:, cols] = act
        down_proj = down_proj + dot(act, down_w[cols, :])
    out_f, out_normal, out_inv = norm_parts(middle.astype(F32) + down_proj, gain[2], shift[2])
    out_hidden[...] = out_f.astype(BF16)

    def note(which, gain_row, shift_row):
        out_norms[which : which + 1, :] = gain_row[None]
        out_norms[3 + which : 4 + which, :] = shift_row[None]

    grad_pre2, gain_row, shift_row = norm_back(
        cotangent[...].astype(F32), out_normal, out_inv, gain[2]
    )
    note(2, gain_row, shift_row)
    grad_down = grad_pre2.astype(BF16)
    sums.right_part("down", True)[...] = grad_down
    sums.send_right("down", sums.right_part("down", True))
    sums.make_left("down", hidden_rows)
    sums.send_left("down")
    grad_mid = grad_pre2
    for block in range(FF // FF_COLS):
        cols = slice(block * FF_COLS, (block + 1) * FF_COLS)
        grad_up = (slopes[:, cols] * back_dot(grad_down, down_w[cols, :])).astype(BF16)
        out_up[:, cols] = grad_up
        grad_mid = grad_mid + back_dot(grad_up, up_w[:, cols])
    grad_pre1, gain_row, shift_row = norm_back(grad_mid, mid_normal, mid_inv, gain[1])
    note(1, gain_row, shift_row)
    grad_attn = grad_pre1.astype(BF16)
    out_attn[...] = grad_attn
    grad_context = back_dot(grad_attn, out_w[...]).astype(BF16)
    stores = []
    for axis in spots:
        for index in (2, 3):
            gathers[axis, index].wait_recv()
        stores.append(pltpu.make_async_copy(rings[axis], out_rings[axis], store_sems.at[axis]))
        stores[-1].start()
    sums.multiply(0)

    for pair in range(PAIRS):
        cols = slice(pair * 128, pair * 128 + 128)
        value_cols = slice(D + pair * 128, D + pair * 128 + 128)
        keys = both[:, :, cols].reshape(SEQ_LEN, 128)
        values = both[:, :, value_cols].reshape(SEQ_LEN, 128)
        grad_rows = stacked(grad_context[:, cols])
        share = probs[pair]
        grad_probs = back_dot(grad_rows, values)
        delta = jnp.sum(share * grad_probs, -1, keepdims=True)
        grad_scores = (share * (grad_probs - delta)).astype(BF16)
        grad_query = unstacked(dot(grad_scores, keys)) * scale
        out_joint[:, cols] = grad_query.astype(BF16)
        grad_keys = first_dot(grad_scores, stacked(joint[:, cols])) * scale
        grads[:, :, cols] = grad_keys.astype(BF16).reshape(4, WORDS, 128)
        grad_values = first_dot(probs_low[pair], grad_rows)
        grads[:, :, value_cols] = grad_values.astype(BF16).reshape(4, WORDS, 128)

    key_half, value_half = pl.ds(0, D), pl.ds(D, D)
    opposite = around(x, 2)
    steps = [
        remote(grads.at[opposite, :, key_half], relay.at[0], sums_sems, 0, right),
        remote(grads.at[opposite, :, value_half], relay.at[1], sums_sems, 1, left),
        remote(grads.at[ahead, :, value_half], last.at[0, :, value_half], sums_sems, 2, right),
        remote(grads.at[behind, :, key_half], last.at[1, :, key_half], sums_sems, 3, left),
    ]
    for copy in steps:
        copy.start()
    sums.relay1(0)
    steps[0].wait_recv()
    grads[ahead, :, 0:D] = (grads[ahead, :, 0:D].astype(F32) + relay[0].astype(F32)).astype(BF16)
    steps.append(
        remote(grads.at[ahead, :, key_half], last.at[0, :, key_half], sums_sems, 4, right)
    )
    steps[4].start()
    steps[1].wait_recv()
    grads[behind, :, D:] = (grads[behind, :, D:].astype(F32) + relay[1].astype(F32)).astype(BF16)
    steps.append(
        remote(grads.at[behind, :, value_half], last.at[1, :, value_half], sums_sems, 5, left)
    )
    steps[5].start()
    sent += steps
    sums.end1(0)
    for copy in steps[2:]:
        copy.wait_recv()
    total = grads[x].astype(F32) + last[0].astype(F32) + last[1].astype(F32)
    out_joint[:, D:] = total.astype(BF16)

    grad_first = grad_pre1
    for start in range(0, 3 * D, D):
        cols = slice(start, start + D)
        grad_first = grad_first + back_dot(out_joint[:, cols], qkv_w[:, cols])
    grad_words, gain_row, shift_row = norm_back(grad_first, first_normal, first_inv, gain[0])
    note(0, gain_row, shift_row)

    out_rows[...] = grad_words.astype(BF16)
    sums.relay2(0)
    sums.end2(0)
    sums.finish(0, {"down": out_down})
    for copy in sent:
        copy.wait_send()
    for store in stores:
        store.wait()
    sums.sent()


def encode(rows, act, length, gains, shifts, cotangent, weights):
    whole = pl.BlockSpec(memory_space=pltpu.VMEM)
    shapes = [(WORDS, D)] * 3 + [(WORDS, 3 * D)] + [(WORDS, D)] * 3 + [(WORDS, FF)]
    out_shapes = [jax.ShapeDtypeStruct(shape, BF16) for shape in shapes]
    for shape in ((6, D), (CHUNK_ROWS["down"], D)):
        out_shapes.append(jax.ShapeDtypeStruct(shape, F32))
    ring_shape = (2, 4, 128, RING_WORDS)
    out_shapes += [jax.ShapeDtypeStruct(ring_shape, BF16)] * 2
    dma = pltpu.SemaphoreType.DMA
    return pl.pallas_call(
        encoder_kernel,
        out_shape=tuple(out_shapes),
        in_specs=[whole] * 6 + [pl.BlockSpec(memory_space=pl.ANY)] * 4,
        out_specs=(whole,) * (len(out_shapes) - 2) + (pl.BlockSpec(memory_space=pl.ANY),) * 2,
        scratch_shapes=[
            *DOWN_PLAN.scratch(),
            *(pltpu.VMEM(weight.shape, BF16) for weight in weights),
            pltpu.VMEM((WORDS, FF), BF16),
            pltpu.VMEM((2, 4, 128, WORDS), BF16),
            dma((2, 2)),
            dma((2, 2, 4)),
            dma((2,)),
            pltpu.VMEM(ring_shape, BF16),
            pltpu.VMEM(ring_shape, BF16),
            dma((4,)),
            dma((2, 6)),
            dma((2, 6)),
            pltpu.VMEM((WORDS, 3 * D), BF16),
            pltpu.VMEM((4, WORDS, 2 * D), BF16),
            pltpu.VMEM((PAIRS, 2 * WORDS, SEQ_LEN), F32),
            pltpu.VMEM((PAIRS, 2 * WORDS, SEQ_LEN), BF16),
            pltpu.VMEM((WORDS, FF), F32),
            pltpu.VMEM((4, WORDS, 2 * D), BF16),
            pltpu.VMEM((2, WORDS, D), BF16),
            pltpu.VMEM((2, WORDS, 2 * D), BF16),
        ],
        compiler_params=pltpu.CompilerParams(
            collective_id=2, has_side_effects=True, vmem_limit_bytes=62 << 20
        ),
    )(rows, act, length, gains, shifts, cotangent, *weights)


CONV_STEP = 10
CONV_COLS = 512
HIGH_ROWS = 256
HIGH_SLOTS = 3


def late_kernel(schedule, *refs):
    rest = list(refs)

    def take(count):
        taken = rest[:count]
        del rest[:count]
        return taken

    act, final_rows, first_norm, context, middle = take(5)
    chars, unfolded, conv_w, pooled, mixed, norms = take(6)
    right_in = dict(zip(("proj", "qkv", "out", "up"), take(4)))
    high_in, proj_in = take(2)
    rings_in = dict(zip((Y, Z), take(2)))
    outs = dict(zip(("high", "proj", "qkv", "out", "up"), take(5)))
    (out_conv,) = take(1)
    out_shared = take(2)
    sums_refs = take(6 + 6 * len(LATE_PLAN.parts))
    shared_refs = [take(2) for _ in SHARED]
    shared_sems, load_sems, high_sems = take(3)
    conv_back, conv_grad, conv_rows, conv_other, conv_sems = take(5)
    conv_tiles, conv_y, conv_z, conv_last, conv_x, char_sums = take(6)
    last_grad, table_grad, high_slots, proj, grad_pooled, small = take(6)
    grad_mixed, ring_sems, deal_sems, pair_sems = take(4)
    rings = dict(zip((Y, Z), take(2)))
    dealt = dict(zip((Y, Z), take(2)))
    conv_sems = (conv_sems.at[0], conv_sems.at[1])

    where = place_of()
    y, z, core, x = where
    partner = device_of(y, z, 1 - core, x)
    sums = Sums(LATE_PLAN, sums_refs, where)
    shared = [
        Shared(pair, rings, (shared_sems.at[0, at], shared_sems.at[1, at]), where)
        for at, (pair, rings) in enumerate(shared_refs)
    ]

    loads = {"proj_w": pltpu.make_async_copy(proj_in, proj, load_sems.at[4])}
    for at, name in enumerate(right_in):
        loads[name] = pltpu.make_async_copy(
            right_in[name], sums.right_part(name, True), load_sems.at[at]
        )
    for axis in (Y, Z):
        loads[axis] = pltpu.make_async_copy(rings_in[axis], rings[axis], ring_sems.at[axis])
    for load in loads.values():
        load.start()
    high_loads = [
        pltpu.make_async_copy(
            high_in.at[0, pl.ds(at * HIGH_ROWS, HIGH_ROWS)],
            high_slots.at[at % HIGH_SLOTS],
            high_sems.at[at],
        )
        for at in range(FILTERS // HIGH_ROWS)
    ]
    for at in range(HIGH_SLOTS):
        high_loads[at].start()

    barrier = pltpu.get_barrier_semaphore()
    peers = sums_peers(where)
    for device in peers:
        pl.semaphore_signal(barrier, inc=1, device_id=device, device_id_type=MESH)
    small[...] = jnp.zeros_like(small)
    small[0:6, :] = norms[...]

    def prepare():
        for name, source in zip(LATE_PLAN.names, (final_rows, first_norm, context, middle)):
            sums.make_left(name, source)

    def greet():
        pl.semaphore_wait(barrier, len(peers))
        for name in ("up", "qkv", "out", "proj"):
            sums.send_right(name, right_in[name])
            sums.send_left(name)

    def multiply(stream):
        for name in LATE_PLAN.stream_names[stream]:
            if name in loads and name != "proj":
                loads[name].wait()
        sums.multiply(stream)

    def gates():
        loads["proj_w"].wait()
        loads["proj"].wait()
        grad_rows = sums.right_part("proj", True)[...]
        for start in range(0, FILTERS, 512):
            near, far = slice(start, start + 512), slice(FILTERS + start, FILTERS + start + 512)
            grad = back_dot(grad_rows, proj[near, :])
            carry = jax.nn.sigmoid(mixed[:, far])
            value, slope = gelu_both(mixed[:, near])
            grad_near = ((1.0 - carry) * slope * grad).astype(BF16)
            grad_far = (act[:, near].astype(F32) - value) * carry * (1.0 - carry) * grad
            grad_far = grad_far.astype(BF16)
            grad_mixed[:, near] = grad_near
            grad_mixed[:, far] = grad_far
            grad_pooled[:, near] = carry * grad
            for grads, at in ((grad_near, start), (grad_far, FILTERS + start)):
                total = jnp.sum(grads.astype(F32), 0, keepdims=True)
                for block in range(0, 512, 256):
                    line, lane_at = divmod(at + block, D)
                    small[6 + line : 7 + line, lane_at : lane_at + 256] = total[
                        :, block : block + 256
                    ]
        for axis, here in spots.items():
            share = lambda at: pl.ds(pl.multiple_of(axis * FILTERS + at * DEAL_COLS, 128), DEAL_COLS)
            rows = pl.ds(pl.multiple_of(here * 2 * WORDS, 128), WORDS)
            for step in (1, 2, 3):
                place = [y, z, x]
                place[axis] = around(here, step)
                copy = remote(
                    grad_mixed.at[:, share(place[axis])],
                    dealt[axis].at[rows, :],
                    (deal_sems.at[0, axis], deal_sems.at[1, axis]),
                    step,
                    device_of(place[0], place[1], core, place[2]),
                )
                copy.start()
                deals[axis, step] = copy
            dealt[axis][rows, :] = grad_mixed[:, share(here)]
            pass_on(axis, 0)

    spots = {Y: y, Z: z}
    deals, passes = {}, {}

    def pass_on(axis, step):
        source = around(spots[axis], 4 - step) * 2 * WORDS
        copy = remote(
            dealt[axis].at[pl.ds(pl.multiple_of(source, 128), WORDS), :],
            dealt[axis].at[pl.ds(pl.multiple_of(source + WORDS, 128), WORDS), :],
            (pair_sems.at[0, axis], pair_sems.at[1, axis]),
            step,
            partner,
        )
        copy.start()
        passes[axis, step] = copy

    def pass_all():
        for step in (1, 3, 2):
            for axis in spots:
                deals[axis, step].wait_recv()
                pass_on(axis, step)

    def multiply_high(axis):
        loads[axis].wait()
        for step in (0, 1, 2, 3):
            passes[axis, step].wait_recv()
        stream = DEALT[axis]
        chosen = [at for at, part in enumerate(LATE_PLAN.parts) if part[0] == stream]

        @pl.loop(0, 4, unroll=4)
        def _(row):
            halves = []
            for group in range(2):
                block = dot(rings[axis][group, row], dealt[axis][...])
                halves.append(block.reshape(16, 1, 8, DEAL_COLS))
            both = jnp.concatenate(halves, axis=1).reshape(4, 4, 16, DEAL_COLS).astype(BF16)
            start = 0
            for at in chosen:
                _, order, _, width = LATE_PLAN.parts[at]
                for at_z in range(4):
                    for at_x in range(4):
                        spot = tuple((row, at_z, at_x)[one] for one in order)
                        sums.parts[at].tiles[spot] = both[at_z, at_x][:, start : start + width]
                start += width

        sums.each(stream, lambda part: part.ring_start(0))

    def finish(stream):
        if stream not in DEALT.values():
            sums.finish(stream, outs)
            return
        start = [(Y if stream == DEALT[Y] else Z) * FILTERS]

        def end(part):
            part.dealt_end(outs["high"], start[0])
            start[0] += part.width

        sums.each(stream, end)

    def highway(first, last):
        for at in range(first, last):
            cols = slice(at * HIGH_ROWS, (at + 1) * HIGH_ROWS)
            high_loads[at].wait()
            weight = high_slots.at[at % HIGH_SLOTS]
            grad = grad_pooled[:, cols]
            grad = grad + back_dot(grad_mixed[:, 0:FILTERS], weight[:, 0:FILTERS])
            grad = grad + back_dot(grad_mixed[:, FILTERS:], weight[:, FILTERS:])
            _, slope = gelu_both(pooled[:, cols])
            grad_pooled[:, cols] = slope * grad
            if at + HIGH_SLOTS < len(high_loads):
                high_loads[at + HIGH_SLOTS].start()

    lane = lax.broadcasted_iota(jnp.int32, (WORDS, 128), 1)

    def conv_start():
        last_grad[...] = jnp.zeros_like(last_grad)
        conv_grad[...] = jnp.zeros_like(conv_grad)
        table_grad[...] = jnp.zeros_like(table_grad)
        tap_row = lax.broadcasted_iota(jnp.int32, (128, 128), 0)
        for block in range(FILTERS // 128):
            weight = conv_w[:, block * 128 : (block + 1) * 128].astype(F32)
            weight = jnp.where(tap_row < BIAS_ROW, weight, 0.0)
            conv_back[block * 128 : (block + 1) * 128, :] = weight.T.astype(BF16)

    def conv_block(step):
        first = CONV_STEP * step
        some = unfolded[pl.ds(first, CONV_STEP)].reshape(CONV_STEP * WORDS, 128)
        unit = jnp.where(
            lax.broadcasted_iota(jnp.int32, (128, 128), 0)
            == lax.broadcasted_iota(jnp.int32, (128, 128), 1),
            1.0,
            0.0,
        ).astype(BF16)
        turned = back_dot(unit, some).astype(BF16)
        back = jnp.zeros((CONV_STEP * WORDS, 128), F32)
        for block in range(FILTERS // CONV_COLS):
            cols = slice(block * CONV_COLS, (block + 1) * CONV_COLS)
            conv = dot(some, conv_w[:, cols]).reshape(CONV_STEP, WORDS, CONV_COLS)
            shares = jnp.exp(conv - pooled[:, cols][None]) * grad_pooled[:, cols][None]
            shares = shares.astype(BF16).reshape(CONV_STEP * WORDS, CONV_COLS)
            conv_grad[:, cols] += dot(turned, shares)
            back = back + dot(shares, conv_back[cols, :])
        back = back.reshape(CONV_STEP, WORDS, 128)
        before = last_grad[...]
        last_grad[...] = back[CONV_STEP - TAPS + 1 :]
        high_low, onehots = [], []
        for side in range(CONV_STEP):
            taps = back[side]
            for tap in range(1, TAPS):
                from_tap = back[side - tap] if side >= tap else before[TAPS - 1 + side - tap]
                taps = jnp.where(lane // CHAR_DIM == tap, from_tap, taps)
            taps = jnp.where(lane < BIAS_ROW, taps, 0.0)
            high = taps.astype(BF16)
            low = (taps - high.astype(F32)).astype(BF16)
            high_low.append(jnp.concatenate([high, low], axis=1))
            code = lax.broadcasted_iota(jnp.int32, (CHAR_ROWS, WORDS), 0)
            ids = chars[pl.ds(first + side, 1), :]
            onehots.append(jnp.where(ids == code, 1.0, 0.0).astype(BF16))
        table_grad[0:CHAR_ROWS, :] += dot(
            jnp.concatenate(onehots, axis=1), jnp.concatenate(high_low, axis=0)
        )

    conv_copies = []

    def conv_send(number, source, target, device):
        copy = remote(source, target, conv_sems, number, device)
        copy.start()
        conv_copies.append(copy)

    def conv_end():
        for block in range(16):
            turned = conv_grad[:, block * 128 : (block + 1) * 128].T
            conv_rows[block] = turned.reshape(2, 64, 128)
        conv_send(0, conv_rows.at[:, 1 - core], conv_other, partner)
        table = table_grad[:, 0:128] + table_grad[:, 128:256]
        turned = jnp.concatenate(
            [table[128 * block : 128 * (block + 1)].T for block in range(3)], axis=1
        )
        folded = turned[0:CHAR_DIM]
        for tap in range(1, TAPS):
            folded = folded + turned[tap * CHAR_DIM : (tap + 1) * CHAR_DIM]
        char_sums[:, 0:384] = folded
        for block in range(16):
            bias = conv_grad[BIAS_ROW : BIAS_ROW + 1, block * 128 : (block + 1) * 128]
            char_sums[block : block + 1, 384:512] = bias
        shared[1].start(0, char_sums[...])

    def conv_sum(level):
        if level == 0:
            conv_copies[0].wait_recv()

            @pl.loop(0, 4)
            def _(at):
                for inner in range(4):
                    total = conv_rows[at * 4 + inner, core] + conv_other[at * 4 + inner]
                    conv_tiles[at, inner] = total.astype(BF16)

            for step in (1, 2, 3):
                place = around(y, step)
                device = device_of(place, z, core, x)
                conv_send(step, conv_tiles.at[place], conv_y.at[step - 1], device)
            return
        for copy in conv_copies[3 * level - 2 : 3 * level + 1]:
            copy.wait_recv()
        if level == 1:

            @pl.loop(0, 4)
            def _(at):
                total = conv_tiles[y, at].astype(F32) + conv_y[0, at].astype(F32)
                total = total + (conv_y[1, at].astype(F32) + conv_y[2, at].astype(F32))
                conv_tiles[y, at] = total.astype(BF16)

            for step in (1, 2, 3):
                place = around(z, step)
                device = device_of(y, place, core, x)
                conv_send(3 + step, conv_tiles.at[y, place], conv_z.at[step - 1], device)
        elif level == 2:
            total = conv_tiles[y, z].astype(F32) + conv_z[0].astype(F32)
            total = total + (conv_z[1].astype(F32) + conv_z[2].astype(F32))
            conv_last[...] = total.reshape(4, 16, 128)
            for step in (1, 2, 3):
                place = around(x, step)
                device = device_of(y, z, core, place)
                conv_send(6 + step, conv_last.at[place], conv_x.at[step - 1], device)
        else:
            out_conv[...] = (conv_last[x] + conv_x[0]) + (conv_x[1] + conv_x[2])

    def shared_step(level, which):
        if level < 3:
            shared[which].start(level + 1, shared[which].end(level))
        else:
            out_shared[which][...] = shared[which].end(level)

    def tail(level):
        conv_sum(level)
        shared_step(level, 1)

    actions = {
        "prepare": prepare,
        "gates": gates,
        "highway": highway,
        "multiply": multiply,
        "relay1": sums.relay1,
        "end1": sums.end1,
        "relay2": sums.relay2,
        "end2": sums.end2,
        "finish": finish,
        "pass_all": pass_all,
        "multiply_high": multiply_high,
        "conv_start": conv_start,
        "conv": lambda first, last: lax.fori_loop(
            first, last, lambda step, nothing: (conv_block(step), nothing)[1], 0
        ),
        "conv_end": conv_end,
        "greet": greet,
        "tail": tail,
        "small": lambda: shared[0].start(0, small[...]),
        "shared": shared_step,
    }
    for name, *given in schedule:
        actions[name](*given)

    sums.sent()
    for one in shared:
        one.sent()
    for copy in (*deals.values(), *passes.values(), *conv_copies):
        copy.wait_send()


LATE_SCHEDULE = (
    ("conv_start",),
    ("prepare",),
    ("greet",),
    ("gates",),
    ("highway", 0, 3),
    ("multiply", 0),
    ("multiply", 1),
    ("small",),
    ("highway", 3, 8),
    ("pass_all",),
    ("conv", 0, 1),
    ("shared", 0, 0),
    ("relay1", 0),
    ("multiply_high", 0),
    ("multiply_high", 1),
    ("conv", 1, 2),
    ("relay1", 1),
    ("shared", 1, 0),
    ("conv", 2, 3),
    ("end1", 0),
    ("relay1", 2),
    ("relay1", 3),
    ("conv", 3, 4),
    ("end1", 1),
    ("shared", 2, 0),
    ("relay2", 0),
    ("conv", 4, 5),
    ("conv_end",),
    ("end1", 2),
    ("end1", 3),
    ("relay2", 1),
    ("shared", 3, 0),
    ("tail", 0),
    ("end2", 0),
    ("relay2", 2),
    ("relay2", 3),
    ("end2", 1),
    ("tail", 1),
    ("end2", 2),
    ("end2", 3),
    ("finish", 0),
    ("tail", 2),
    ("finish", 1),
    ("finish", 2),
    ("finish", 3),
    ("tail", 3),
)


def late_sums(vmem_in, right, high_weight, proj_weight, rings):
    dma = pltpu.SemaphoreType.DMA
    scratch = LATE_PLAN.scratch()
    for shape in SHARED:
        scratch += [pltpu.VMEM((2,) + shape, F32), pltpu.VMEM((3, 4) + shape, F32)]
    scratch += [
        dma((2, len(SHARED), 10)),
        dma((5,)),
        dma((FILTERS // HIGH_ROWS,)),
        pltpu.VMEM((FILTERS, 128), BF16),
        pltpu.VMEM((128, FILTERS), F32),
        pltpu.VMEM((16, 2, 64, 128), F32),
        pltpu.VMEM((16, 64, 128), F32),
        dma((2, 10)),
        pltpu.VMEM((4, 4, 64, 128), BF16),
        pltpu.VMEM((3, 4, 64, 128), BF16),
        pltpu.VMEM((3, 64, 128), BF16),
        pltpu.VMEM((4, 16, 128), F32),
        pltpu.VMEM((3, 16, 128), F32),
        pltpu.VMEM(SHARED[1], F32),
        pltpu.VMEM((TAPS - 1, WORDS, 128), F32),
        pltpu.VMEM((384, 256), F32),
        pltpu.VMEM((HIGH_SLOTS, HIGH_ROWS, 2 * FILTERS), BF16),
        pltpu.VMEM((FILTERS, D), BF16),
        pltpu.VMEM((WORDS, FILTERS), F32),
        pltpu.VMEM(SHARED[0], F32),
        pltpu.VMEM((WORDS, 2 * FILTERS), BF16),
        dma((2,)),
        dma((2, 2, 4)),
        dma((2, 2, 4)),
        pltpu.VMEM((2, 4, 128, RING_WORDS), BF16),
        pltpu.VMEM((2, 4, 128, RING_WORDS), BF16),
        pltpu.VMEM((RING_WORDS, DEAL_COLS), BF16),
        pltpu.VMEM((RING_WORDS, DEAL_COLS), BF16),
    ]
    whole = pl.BlockSpec(memory_space=pltpu.VMEM)
    outside = pl.BlockSpec(memory_space=pl.ANY)
    names = ("high", "proj", "qkv", "out", "up")
    shapes = [(CHUNK_ROWS[name], RIGHT_COLS[name]) for name in names]
    shapes += [(16, 128)] + list(SHARED)
    return pl.pallas_call(
        functools.partial(late_kernel, LATE_SCHEDULE),
        out_shape=tuple(jax.ShapeDtypeStruct(shape, F32) for shape in shapes),
        in_specs=[whole] * len(vmem_in) + [outside] * 8,
        out_specs=tuple(whole for _ in shapes),
        scratch_shapes=scratch,
        compiler_params=pltpu.CompilerParams(
            collective_id=1, has_side_effects=True, vmem_limit_bytes=64 << 20
        ),
    )(*vmem_in, *right, high_weight, proj_weight, *rings)


def results_kernel(*refs):
    hidden, high, proj, qkv, out, up, down, conv, small, chars = refs[:10]
    (
        to_hidden,
        to_table,
        to_conv,
        to_conv_bias,
        to_high,
        to_high_bias,
        to_proj,
        to_gain,
        to_shift,
        to_qkv,
        to_out,
        to_up,
        to_down,
    ) = refs[10:]
    to_hidden[0] = hidden[...]
    to_high[0] = high[...]
    for source, target in ((proj, to_proj), (qkv, to_qkv), (out, to_out), (up, to_up), (down, to_down)):
        target[...] = source[...]
    to_gain[...] = small[0:3, :]
    to_shift[...] = small[3:6, :]
    for line in range(0, 2 * FILTERS, D):
        used = min(D, 2 * FILTERS - line)
        to_high_bias[:, line : line + used] = small[6 + line // D : 7 + line // D, 0:used]
    to_table[...] = chars[:, 0:CHARS]
    for block in range(16):
        to_conv_bias[:, block * 128 : (block + 1) * 128] = chars[block : block + 1, 384:512]
    me = lax.axis_index("dp") * 4 + lax.axis_index("ctx")
    filters = me * 16 + lax.broadcasted_iota(jnp.int32, (16, BIAS_ROW), 0)
    widths = jnp.ones((16, BIAS_ROW), jnp.int32)
    for bound in (1, 2, 4, 8, 16, 32):
        widths = widths + (filters >= FILTERS // 64 * bound).astype(jnp.int32)
    taps = lax.broadcasted_iota(jnp.int32, (16, BIAS_ROW), 1) // CHAR_DIM
    to_conv[...] = jnp.where(taps < widths, conv[:, 0:BIAS_ROW], 0.0)


def results(*arrays):
    shapes = [
        ((1, WORDS, D), BF16),
        ((CHAR_DIM, CHARS), F32),
        ((16, BIAS_ROW), F32),
        ((1, FILTERS), F32),
        ((1, 16, 2 * FILTERS), F32),
        ((1, 2 * FILTERS), F32),
        ((16, D), F32),
        ((3, D), F32),
        ((3, D), F32),
        ((6, 3 * D), F32),
        ((6, D), F32),
        ((6, FF), F32),
        ((24, D), F32),
    ]
    whole = pl.BlockSpec(memory_space=pltpu.VMEM)
    return pl.pallas_call(
        results_kernel,
        out_shape=tuple(jax.ShapeDtypeStruct(*shape) for shape in shapes),
        in_specs=[whole] * len(arrays),
        out_specs=tuple(whole for _ in shapes),
    )(*arrays)


def body(
    char_ids,
    word_lengths,
    word_home,
    seq_lengths,
    char_table,
    conv_weight,
    conv_bias,
    highway_weight,
    highway_bias,
    proj_weight,
    norm_gain,
    norm_shift,
    qkv_weight,
    out_weight,
    up_weight,
    down_weight,
    cotangent,
):
    act, pooled, unfolded, conv_w, chars, mixed, final_rows, embedded = embed_words(
        char_ids.T,
        word_lengths[None, :],
        word_home[None, :],
        char_table.T,
        conv_weight,
        conv_bias,
        highway_weight,
        highway_bias,
        proj_weight,
    )
    (
        out_hidden,
        first_norm,
        context,
        grad_joint,
        grad_attn,
        grad_embedded,
        middle,
        grad_up,
        norms,
        grad_down_weight,
        *rings,
    ) = encode(
        embedded,
        act,
        seq_lengths[None, :],
        norm_gain,
        norm_shift,
        cotangent.reshape(WORDS, D),
        (qkv_weight, out_weight, up_weight, down_weight),
    )
    high, proj, qkv, out, grad_up_weight, conv, small, char_sums = late_sums(
        (
            act,
            final_rows,
            first_norm,
            context,
            middle,
            chars,
            unfolded,
            conv_w,
            pooled,
            mixed,
            norms,
        ),
        (grad_embedded, grad_joint, grad_attn, grad_up),
        highway_weight,
        proj_weight,
        rings,
    )
    outs = list(
        results(
            out_hidden,
            high,
            proj,
            qkv,
            out,
            grad_up_weight,
            grad_down_weight,
            conv,
            small,
            char_sums,
        )
    )
    outs[1], outs[2] = outs[1].T, outs[2].T
    outs[3] = outs[3].reshape(-1)
    return tuple(outs)


def solution(mesh):
    placed = (
        P(("dp", "ctx"), None),
        P(("dp", "ctx")),
        P(("dp", "ctx")),
        P("dp"),
        P(),
        P(),
        P(),
        P(),
        P(),
        P(),
        P(),
        P(),
        P(),
        P(),
        P(),
        P(),
        P("dp", "ctx", None),
    )
    return jax.shard_map(
        body,
        mesh=mesh,
        in_specs=placed,
        out_specs=(
            P("dp", "ctx", None),
            P(),
            P(None, ("dp", "ctx")),
            P(),
            P(None, ("dp", "ctx"), None),
            P(),
            P(("dp", "ctx"), None),
            P(),
            P(),
            P(("dp", "ctx"), None),
            P(("dp", "ctx"), None),
            P(("dp", "ctx"), None),
            P(("dp", "ctx"), None),
        ),
        check_vma=False,
    )
```

```python
import functools
import jax
import jax.numpy as jnp
from jax import lax
from jax.experimental import pallas as pl
from jax.experimental.pallas import tpu as pltpu
from jax.sharding import PartitionSpec as P

D = 768
FF = 3072
HEADS = 12
HEAD_DIM = 64
FILTERS = 2048
CHAR_DIM = 16
CHARS = 262
WORD_CHARS = 50
TAPS = 7
SEQ_LEN = 512
WORDS = 128

EPSILON = 1e-05
NEG_LARGE = -1e30
MESH = pl.DeviceIdType.MESH
BF16 = jnp.bfloat16
F32 = jnp.float32

BIAS_ROW = TAPS * CHAR_DIM
ABSENT_ROW = BIAS_ROW + 1
CHAR_ROWS = 272


def norm_parts(values_in, gain_row, shift_row):
    mean_val = jnp.mean(values_in, -1, keepdims=True)
    centred = values_in - mean_val
    inverse = lax.rsqrt(jnp.mean(centred * centred, -1, keepdims=True) + EPSILON)
    normal = centred * inverse
    return (normal * gain_row + shift_row, normal, inverse)


def norm_back(grad_out, normal, inverse, gain_row):
    scaled = grad_out * gain_row
    grad_in = inverse * (
        scaled
        - jnp.mean(scaled, -1, keepdims=True)
        - normal * jnp.mean(scaled * normal, -1, keepdims=True)
    )
    return (grad_in, jnp.sum(grad_out * normal, 0), jnp.sum(grad_out, 0))


def dot(left, right):
    return jnp.dot(left, right, preferred_element_type=F32)


def back_dot(rows_in, weight_rows):
    return lax.dot_general(
        rows_in, weight_rows, (((1,), (1,)), ((), ())), preferred_element_type=F32
    )


def first_dot(left, right):
    return lax.dot_general(left, right, (((0,), (0,)), ((), ())), preferred_element_type=F32)


def place_of():
    index = lax.axis_index("dp")
    return index // 8, lax.rem(index // 2, 4), lax.rem(index, 2), lax.axis_index("ctx")


def device_of(y, z, core, x):
    return ((y * 4 + z) * 2 + core, x)


def around(value, step):
    return lax.rem(value + step, 4)


def remote(source, target, sems, index, device):
    return pltpu.make_async_remote_copy(
        src_ref=source,
        dst_ref=target,
        send_sem=sems[0].at[index],
        recv_sem=sems[1].at[index],
        device_id=device,
        device_id_type=MESH,
    )


def near_peers_of(where):
    y, z, core, x = where
    peers = []
    for number in range(1, 8):
        their_core, their_x = lax.rem(core + number // 4, 2), around(x, number % 4)
        peers.append((number, their_core * 4 + their_x, device_of(y, z, their_core, their_x)))
    return peers


def far_peers_of(where):
    y, z, core, x = where
    peers = []
    for number in range(1, 16):
        their_y, their_z = around(y, number // 4), around(z, number % 4)
        peers.append((number, their_y * 4 + their_z, device_of(their_y, their_z, core, x)))
    return peers


def exchange(peers, mine, sems, source, target):
    copies = []
    for number, index, device in peers:
        copy = remote(source.at[index], target.at[mine], sems, number, device)
        copy.start()
        copies.append(copy)
    target[mine] = source[mine]
    for copy in copies:
        copy.wait_recv()
    return copies


def exact_dot(left, right):
    return jnp.dot(left, right, preferred_element_type=F32, precision=lax.Precision.HIGHEST)


POOL_COLS = 512
POOL_STEP = 10
HIGH_PARTS = 4


def embed_kernel(
    ids_ref,
    lengths_ref,
    home_ref,
    table_ref,
    conv_ref,
    conv_bias_ref,
    high_in,
    high_bias_ref,
    proj_in,
    act_ref,
    chars_ref,
    final_ref,
    embedded_ref,
    pooled_out,
    unfolded_out,
    weight_out,
    mixed_out,
    pooled_ref,
    unfolded_ref,
    weight_ref,
    mixed_ref,
    store_sems,
    values,
    ids_turned,
    ids_wide,
    table_wide,
    high,
    proj,
    sems,
    near_sems,
    far_sems,
    go_near,
    near,
    go_far,
    far,
    conv_rows,
):
    where = place_of()
    y, z, core, x = where
    kept = (
        (unfolded_ref, unfolded_out),
        (pooled_ref, pooled_out),
        (weight_ref, weight_out),
        (mixed_ref, mixed_out),
    )
    stores = [
        pltpu.make_async_copy(source, target, store_sems.at[at])
        for at, (source, target) in enumerate(kept)
    ]
    rows_each = FILTERS // HIGH_PARTS
    loads = []
    for part in range(HIGH_PARTS):
        rows = pl.ds(part * rows_each, rows_each)
        loads.append(pltpu.make_async_copy(high_in.at[0, rows], high.at[rows], sems.at[part]))
    loads.append(pltpu.make_async_copy(proj_in, proj, sems.at[HIGH_PARTS]))
    for load in loads:
        load.start()

    near_peers, far_peers = near_peers_of(where), far_peers_of(where)
    barrier = pltpu.get_barrier_semaphore()
    for _, _, device in near_peers + far_peers:
        pl.semaphore_signal(barrier, inc=1, device_id=device, device_id_type=MESH)

    lane = lax.broadcasted_iota(jnp.int32, (WORDS, 128), 1)
    row = lax.broadcasted_iota(jnp.int32, (WORDS, 128), 0)
    home = home_ref[...]
    seat, spot = home // SEQ_LEN, lax.rem(home, SEQ_LEN)
    order = (lax.rem(seat, 2) * 4 + spot // WORDS) * 16 + seat // 2
    ids_turned[...] = jnp.full((128, WORDS), -1.0, F32)
    place = lax.broadcasted_iota(jnp.int32, (WORD_CHARS, WORDS), 0)
    ids_turned[0:WORD_CHARS, :] = jnp.where(place < lengths_ref[...], ids_ref[...], -1).astype(F32)
    carried = jnp.where(row == 127, lax.rem(spot, WORDS).astype(F32), ids_turned[...]).T
    carried = exact_dot(jnp.where(order == row, 1.0, 0.0), carried)
    go_near[...] = carried.reshape(8, 16, 128)
    pl.semaphore_wait(barrier, len(near_peers) + len(far_peers))
    sent = exchange(near_peers, core * 4 + x, (near_sems.at[0], near_sems.at[1]), go_near, near)
    for number in range(8):
        go_far[:, number : number + 1, :] = near[number].reshape(16, 1, 128)
    sent += exchange(far_peers, y * 4 + z, (far_sems.at[0], far_sems.at[1]), go_far, far)
    arrived = far[...].reshape(WORDS, 128)
    slots = jnp.sum(jnp.where(lane == 127, arrived, 0.0), -1, keepdims=True)
    placed = jnp.where(slots == lane.astype(F32), 1.0, 0.0).T
    placed = jnp.where(lane < WORD_CHARS, exact_dot(placed, arrived), -1.0)
    ids_wide[...] = placed.astype(jnp.int32)
    chars_ref[...] = placed.T.astype(jnp.int32)

    code = lax.broadcasted_iota(jnp.int32, (WORDS, 384), 1)
    spread_lane = lax.broadcasted_iota(jnp.int32, (CHAR_DIM, 128), 1)
    spread_row = lax.broadcasted_iota(jnp.int32, (CHAR_DIM, 128), 0)
    spread = jnp.logical_and(lax.rem(spread_lane, CHAR_DIM) == spread_row, spread_lane < BIAS_ROW)
    spread = jnp.where(spread, 1.0, 0.0).astype(BF16)
    table_wide[...] = jnp.zeros((384, 128), BF16)
    table_wide[0:CHARS, :] = first_dot(table_ref[...], spread).astype(BF16)
    values[WORD_CHARS:, :, :] = jnp.zeros((TAPS - 1, WORDS, 128), F32)

    def look_up(step, ids):
        onehots, absents = [], []
        for side in range(POOL_STEP):
            column = ids[:, side : side + 1]
            onehots.append((column == code).astype(F32).astype(BF16))
            absents.append(jnp.where(column < 0, 1.0, 0.0))
        found = dot(jnp.concatenate(onehots, axis=0), table_wide[...])
        found = found.reshape(POOL_STEP, WORDS, 128)
        for side in range(POOL_STEP):
            taps = jnp.where(lane == BIAS_ROW, 1.0, found[side])
            values[POOL_STEP * step + side] = jnp.where(lane == ABSENT_ROW, absents[side], taps)
        return pltpu.roll(ids, 128 - POOL_STEP, 1)

    lax.fori_loop(0, WORD_CHARS // POOL_STEP, look_up, ids_wide[...])

    @pl.loop(0, WORD_CHARS, unroll=5)
    def _(place):
        taps = values[place]
        for tap in range(1, TAPS):
            taps = jnp.where(lane // CHAR_DIM == tap, values[place + tap], taps)
        unfolded_ref[place] = taps.astype(BF16)

    stores[0].start()

    @pl.loop(0, FILTERS // POOL_COLS)
    def _(block):
        cols = pl.ds(pl.multiple_of(block * POOL_COLS, POOL_COLS), POOL_COLS)
        filters = lax.broadcasted_iota(jnp.int32, (BIAS_ROW, POOL_COLS), 1) + block * POOL_COLS
        tap_rows = lax.broadcasted_iota(jnp.int32, (BIAS_ROW, POOL_COLS), 0) // CHAR_DIM
        widths = jnp.ones((BIAS_ROW, POOL_COLS), jnp.int32)
        for bound in (1, 2, 4, 8, 16, 32):
            widths = widths + (filters >= FILTERS // 64 * bound).astype(jnp.int32)
        masked = jnp.where(tap_rows < widths, conv_ref[:, cols].astype(F32), 0.0)
        rest_row = lax.broadcasted_iota(jnp.int32, (128 - BIAS_ROW, POOL_COLS), 0)
        rest = jnp.where(rest_row == 0, conv_bias_ref[cols].astype(F32)[None], 0.0)
        rest = jnp.where(rest_row == ABSENT_ROW - BIAS_ROW, NEG_LARGE, rest)
        weight = jnp.concatenate([masked, rest], axis=0).astype(BF16)
        weight_ref[:, cols] = weight

        def convolve(step):
            left = unfolded_ref[POOL_STEP * step : POOL_STEP * (step + 1)]
            rows = dot(left.reshape(POOL_STEP * WORDS, 128), weight)
            return rows.reshape(POOL_STEP, WORDS, POOL_COLS)

        steps = WORD_CHARS // POOL_STEP
        conv_rows[0] = convolve(0)
        top = jnp.full((WORDS, POOL_COLS), -3e38, F32)
        total = jnp.zeros((WORDS, POOL_COLS), F32)
        for step in range(steps):
            if step + 1 < steps:
                conv_rows[(step + 1) % 2] = convolve(step + 1)
            rows = conv_rows[step % 2]
            higher = jnp.maximum(top, jnp.max(rows, axis=0))
            more = jnp.sum(jnp.exp(rows - higher[None]), axis=0)
            total = total * jnp.exp(top - higher) + more
            top = higher
        pooled = top + jnp.log(total)
        pooled_ref[:, cols] = pooled
        act_ref[:, cols] = jax.nn.gelu(pooled).astype(BF16)

    stores[1].start()
    stores[2].start()
    for load in loads:
        load.wait()
    act = act_ref[...]
    for start in range(0, FILTERS, 512):
        near_cols, far_cols = slice(start, start + 512), slice(FILTERS + start, FILTERS + start + 512)
        mixed = dot(act, high[:, near_cols]) + high_bias_ref[:, near_cols].astype(F32)
        gates = dot(act, high[:, far_cols]) + high_bias_ref[:, far_cols].astype(F32)
        mixed_ref[:, near_cols] = mixed
        mixed_ref[:, far_cols] = gates
        carry = jax.nn.sigmoid(gates)
        final = carry * act[:, near_cols].astype(F32) + (1.0 - carry) * jax.nn.gelu(mixed)
        final_ref[:, near_cols] = final.astype(BF16)
    stores[3].start()
    embedded_ref[...] = dot(final_ref[...], proj[...]).astype(BF16)
    for copy in sent:
        copy.wait_send()
    for store in stores:
        store.wait()


def embed_words(ids, lengths, home, table, conv, conv_bias, high, high_bias, proj):
    whole = pl.BlockSpec(memory_space=pltpu.VMEM)
    outside = pl.BlockSpec(memory_space=pl.ANY)
    shapes = [
        ((WORDS, FILTERS), BF16),
        ((128, WORDS), jnp.int32),
        ((WORDS, FILTERS), BF16),
        ((WORDS, D), BF16),
    ]
    kept = [
        ((WORDS, FILTERS), F32),
        ((WORD_CHARS, WORDS, 128), BF16),
        ((128, FILTERS), BF16),
        ((WORDS, 2 * FILTERS), F32),
    ]
    dma = pltpu.SemaphoreType.DMA
    return pl.pallas_call(
        embed_kernel,
        out_shape=tuple(jax.ShapeDtypeStruct(*shape) for shape in shapes + kept),
        in_specs=[whole] * 6 + [outside, whole, outside],
        out_specs=(whole,) * len(shapes) + (outside,) * len(kept),
        scratch_shapes=[
            *(pltpu.VMEM(*shape) for shape in kept),
            dma((len(kept),)),
            pltpu.VMEM((WORD_CHARS + TAPS - 1, WORDS, 128), F32),
            pltpu.VMEM((128, WORDS), F32),
            pltpu.VMEM((WORDS, 128), jnp.int32),
            pltpu.VMEM((384, 128), BF16),
            pltpu.VMEM((FILTERS, 2 * FILTERS), BF16),
            pltpu.VMEM((FILTERS, D), BF16),
            dma((HIGH_PARTS + 1,)),
            dma((2, 8)),
            dma((2, 16)),
            pltpu.VMEM((8, 16, 128), F32),
            pltpu.VMEM((8, 16, 128), F32),
            pltpu.VMEM((16, 8, 128), F32),
            pltpu.VMEM((16, 8, 128), F32),
            pltpu.VMEM((2, POOL_STEP, WORDS, POOL_COLS), F32),
        ],
        compiler_params=pltpu.CompilerParams(
            collective_id=3, has_side_effects=True, vmem_limit_bytes=60 << 20
        ),
    )(ids, lengths, home, table, conv, conv_bias, high, high_bias, proj)


Y, Z, X = 0, 1, 2
LEFT_COLS = {"high": 2048, "proj": 2048, "qkv": 768, "out": 768, "up": 768, "down": 3072}
RIGHT_COLS = {"high": 4096, "proj": 768, "qkv": 2304, "out": 768, "up": 3072, "down": 768}
CHUNK_ROWS = {"high": 16, "proj": 16, "qkv": 6, "out": 6, "up": 6, "down": 24}

PIECES = {
    "high": (("high", 0, 0, 1, 0, 2048), ("high", 0, 2048, 1, 2048, 2048)),
    "proj": (("proj", 0, 0, 1, 0, 768),),
    "qkv": (("qkv", 0, 0, 0, 1152, 1152),),
    "out": (("out", 0, 0, 0, 384, 384),),
    "up": (("up", 0, 0, 0, 1536, 1536),),
    "down": (("down", 0, 0, 1, 0, 768), ("down", 2, 0, 2, 384, 384)),
}


def cut(pieces, widths):
    parts, rest = [], list(pieces)
    for width in widths:
        part, room = [], width
        while room:
            name, upper, upper_at, lower, lower_at, cols = rest.pop(0)
            used = min(cols, room)
            part.append((name, upper, upper_at, lower, lower_at, used))
            room -= used
            if used < cols:
                rest.insert(
                    0, (name, upper, upper_at + used, lower, lower_at + used, cols - used)
                )
        parts.append(tuple(part))
    assert not rest
    return tuple(parts)


def narrow(piece, most):
    name, upper, upper_at, lower, lower_at, cols = piece
    start = 0
    while start < cols:
        used = min(most, cols - start)
        yield (name, upper, upper_at + start, lower, lower_at + start, used, start)
        start += used


class Plan:
    def __init__(self, names, streams, plain=()):
        self.names = names
        self.stream_names, self.parts = [], []
        self.groups, self.group_at, self.right_at = 0, {}, {}
        self.right_cols = 0
        for name in names:
            self.group_at[name] = self.groups
            self.groups += -(-CHUNK_ROWS[name] // 8)
            self.right_at[name] = self.right_cols
            self.right_cols += RIGHT_COLS[name]
        for stream, (of, pieces, orders, widths) in enumerate(streams):
            self.stream_names.append(of)
            for order, part, width in zip(orders, cut(pieces, widths), widths, strict=True):
                self.parts.append((stream, order, part, width))
        for stream, order, width in plain:
            self.parts.append((stream, order, (), width))

    def scratch(self):
        dma = pltpu.SemaphoreType.DMA
        shapes = [
            pltpu.VMEM((self.groups, 4, 128, 2 * WORDS), BF16),
            pltpu.VMEM((self.groups, 4, 128, WORDS), BF16),
            pltpu.VMEM((2 * WORDS, self.right_cols), BF16),
            dma((2, len(self.names))),
            dma((2, len(self.names))),
            dma((2, len(self.parts), 15)),
        ]
        for _, _, _, width in self.parts:
            shapes += [
                pltpu.VMEM((4, 4, 4, 16, width), BF16),
                pltpu.VMEM((2, 2, 4, 16, width), BF16),
                pltpu.VMEM((2, 4, 4, 16, width), BF16),
                pltpu.VMEM((2, 2, 16, width), BF16),
                pltpu.VMEM((2, 4, 16, width), BF16),
                pltpu.VMEM((3, 16, width), BF16),
            ]
        return shapes


ORDERS = ((Y, Z, X), (Z, X, Y), (X, Y, Z))
DOWN_PLAN = Plan(("down",), ((("down",), PIECES["down"], ((Y, Z, X), (Z, Y, X)), (640, 512)),))
LATE_PLAN = Plan(
    ("proj", "qkv", "out", "up"),
    (
        (("up",), PIECES["up"], ORDERS, (512, 512, 512)),
        (
            ("proj", "qkv", "out"),
            PIECES["qkv"] + PIECES["out"] + PIECES["proj"],
            ORDERS,
            (768, 768, 768),
        ),
    ),
    plain=(
        (2, (Z, X, Y), 384),
        (2, (X, Z, Y), 128),
        (3, (Y, X, Z), 384),
        (3, (X, Y, Z), 128),
    ),
)
DEALT = {Y: 2, Z: 3}
RING_WORDS = 8 * WORDS
DEAL_COLS = 512
SHARED = ((16, D), (16, 512))


class Part:
    def __init__(self, order, refs, sems, where):
        self.tiles, self.relay1, self.last1, self.relay2, self.last2, self.last3 = refs
        self.order, self.sems, self.where = order, sems, where
        self.width = self.tiles.shape[-1]
        y, z, core, x = where
        self.here = [(y, z, x)[axis] for axis in order]
        self.copies = {}

    def peer(self, level, step):
        y, z, core, x = self.where
        spot = [y, z, x]
        spot[self.order[level]] = around(self.here[level], step)
        return device_of(spot[0], spot[1], core, spot[2])

    def start(self, index, source, target, level, step):
        copy = remote(source, target, self.sems, index, self.peer(level, step))
        copy.start()
        self.copies[index] = copy

    def slices(self, level):
        prefix = tuple(self.here[:level])
        return lambda at, half=None: self.tiles.at[
            prefix + (at,) + (() if half is None else (pl.ds(2 * half, 2),))
        ]

    def buffers(self, level):
        return (self.relay1, self.last1) if level == 0 else (self.relay2, self.last2)

    def ring_start(self, level):
        me, base, tiles = self.here[level], 6 * level, self.slices(level)
        relay, last = self.buffers(level)
        far, right, left = around(me, 2), around(me, 1), around(me, 3)
        self.start(base, tiles(far, 0), relay.at[0], level, 1)
        self.start(base + 1, tiles(far, 1), relay.at[1], level, 3)
        self.start(base + 2, tiles(right, 1), last.at[0, pl.ds(2, 2)], level, 1)
        self.start(base + 3, tiles(left, 0), last.at[1, pl.ds(0, 2)], level, 3)

    def ring_relay(self, level):
        me, base, tiles = self.here[level], 6 * level, self.slices(level)
        relay, last = self.buffers(level)
        for side in (0, 1):
            target = tiles(around(me, (1, 3)[side]), side)
            self.copies[base + side].wait_recv()
            self.add(target, (relay.at[side],), 3 - level)
            self.start(
                base + 4 + side, target, last.at[side, pl.ds(2 * side, 2)], level, (1, 3)[side]
            )

    def ring_end(self, level):
        me, base, tiles = self.here[level], 6 * level, self.slices(level)
        _, last = self.buffers(level)
        for index in range(2, 6):
            self.copies[base + index].wait_recv()
        self.add(tiles(me), (last.at[0], last.at[1]), 3 - level)

    def add(self, target, terms, dims):
        lead = target.shape[:-2]
        count = 1
        for size in lead:
            count *= size

        @pl.loop(0, count)
        def _(flat):
            at, rest = [], flat
            for size in reversed(lead):
                at.insert(0, lax.rem(rest, size))
                rest = rest // size
            at = tuple(at)
            total = target[at].astype(F32)
            for term in terms:
                total = total + term[at].astype(F32)
            target[at] = total.astype(BF16)

    def direct_start(self):
        for step in (1, 2, 3):
            source = self.tiles.at[self.here[0], self.here[1], around(self.here[2], step)]
            self.start(11 + step, source, self.last3.at[step - 1], 2, step)

    def dealt_end(self, out, start):
        for step in (0, 1, 2, 3):
            if step:
                self.copies[11 + step].wait_recv()
                block = self.last3[step - 1]
            else:
                block = self.tiles[tuple(self.here)]
            column = around(self.here[2], 4 - step) * DEAL_COLS + start
            out[:, pl.ds(pl.multiple_of(column, 128), self.width)] = block.astype(F32)

    def direct_end(self):
        total = self.tiles[tuple(self.here)].astype(F32)
        for step in (1, 2, 3):
            self.copies[11 + step].wait_recv()
            total = total + self.last3[step - 1].astype(F32)
        return total

    def sent(self):
        for copy in self.copies.values():
            copy.wait_send()


class Shared:
    def __init__(self, pair, rings, sems, where):
        self.pair, self.rings, self.sems, self.where = pair, rings, sems, where
        self.copies = []

    def start(self, level, value):
        y, z, core, x = self.where
        if level == 0:
            self.pair[core] = value
            mine = self.pair.at[core]
            peers = [device_of(y, z, 1 - core, x)]
            targets = mine
        else:
            axis = level - 1
            here = (y, z, x)[axis]
            self.rings[axis, here] = value
            mine = self.rings.at[axis, here]
            peers = []
            for step in (1, 2, 3):
                spot = [y, z, x]
                spot[axis] = around(here, step)
                peers.append(device_of(spot[0], spot[1], core, spot[2]))
            targets = mine
        base = 0 if level == 0 else 3 * level - 2
        self.now = []
        for number, peer in enumerate(peers):
            copy = remote(mine, targets, self.sems, base + number, peer)
            copy.start()
            self.now.append(copy)
        self.copies += self.now

    def end(self, level):
        for copy in self.now:
            copy.wait_recv()
        if level == 0:
            return self.pair[0] + self.pair[1]
        ring = self.rings.at[level - 1]
        return (ring[0] + ring[1]) + (ring[2] + ring[3])

    def sent(self):
        for copy in self.copies:
            copy.wait_send()


def pick(rows_per_chunk, group, core, blocks, lanes):
    rows = blocks * 32
    row = lax.broadcasted_iota(jnp.int32, (rows, lanes), 0)
    lane = lax.broadcasted_iota(jnp.int32, (rows, lanes), 1)
    inner = lax.rem(row, 8) + 8 * group
    wanted = ((row // 32 * 2 + core) * 4 + lax.rem(row // 8, 4)) * rows_per_chunk + inner
    hit = jnp.logical_and(wanted == lane, inner < rows_per_chunk)
    return jnp.where(hit, 1.0, 0.0).astype(BF16)


PICK_LANES = {16: 512, 6: 384, 24: 768}


class Sums:
    def __init__(self, plan, refs, where):
        self.plan, self.where = plan, where
        y, z, core, x = where
        self.partner = device_of(y, z, 1 - core, x)
        self.left, self.left_out, self.right, left_sems, right_sems, part_sems = refs[:6]
        self.left_sems = (left_sems.at[0], left_sems.at[1])
        self.right_sems = (right_sems.at[0], right_sems.at[1])
        self.parts = []
        for at, (_, order, _, _) in enumerate(plan.parts):
            sems = (part_sems.at[0, at], part_sems.at[1, at])
            self.parts.append(Part(order, refs[6 + 6 * at : 12 + 6 * at], sems, where))
        self.picks, self.copies = {}, {}

    def right_part(self, name, mine):
        cols = pl.ds(self.plan.right_at[name], RIGHT_COLS[name])
        return self.right.at[pl.ds(0 if mine else WORDS, WORDS), cols]

    def send_right(self, name, source):
        copy = remote(
            source,
            self.right_part(name, False),
            self.right_sems,
            self.plan.names.index(name),
            self.partner,
        )
        copy.start()
        self.copies["right", name] = copy

    def picked(self, rows_per_chunk, group, mine):
        key = (rows_per_chunk, group, mine)
        if key not in self.picks:
            lanes = PICK_LANES[rows_per_chunk]
            core = self.where[2] if mine else 1 - self.where[2]
            self.picks[key] = pick(
                rows_per_chunk, group, core, lanes // (8 * rows_per_chunk), lanes
            )
        return self.picks[key]

    def make_left(self, name, source):
        rows_per_chunk = CHUNK_ROWS[name]
        lanes = PICK_LANES[rows_per_chunk]
        ys = lanes // (32 * rows_per_chunk)
        groups = -(-rows_per_chunk // 8)
        first = self.plan.group_at[name]
        for mine in (False, True):
            for group in range(groups):
                for block in range(4 // ys):
                    columns = source[:, block * lanes : (block + 1) * lanes]
                    rows = back_dot(self.picked(rows_per_chunk, group, mine), columns)
                    rows = rows.astype(BF16).reshape(ys, 128, WORDS)
                    span = pl.ds(block * ys, ys)
                    if mine:
                        self.left[first + group, span, :, 0:WORDS] = rows
                    else:
                        self.left_out[first + group, span] = rows

    def send_left(self, name):
        span = pl.ds(self.plan.group_at[name], -(-CHUNK_ROWS[name] // 8))
        copy = remote(
            self.left_out.at[span],
            self.left.at[span, :, :, pl.ds(WORDS, WORDS)],
            self.left_sems,
            self.plan.names.index(name),
            self.partner,
        )
        copy.start()
        self.copies["left", name] = copy

    def multiply(self, stream):
        for name in self.plan.stream_names[stream]:
            self.copies["right", name].wait_recv()
            self.copies["left", name].wait_recv()
        for at, (of, order, pieces, _) in enumerate(self.plan.parts):
            if of != stream:
                continue
            tiles = self.parts[at].tiles
            offset = 0
            for piece in pieces:
                for name, upper, upper_at, lower, lower_at, cols, start in narrow(piece, 512):
                    base, first = self.plan.right_at[name], self.plan.group_at[name]
                    lanes = pl.ds(offset + start, cols)

                    @pl.loop(0, 4, unroll=4)
                    def _(row):
                        halves = []
                        for group, column in ((upper, upper_at), (lower, lower_at)):
                            factor = self.right[:, base + column : base + column + cols]
                            block = dot(self.left[first + group, row], factor)
                            halves.append(block.reshape(16, 1, 8, cols))
                        both = jnp.concatenate(halves, axis=1).reshape(4, 4, 16, cols)
                        both = both.astype(BF16)
                        for at_z in range(4):
                            for at_x in range(4):
                                spot = tuple((row, at_z, at_x)[axis] for axis in order)
                                tiles[spot + (slice(None), lanes)] = both[at_z, at_x]

                offset += piece[5]
        self.each(stream, lambda part: part.ring_start(0))

    def each(self, stream, action):
        for at, (of, _, _, _) in enumerate(self.plan.parts):
            if of == stream:
                action(self.parts[at])

    def relay1(self, stream):
        self.each(stream, lambda part: part.ring_relay(0))

    def end1(self, stream):
        self.each(stream, lambda part: (part.ring_end(0), part.ring_start(1)))

    def relay2(self, stream):
        self.each(stream, lambda part: part.ring_relay(1))

    def end2(self, stream):
        self.each(stream, lambda part: (part.ring_end(1), part.direct_start()))

    def finish(self, stream, outs):
        for at, (of, _, pieces, _) in enumerate(self.plan.parts):
            if of != stream:
                continue
            total = self.parts[at].direct_end()
            offset = 0
            for name, upper, upper_at, lower, lower_at, cols in pieces:
                block = total[:, offset : offset + cols]
                for group, column, top in ((upper, upper_at, 0), (lower, lower_at, 8)):
                    rows = min(8, CHUNK_ROWS[name] - 8 * group)
                    outs[name][8 * group : 8 * group + rows, column : column + cols] = block[
                        top : top + rows
                    ]
                offset += cols

    def sent(self):
        for part in self.parts:
            part.sent()
        for copy in self.copies.values():
            copy.wait_send()


def sums_peers(where):
    y, z, core, x = where
    peers = [device_of(y, z, 1 - core, x)]
    for step in (1, 2, 3):
        peers.append(device_of(around(y, step), z, core, x))
        peers.append(device_of(y, around(z, step), core, x))
        peers.append(device_of(y, z, core, around(x, step)))
    return peers


PAIRS = HEADS // 2
GELU_SCALE = 0.7978845608028654
GELU_CUBE = 0.044715
FF_COLS = 512
HEAD_COLS = D // 2
CONV_STEP = 10
CONV_COLS = 512
CONV_STEPS = WORD_CHARS // CONV_STEP
SHARES_SHAPE = (CONV_STEPS, FILTERS // CONV_COLS, CONV_STEP, WORDS, CONV_COLS)
TURNED_SHAPE = (CONV_STEPS, 128, CONV_STEP * WORDS)


def gelu_both(value):
    square = value * value
    bend = jnp.tanh(GELU_SCALE * value * (1.0 + GELU_CUBE * square))
    half = 0.5 * (1.0 + bend)
    slope = half + 0.5 * GELU_SCALE * value * (1.0 - bend * bend) * (
        1.0 + 3.0 * GELU_CUBE * square
    )
    return value * half, slope


def encoder_kernel(*refs):
    rest = list(refs)

    def take(count):
        taken = rest[:count]
        del rest[:count]
        return taken

    rows_in, act, length_in, gains, shifts, cotangent = take(6)
    weights_in = take(4)
    conv_in = take(3)
    out_hidden, out_first, out_context, out_joint, out_attn, out_rows = take(6)
    out_middle, out_up, out_norms, out_down = take(4)
    out_rings = dict(zip((Y, Z), take(2)))
    out_shares, out_turned, out_back = take(3)
    sums_refs = take(6 + 6 * len(DOWN_PLAN.parts))
    weights = take(4)
    (hidden_rows,) = take(1)
    high_out, high_sems, ring_sems, store_sems = take(4)
    rings = dict(zip((Y, Z), take(2)))
    unfolded, conv_w, pooled = conv_refs = take(3)
    share_slots, turned, conv_back, conv_sems, share_sems = take(5)
    load_sems, keys_sems, sums_sems = take(3)
    joint, both, probs, probs_low, slopes = take(5)
    grads, relay, last = take(3)
    keys_sems = (keys_sems.at[0], keys_sems.at[1])
    sums_sems = (sums_sems.at[0], sums_sems.at[1])

    where = place_of()
    y, z, core, x = where
    sums = Sums(DOWN_PLAN, sums_refs, where)
    loads = []
    for at in range(4):
        loads.append(pltpu.make_async_copy(weights_in[at], weights[at], load_sems.at[at]))
        loads[at].start()
    qkv_w, out_w, up_w, down_w = weights
    conv_loads = [
        pltpu.make_async_copy(source, target, conv_sems.at[at])
        for at, (source, target) in enumerate(zip(conv_in, conv_refs))
    ]
    for load in conv_loads:
        load.start()
    share_stores = []

    def make_shares(first, last):
        if first == 0:
            for load in conv_loads:
                load.wait()
        for tile in range(first, last):
            step, block = divmod(tile, FILTERS // CONV_COLS)
            places = slice(step * CONV_STEP, (step + 1) * CONV_STEP)
            cols = slice(block * CONV_COLS, (block + 1) * CONV_COLS)
            some = unfolded[places].reshape(CONV_STEP * WORDS, 128)
            conv = dot(some, conv_w[:, cols]).reshape(CONV_STEP, WORDS, CONV_COLS)
            if tile >= 2:
                share_stores[tile - 2].wait()
            share_slots[tile % 2] = jnp.exp(conv - pooled[:, cols][None]).astype(BF16)
            copy = pltpu.make_async_copy(
                share_slots.at[tile % 2], out_shares.at[step, block], share_sems.at[tile % 2]
            )
            copy.start()
            share_stores.append(copy)
            if block == 0:
                unit = jnp.where(
                    lax.broadcasted_iota(jnp.int32, (128, 128), 0)
                    == lax.broadcasted_iota(jnp.int32, (128, 128), 1),
                    1.0,
                    0.0,
                ).astype(BF16)
                turned[step] = back_dot(unit, some).astype(BF16)
            if step == 0:
                tap_row = lax.broadcasted_iota(jnp.int32, (128, CONV_COLS), 0)
                weight = jnp.where(tap_row < BIAS_ROW, conv_w[:, cols].astype(F32), 0.0)
                conv_back[cols, :] = weight.T.astype(BF16)


    right = device_of(y, z, core, around(x, 1))
    left = device_of(y, z, core, around(x, 3))

    barrier = pltpu.get_barrier_semaphore()
    greeted = sums_peers(where)
    for device in greeted:
        pl.semaphore_signal(barrier, inc=1, device_id=device, device_id_type=MESH)

    lane = lax.broadcasted_iota(jnp.int32, (WORDS, WORDS), 1)
    one_hot = lambda hit: jnp.where(hit, 1.0, 0.0).astype(BF16)
    sent = []
    word_rows = rows_in[...].astype(F32)
    gain = [gains[at : at + 1, :].astype(F32) for at in range(3)]
    shift = [shifts[at : at + 1, :].astype(F32) for at in range(3)]
    first_f, first_normal, first_inv = norm_parts(word_rows, gain[0], shift[0])
    first_norm = first_f.astype(BF16)
    out_first[...] = first_norm
    loads[0].wait()
    pl.semaphore_wait(barrier, len(greeted))
    behind, ahead = around(x, 3), around(x, 1)
    ways = ((0, right), (1, left))
    key_copies = {}

    def head_cols(group, value):
        return pl.ds(value * D + group * HEAD_COLS, HEAD_COLS)

    def send_keys(group, value, way, owner):
        number, device = ways[way]
        view = both.at[owner, :, head_cols(group, value)]
        step = 0 if owner is x else 1
        copy = remote(view, view, keys_sems, ((group * 2 + value) * 2 + number) * 2 + step, device)
        copy.start()
        sent.append(copy)
        key_copies[group, value, way, step] = copy

    def pass_keys(group):
        for value in (0, 1):
            key_copies[group, value, value, 0].wait_recv()
            send_keys(group, value, value, (behind, ahead)[value])

    def have_keys(group):
        for value in (0, 1):
            key_copies[group, value, 1 - value, 0].wait_recv()
            key_copies[group, value, value, 1].wait_recv()

    for start in (D, 2 * D, 0):
        cols = slice(start, start + D)
        joint[:, cols] = dot(first_norm, qkv_w[:, cols]).astype(BF16)
        if start:
            value = start // D - 1
            both[x, :, start - D : start] = joint[:, cols]
            send_keys(0, value, 0, x)
            send_keys(0, value, 1, x)

    span = lambda at: pl.ds(pl.multiple_of(at * 2 * WORDS, 128), 2 * WORDS)
    mine = lambda at: pl.ds(pl.multiple_of(at * 2 * WORDS, 128), WORDS)
    theirs = lambda at: pl.ds(pl.multiple_of(at * 2 * WORDS + WORDS, 128), WORDS)
    spots = {Y: y, Z: z}
    partner = device_of(y, z, 1 - core, x)
    for keep in (False, True):
        for group in range(2):
            chosen = sums.picked(16, group, keep)
            for block in range(4):
                rows = back_dot(chosen, act[:, block * 512 : (block + 1) * 512]).astype(BF16)
                if not keep:
                    high_out[group, block] = rows
                    continue
                for axis, spot in spots.items():
                    rings[axis][group, block, :, mine(spot)] = rows
        if not keep:
            for axis, spot in spots.items():
                copy = remote(
                    high_out,
                    rings[axis].at[:, :, :, theirs(spot)],
                    (high_sems.at[0], high_sems.at[1]),
                    axis,
                    partner,
                )
                copy.start()
                sent.append(copy)
    for copy in sent[-2:]:
        copy.wait_recv()
    gathers = {}

    def gather(axis, index, source, group, step):
        place = [y, z, x]
        place[axis] = around(spots[axis], step)
        view = rings[axis].at[:, :, :, span(source)]
        if group is not None:
            view = rings[axis].at[group, :, :, span(source)]
        copy = remote(
            view,
            view,
            (ring_sems.at[0, axis], ring_sems.at[1, axis]),
            index,
            device_of(place[0], place[1], core, place[2]),
        )
        copy.start()
        sent.append(copy)
        gathers[axis, index] = copy

    pass_keys(0)
    for value in (0, 1):
        send_keys(1, value, 0, x)
        send_keys(1, value, 1, x)
    for axis, spot in spots.items():
        gather(axis, 0, spot, None, 1)
        gather(axis, 1, spot, None, 3)
    scale = HEAD_DIM ** (-0.5)
    low_lanes = one_hot(lane < HEAD_DIM)
    high_lanes = one_hot(lane >= HEAD_DIM)
    valid = lax.broadcasted_iota(jnp.int32, (1, SEQ_LEN), 1) < length_in[...]

    def stacked(rows):
        return jnp.concatenate([rows * low_lanes, rows * high_lanes], axis=0)

    def unstacked(rows):
        return jnp.where(lane < HEAD_DIM, rows[:WORDS], rows[WORDS:])

    for pair in range(PAIRS):
        if pair == 0:
            make_shares(0, 6)
            have_keys(0)
        elif pair == PAIRS // 2:
            pass_keys(1)
            make_shares(6, 11)
            have_keys(1)
        cols = slice(pair * 128, pair * 128 + 128)
        keys = both[:, :, cols].reshape(SEQ_LEN, 128)
        values = both[:, :, D + pair * 128 : D + pair * 128 + 128].reshape(SEQ_LEN, 128)
        scores = back_dot(stacked(joint[:, cols]), keys) * scale
        masked = jnp.where(valid, scores, NEG_LARGE)
        top = jnp.max(masked, -1, keepdims=True)
        expo = jnp.where(valid, jnp.exp(masked - top), 0.0)
        share = expo / jnp.sum(expo, -1, keepdims=True)
        probs[pair] = share
        share = share.astype(BF16)
        probs_low[pair] = share
        out_context[:, cols] = unstacked(dot(share, values)).astype(BF16)
    for axis, spot in spots.items():
        for index, step in ((0, 1), (1, 3)):
            gathers[axis, index].wait_recv()
            gather(axis, 2 + index, around(spot, 4 - step), index, step)
    loads[1].wait()
    attn_out = dot(out_context[...], out_w[...])
    mid_f, mid_normal, mid_inv = norm_parts(first_norm.astype(F32) + attn_out, gain[1], shift[1])
    middle = mid_f.astype(BF16)
    out_middle[...] = middle
    loads[2].wait()
    loads[3].wait()

    down_proj = jnp.zeros((WORDS, D), F32)
    for block in range(FF // FF_COLS):
        cols = slice(block * FF_COLS, (block + 1) * FF_COLS)
        act, slope = gelu_both(dot(middle, up_w[:, cols]))
        act = act.astype(BF16)
        slopes[:, cols] = slope
        hidden_rows[:, cols] = act
        down_proj = down_proj + dot(act, down_w[cols, :])
    out_f, out_normal, out_inv = norm_parts(middle.astype(F32) + down_proj, gain[2], shift[2])
    out_hidden[...] = out_f.astype(BF16)

    def note(which, gain_row, shift_row):
        out_norms[which : which + 1, :] = gain_row[None]
        out_norms[3 + which : 4 + which, :] = shift_row[None]

    grad_pre2, gain_row, shift_row = norm_back(
        cotangent[...].astype(F32), out_normal, out_inv, gain[2]
    )
    note(2, gain_row, shift_row)
    grad_down = grad_pre2.astype(BF16)
    sums.right_part("down", True)[...] = grad_down
    sums.send_right("down", sums.right_part("down", True))
    sums.make_left("down", hidden_rows)
    sums.send_left("down")
    grad_mid = grad_pre2
    for block in range(FF // FF_COLS):
        cols = slice(block * FF_COLS, (block + 1) * FF_COLS)
        grad_up = (slopes[:, cols] * back_dot(grad_down, down_w[cols, :])).astype(BF16)
        out_up[:, cols] = grad_up
        grad_mid = grad_mid + back_dot(grad_up, up_w[:, cols])
    grad_pre1, gain_row, shift_row = norm_back(grad_mid, mid_normal, mid_inv, gain[1])
    note(1, gain_row, shift_row)
    grad_attn = grad_pre1.astype(BF16)
    out_attn[...] = grad_attn
    grad_context = back_dot(grad_attn, out_w[...]).astype(BF16)
    stores = []
    for axis in spots:
        for index in (2, 3):
            gathers[axis, index].wait_recv()
        stores.append(pltpu.make_async_copy(rings[axis], out_rings[axis], store_sems.at[axis]))
        stores[-1].start()
    sums.multiply(0)

    opposite = around(x, 2)
    steps = {}

    def send_sum(group, number, source, target, value, way):
        cols = head_cols(group, value)
        source, target = source.at[:, cols], target.at[:, cols]
        copy = remote(source, target, sums_sems, group * 6 + number, ways[way][1])
        copy.start()
        sent.append(copy)
        steps[group, number] = copy

    def send_sums(group):
        send_sum(group, 0, grads.at[opposite], relay.at[0], 0, 0)
        send_sum(group, 1, grads.at[opposite], relay.at[1], 1, 1)
        send_sum(group, 2, grads.at[ahead], last.at[0], 1, 0)
        send_sum(group, 3, grads.at[behind], last.at[1], 0, 1)

    def pass_sums(group):
        for way, chip in ((0, ahead), (1, behind)):
            steps[group, way].wait_recv()
            cols = slice(way * D + group * HEAD_COLS, way * D + (group + 1) * HEAD_COLS)
            total = grads[chip, :, cols].astype(F32) + relay[way, :, cols].astype(F32)
            grads[chip, :, cols] = total.astype(BF16)
            send_sum(group, 4 + way, grads.at[chip], last.at[way], way, way)

    for pair in range(PAIRS):
        if pair == PAIRS // 2:
            send_sums(0)
        cols = slice(pair * 128, pair * 128 + 128)
        value_cols = slice(D + pair * 128, D + pair * 128 + 128)
        keys = both[:, :, cols].reshape(SEQ_LEN, 128)
        values = both[:, :, value_cols].reshape(SEQ_LEN, 128)
        grad_rows = stacked(grad_context[:, cols])
        share = probs[pair]
        grad_probs = back_dot(grad_rows, values)
        delta = jnp.sum(share * grad_probs, -1, keepdims=True)
        grad_scores = (share * (grad_probs - delta)).astype(BF16)
        grad_query = unstacked(dot(grad_scores, keys)) * scale
        out_joint[:, cols] = grad_query.astype(BF16)
        grad_keys = first_dot(grad_scores, stacked(joint[:, cols])) * scale
        grads[:, :, cols] = grad_keys.astype(BF16).reshape(4, WORDS, 128)
        grad_values = first_dot(probs_low[pair], grad_rows)
        grads[:, :, value_cols] = grad_values.astype(BF16).reshape(4, WORDS, 128)

    send_sums(1)
    make_shares(11, 13)
    pass_sums(0)
    sums.relay1(0)
    make_shares(13, 16)
    pass_sums(1)
    make_shares(16, 20)
    for at, (source, target) in enumerate(((turned, out_turned), (conv_back, out_back))):
        stores.append(pltpu.make_async_copy(source, target, conv_sems.at[at]))
        stores[-1].start()
    sums.end1(0)
    for group in (0, 1):
        for number in (2, 3, 4, 5):
            steps[group, number].wait_recv()
    total = grads[x].astype(F32) + last[0].astype(F32) + last[1].astype(F32)
    out_joint[:, D:] = total.astype(BF16)

    grad_first = grad_pre1
    for start in range(0, 3 * D, D):
        cols = slice(start, start + D)
        grad_first = grad_first + back_dot(out_joint[:, cols], qkv_w[:, cols])
    grad_words, gain_row, shift_row = norm_back(grad_first, first_normal, first_inv, gain[0])
    note(0, gain_row, shift_row)

    out_rows[...] = grad_words.astype(BF16)
    sums.relay2(0)
    sums.end2(0)
    sums.finish(0, {"down": out_down})
    for copy in sent:
        copy.wait_send()
    for store in stores + share_stores[-2:]:
        store.wait()
    sums.sent()


def encode(rows, act, length, gains, shifts, cotangent, weights, conv):
    whole = pl.BlockSpec(memory_space=pltpu.VMEM)
    shapes = [(WORDS, D)] * 3 + [(WORDS, 3 * D)] + [(WORDS, D)] * 3 + [(WORDS, FF)]
    out_shapes = [jax.ShapeDtypeStruct(shape, BF16) for shape in shapes]
    for shape in ((6, D), (CHUNK_ROWS["down"], D)):
        out_shapes.append(jax.ShapeDtypeStruct(shape, F32))
    ring_shape = (2, 4, 128, RING_WORDS)
    out_shapes += [jax.ShapeDtypeStruct(ring_shape, BF16)] * 2
    for shape in (SHARES_SHAPE, TURNED_SHAPE, (FILTERS, 128)):
        out_shapes.append(jax.ShapeDtypeStruct(shape, BF16))
    dma = pltpu.SemaphoreType.DMA
    return pl.pallas_call(
        encoder_kernel,
        out_shape=tuple(out_shapes),
        in_specs=[whole] * 6 + [pl.BlockSpec(memory_space=pl.ANY)] * 7,
        out_specs=(whole,) * (len(out_shapes) - 5) + (pl.BlockSpec(memory_space=pl.ANY),) * 5,
        scratch_shapes=[
            *DOWN_PLAN.scratch(),
            *(pltpu.VMEM(weight.shape, BF16) for weight in weights),
            pltpu.VMEM((WORDS, FF), BF16),
            pltpu.VMEM((2, 4, 128, WORDS), BF16),
            dma((2, 2)),
            dma((2, 2, 4)),
            dma((2,)),
            pltpu.VMEM(ring_shape, BF16),
            pltpu.VMEM(ring_shape, BF16),
            pltpu.VMEM((WORD_CHARS, WORDS, 128), BF16),
            pltpu.VMEM((128, FILTERS), BF16),
            pltpu.VMEM((WORDS, FILTERS), F32),
            pltpu.VMEM((2, CONV_STEP, WORDS, CONV_COLS), BF16),
            pltpu.VMEM(TURNED_SHAPE, BF16),
            pltpu.VMEM((FILTERS, 128), BF16),
            dma((3,)),
            dma((2,)),
            dma((4,)),
            dma((2, 16)),
            dma((2, 12)),
            pltpu.VMEM((WORDS, 3 * D), BF16),
            pltpu.VMEM((4, WORDS, 2 * D), BF16),
            pltpu.VMEM((PAIRS, 2 * WORDS, SEQ_LEN), F32),
            pltpu.VMEM((PAIRS, 2 * WORDS, SEQ_LEN), BF16),
            pltpu.VMEM((WORDS, FF), F32),
            pltpu.VMEM((4, WORDS, 2 * D), BF16),
            pltpu.VMEM((2, WORDS, 2 * D), BF16),
            pltpu.VMEM((2, WORDS, 2 * D), BF16),
        ],
        compiler_params=pltpu.CompilerParams(
            collective_id=2, has_side_effects=True, vmem_limit_bytes=62 << 20
        ),
    )(rows, act, length, gains, shifts, cotangent, *weights, *conv)


HIGH_ROWS = 256
HIGH_SLOTS = 3


def late_kernel(schedule, *refs):
    rest = list(refs)

    def take(count):
        taken = rest[:count]
        del rest[:count]
        return taken

    act, final_rows, first_norm, context, middle = take(5)
    chars, norms = take(2)
    late_in = dict(zip(("mixed", "pooled", "turned", "conv_back"), take(4)))
    right_in = dict(zip(("proj", "qkv", "out", "up"), take(4)))
    high_in, proj_in, shares_in = take(3)
    rings_in = dict(zip((Y, Z), take(2)))
    outs = dict(zip(("high", "proj", "qkv", "out", "up"), take(5)))
    (out_conv,) = take(1)
    out_shared = take(2)
    sums_refs = take(6 + 6 * len(LATE_PLAN.parts))
    shared_refs = [take(2) for _ in SHARED]
    shared_sems, load_sems, high_sems = take(3)
    conv_grad, conv_rows, conv_other, conv_sems = take(4)
    conv_tiles, conv_y, conv_z, conv_last, conv_x, char_sums = take(6)
    last_grad, table_grad, high_slots, proj, grad_pooled, small = take(6)
    grad_mixed, ring_sems, deal_sems, pair_sems = take(4)
    late = dict(zip(late_in, take(4)))
    (late_sems,) = take(1)
    mixed, pooled, turned, conv_back = late.values()
    share_slots, share_sems = take(2)
    rings = dict(zip((Y, Z), take(2)))
    dealt = dict(zip((Y, Z), take(2)))
    conv_sems = (conv_sems.at[0], conv_sems.at[1])

    where = place_of()
    y, z, core, x = where
    partner = device_of(y, z, 1 - core, x)
    sums = Sums(LATE_PLAN, sums_refs, where)
    shared = [
        Shared(pair, rings, (shared_sems.at[0, at], shared_sems.at[1, at]), where)
        for at, (pair, rings) in enumerate(shared_refs)
    ]

    late_loads = {
        name: pltpu.make_async_copy(late_in[name], late[name], late_sems.at[at])
        for at, name in enumerate(late)
    }
    late_loads["mixed"].start()
    loads = {"proj_w": pltpu.make_async_copy(proj_in, proj, load_sems.at[4])}
    for at, name in enumerate(right_in):
        loads[name] = pltpu.make_async_copy(
            right_in[name], sums.right_part(name, True), load_sems.at[at]
        )
    for axis in (Y, Z):
        loads[axis] = pltpu.make_async_copy(rings_in[axis], rings[axis], ring_sems.at[axis])
    for load in loads.values():
        load.start()
    high_loads = [
        pltpu.make_async_copy(
            high_in.at[0, pl.ds(at * HIGH_ROWS, HIGH_ROWS)],
            high_slots.at[at % HIGH_SLOTS],
            high_sems.at[at],
        )
        for at in range(FILTERS // HIGH_ROWS)
    ]
    for at in range(HIGH_SLOTS):
        high_loads[at].start()

    for name in ("pooled", "turned", "conv_back"):
        late_loads[name].start()

    def share_load(step, block):
        return pltpu.make_async_copy(
            shares_in.at[step, block], share_slots.at[block], share_sems.at[block]
        )

    for block in range(FILTERS // CONV_COLS):
        share_load(0, block).start()

    barrier = pltpu.get_barrier_semaphore()
    peers = sums_peers(where)
    for device in peers:
        pl.semaphore_signal(barrier, inc=1, device_id=device, device_id_type=MESH)
    small[...] = jnp.zeros_like(small)
    small[0:6, :] = norms[...]

    def prepare():
        for name, source in zip(LATE_PLAN.names, (final_rows, first_norm, context, middle)):
            sums.make_left(name, source)

    def greet():
        pl.semaphore_wait(barrier, len(peers))
        for name in ("up", "qkv", "out", "proj"):
            sums.send_right(name, right_in[name])
            sums.send_left(name)

    def multiply(stream):
        for name in LATE_PLAN.stream_names[stream]:
            if name in loads and name != "proj":
                loads[name].wait()
        sums.multiply(stream)

    def gates():
        loads["proj_w"].wait()
        loads["proj"].wait()
        late_loads["mixed"].wait()
        grad_rows = sums.right_part("proj", True)[...]
        for start in range(0, FILTERS, 512):
            near, far = slice(start, start + 512), slice(FILTERS + start, FILTERS + start + 512)
            grad = back_dot(grad_rows, proj[near, :])
            carry = jax.nn.sigmoid(mixed[:, far])
            value, slope = gelu_both(mixed[:, near])
            grad_near = ((1.0 - carry) * slope * grad).astype(BF16)
            grad_far = (act[:, near].astype(F32) - value) * carry * (1.0 - carry) * grad
            grad_far = grad_far.astype(BF16)
            grad_mixed[:, near] = grad_near
            grad_mixed[:, far] = grad_far
            grad_pooled[:, near] = carry * grad
            for grads, at in ((grad_near, start), (grad_far, FILTERS + start)):
                total = jnp.sum(grads.astype(F32), 0, keepdims=True)
                for block in range(0, 512, 256):
                    line, lane_at = divmod(at + block, D)
                    small[6 + line : 7 + line, lane_at : lane_at + 256] = total[
                        :, block : block + 256
                    ]
        for axis, here in spots.items():
            share = lambda at: pl.ds(pl.multiple_of(axis * FILTERS + at * DEAL_COLS, 128), DEAL_COLS)
            rows = pl.ds(pl.multiple_of(here * 2 * WORDS, 128), WORDS)
            for step in (1, 2, 3):
                place = [y, z, x]
                place[axis] = around(here, step)
                copy = remote(
                    grad_mixed.at[:, share(place[axis])],
                    dealt[axis].at[rows, :],
                    (deal_sems.at[0, axis], deal_sems.at[1, axis]),
                    step,
                    device_of(place[0], place[1], core, place[2]),
                )
                copy.start()
                deals[axis, step] = copy
            dealt[axis][rows, :] = grad_mixed[:, share(here)]
            pass_on(axis, 0)

    spots = {Y: y, Z: z}
    deals, passes = {}, {}

    def pass_on(axis, step):
        source = around(spots[axis], 4 - step) * 2 * WORDS
        copy = remote(
            dealt[axis].at[pl.ds(pl.multiple_of(source, 128), WORDS), :],
            dealt[axis].at[pl.ds(pl.multiple_of(source + WORDS, 128), WORDS), :],
            (pair_sems.at[0, axis], pair_sems.at[1, axis]),
            step,
            partner,
        )
        copy.start()
        passes[axis, step] = copy

    def pass_all():
        for step in (1, 3, 2):
            for axis in spots:
                deals[axis, step].wait_recv()
                pass_on(axis, step)

    def multiply_high(axis):
        loads[axis].wait()
        for step in (0, 1, 2, 3):
            passes[axis, step].wait_recv()
        stream = DEALT[axis]
        chosen = [at for at, part in enumerate(LATE_PLAN.parts) if part[0] == stream]

        @pl.loop(0, 4, unroll=4)
        def _(row):
            halves = []
            for group in range(2):
                block = dot(rings[axis][group, row], dealt[axis][...])
                halves.append(block.reshape(16, 1, 8, DEAL_COLS))
            both = jnp.concatenate(halves, axis=1).reshape(4, 4, 16, DEAL_COLS).astype(BF16)
            start = 0
            for at in chosen:
                _, order, _, width = LATE_PLAN.parts[at]
                for at_z in range(4):
                    for at_x in range(4):
                        spot = tuple((row, at_z, at_x)[one] for one in order)
                        sums.parts[at].tiles[spot] = both[at_z, at_x][:, start : start + width]
                start += width

        sums.each(stream, lambda part: part.ring_start(0))

    def finish(stream):
        if stream not in DEALT.values():
            sums.finish(stream, outs)
            return
        start = [(Y if stream == DEALT[Y] else Z) * FILTERS]

        def end(part):
            part.dealt_end(outs["high"], start[0])
            start[0] += part.width

        sums.each(stream, end)

    def highway(first, last):
        if first == 0:
            late_loads["pooled"].wait()
        for at in range(first, last):
            cols = slice(at * HIGH_ROWS, (at + 1) * HIGH_ROWS)
            high_loads[at].wait()
            weight = high_slots.at[at % HIGH_SLOTS]
            grad = grad_pooled[:, cols]
            grad = grad + back_dot(grad_mixed[:, 0:FILTERS], weight[:, 0:FILTERS])
            grad = grad + back_dot(grad_mixed[:, FILTERS:], weight[:, FILTERS:])
            _, slope = gelu_both(pooled[:, cols])
            grad_pooled[:, cols] = slope * grad
            if at + HIGH_SLOTS < len(high_loads):
                high_loads[at + HIGH_SLOTS].start()

    lane = lax.broadcasted_iota(jnp.int32, (WORDS, 128), 1)

    def conv_start():
        last_grad[...] = jnp.zeros_like(last_grad)
        conv_grad[...] = jnp.zeros_like(conv_grad)
        table_grad[...] = jnp.zeros_like(table_grad)

    def conv_block(step):
        first = CONV_STEP * step
        back = jnp.zeros((CONV_STEP * WORDS, 128), F32)
        for block in range(FILTERS // CONV_COLS):
            cols = slice(block * CONV_COLS, (block + 1) * CONV_COLS)
            share_load(step, block).wait()
            shares = share_slots[block].astype(F32) * grad_pooled[:, cols][None]
            shares = shares.astype(BF16).reshape(CONV_STEP * WORDS, CONV_COLS)

            @pl.when(step + 1 < CONV_STEPS)
            def _():
                share_load(step + 1, block).start()

            conv_grad[:, cols] += dot(turned[step], shares)
            back = back + dot(shares, conv_back[cols, :])
        back = back.reshape(CONV_STEP, WORDS, 128)
        before = last_grad[...]
        last_grad[...] = back[CONV_STEP - TAPS + 1 :]
        high_low, onehots = [], []
        for side in range(CONV_STEP):
            taps = back[side]
            for tap in range(1, TAPS):
                from_tap = back[side - tap] if side >= tap else before[TAPS - 1 + side - tap]
                taps = jnp.where(lane // CHAR_DIM == tap, from_tap, taps)
            taps = jnp.where(lane < BIAS_ROW, taps, 0.0)
            high = taps.astype(BF16)
            low = (taps - high.astype(F32)).astype(BF16)
            high_low.append(jnp.concatenate([high, low], axis=1))
            code = lax.broadcasted_iota(jnp.int32, (CHAR_ROWS, WORDS), 0)
            ids = chars[pl.ds(first + side, 1), :]
            onehots.append(jnp.where(ids == code, 1.0, 0.0).astype(BF16))
        table_grad[0:CHAR_ROWS, :] += dot(
            jnp.concatenate(onehots, axis=1), jnp.concatenate(high_low, axis=0)
        )

    def conv(first, last):
        if first == 0:
            late_loads["turned"].wait()
            late_loads["conv_back"].wait()

        @pl.loop(first, last)
        def _(step):
            conv_block(step)

    conv_copies = []

    def conv_send(number, source, target, device):
        copy = remote(source, target, conv_sems, number, device)
        copy.start()
        conv_copies.append(copy)

    def conv_end():
        for block in range(16):
            turned = conv_grad[:, block * 128 : (block + 1) * 128].T
            conv_rows[block] = turned.reshape(2, 64, 128)
        conv_send(0, conv_rows.at[:, 1 - core], conv_other, partner)
        table = table_grad[:, 0:128] + table_grad[:, 128:256]
        turned = jnp.concatenate(
            [table[128 * block : 128 * (block + 1)].T for block in range(3)], axis=1
        )
        folded = turned[0:CHAR_DIM]
        for tap in range(1, TAPS):
            folded = folded + turned[tap * CHAR_DIM : (tap + 1) * CHAR_DIM]
        char_sums[:, 0:384] = folded
        for block in range(16):
            bias = conv_grad[BIAS_ROW : BIAS_ROW + 1, block * 128 : (block + 1) * 128]
            char_sums[block : block + 1, 384:512] = bias
        shared[1].start(0, char_sums[...])

    def conv_sum(level):
        if level == 0:
            conv_copies[0].wait_recv()

            @pl.loop(0, 4)
            def _(at):
                for inner in range(4):
                    total = conv_rows[at * 4 + inner, core] + conv_other[at * 4 + inner]
                    conv_tiles[at, inner] = total.astype(BF16)

            for step in (1, 2, 3):
                place = around(y, step)
                device = device_of(place, z, core, x)
                conv_send(step, conv_tiles.at[place], conv_y.at[step - 1], device)
            return
        for copy in conv_copies[3 * level - 2 : 3 * level + 1]:
            copy.wait_recv()
        if level == 1:

            @pl.loop(0, 4)
            def _(at):
                total = conv_tiles[y, at].astype(F32) + conv_y[0, at].astype(F32)
                total = total + (conv_y[1, at].astype(F32) + conv_y[2, at].astype(F32))
                conv_tiles[y, at] = total.astype(BF16)

            for step in (1, 2, 3):
                place = around(z, step)
                device = device_of(y, place, core, x)
                conv_send(3 + step, conv_tiles.at[y, place], conv_z.at[step - 1], device)
        elif level == 2:
            total = conv_tiles[y, z].astype(F32) + conv_z[0].astype(F32)
            total = total + (conv_z[1].astype(F32) + conv_z[2].astype(F32))
            conv_last[...] = total.reshape(4, 16, 128)
            for step in (1, 2, 3):
                place = around(x, step)
                device = device_of(y, z, core, place)
                conv_send(6 + step, conv_last.at[place], conv_x.at[step - 1], device)
        else:
            out_conv[...] = (conv_last[x] + conv_x[0]) + (conv_x[1] + conv_x[2])

    def shared_step(level, which):
        if level < 3:
            shared[which].start(level + 1, shared[which].end(level))
        else:
            out_shared[which][...] = shared[which].end(level)

    def tail(level):
        conv_sum(level)
        shared_step(level, 1)

    actions = {
        "prepare": prepare,
        "gates": gates,
        "highway": highway,
        "multiply": multiply,
        "relay1": sums.relay1,
        "end1": sums.end1,
        "relay2": sums.relay2,
        "end2": sums.end2,
        "finish": finish,
        "pass_all": pass_all,
        "multiply_high": multiply_high,
        "conv_start": conv_start,
        "conv": conv,
        "conv_end": conv_end,
        "greet": greet,
        "tail": tail,
        "small": lambda: shared[0].start(0, small[...]),
        "shared": shared_step,
    }
    for name, *given in schedule:
        actions[name](*given)

    sums.sent()
    for one in shared:
        one.sent()
    for copy in (*deals.values(), *passes.values(), *conv_copies):
        copy.wait_send()


LATE_SCHEDULE = (
    ("conv_start",),
    ("prepare",),
    ("greet",),
    ("gates",),
    ("multiply", 0),
    ("highway", 0, 3),
    ("multiply", 1),
    ("highway", 3, 8),
    ("pass_all",),
    ("multiply_high", 0),
    ("multiply_high", 1),
    ("relay1", 0),
    ("conv", 0, 2),
    ("relay1", 1),
    ("end1", 0),
    ("relay1", 2),
    ("relay1", 3),
    ("conv", 2, 5),
    ("conv_end",),
    ("small",),
    ("end1", 1),
    ("relay2", 0),
    ("end1", 2),
    ("end1", 3),
    ("tail", 0),
    ("shared", 0, 0),
    ("relay2", 1),
    ("end2", 0),
    ("relay2", 2),
    ("relay2", 3),
    ("tail", 1),
    ("shared", 1, 0),
    ("end2", 1),
    ("finish", 0),
    ("end2", 2),
    ("end2", 3),
    ("tail", 2),
    ("shared", 2, 0),
    ("finish", 1),
    ("finish", 2),
    ("finish", 3),
    ("tail", 3),
    ("shared", 3, 0),
)


def late_sums(vmem_in, late, right, high_weight, proj_weight, shares, rings):
    dma = pltpu.SemaphoreType.DMA
    scratch = LATE_PLAN.scratch()
    for shape in SHARED:
        scratch += [pltpu.VMEM((2,) + shape, F32), pltpu.VMEM((3, 4) + shape, F32)]
    scratch += [
        dma((2, len(SHARED), 10)),
        dma((5,)),
        dma((FILTERS // HIGH_ROWS,)),
        pltpu.VMEM((128, FILTERS), F32),
        pltpu.VMEM((16, 2, 64, 128), F32),
        pltpu.VMEM((16, 64, 128), F32),
        dma((2, 10)),
        pltpu.VMEM((4, 4, 64, 128), BF16),
        pltpu.VMEM((3, 4, 64, 128), BF16),
        pltpu.VMEM((3, 64, 128), BF16),
        pltpu.VMEM((4, 16, 128), F32),
        pltpu.VMEM((3, 16, 128), F32),
        pltpu.VMEM(SHARED[1], F32),
        pltpu.VMEM((TAPS - 1, WORDS, 128), F32),
        pltpu.VMEM((384, 256), F32),
        pltpu.VMEM((HIGH_SLOTS, HIGH_ROWS, 2 * FILTERS), BF16),
        pltpu.VMEM((FILTERS, D), BF16),
        pltpu.VMEM((WORDS, FILTERS), F32),
        pltpu.VMEM(SHARED[0], F32),
        pltpu.VMEM((WORDS, 2 * FILTERS), BF16),
        dma((2,)),
        dma((2, 2, 4)),
        dma((2, 2, 4)),
        pltpu.VMEM((WORDS, 2 * FILTERS), F32),
        pltpu.VMEM((WORDS, FILTERS), F32),
        pltpu.VMEM(TURNED_SHAPE, BF16),
        pltpu.VMEM((FILTERS, 128), BF16),
        dma((4,)),
        pltpu.VMEM(SHARES_SHAPE[1:], BF16),
        dma((FILTERS // CONV_COLS,)),
        pltpu.VMEM((2, 4, 128, RING_WORDS), BF16),
        pltpu.VMEM((2, 4, 128, RING_WORDS), BF16),
        pltpu.VMEM((RING_WORDS, DEAL_COLS), BF16),
        pltpu.VMEM((RING_WORDS, DEAL_COLS), BF16),
    ]
    whole = pl.BlockSpec(memory_space=pltpu.VMEM)
    outside = pl.BlockSpec(memory_space=pl.ANY)
    names = ("high", "proj", "qkv", "out", "up")
    shapes = [(CHUNK_ROWS[name], RIGHT_COLS[name]) for name in names]
    shapes += [(16, 128)] + list(SHARED)
    return pl.pallas_call(
        functools.partial(late_kernel, LATE_SCHEDULE),
        out_shape=tuple(jax.ShapeDtypeStruct(shape, F32) for shape in shapes),
        in_specs=[whole] * len(vmem_in) + [outside] * 13,
        out_specs=tuple(whole for _ in shapes),
        scratch_shapes=scratch,
        compiler_params=pltpu.CompilerParams(
            collective_id=1, has_side_effects=True, vmem_limit_bytes=64 << 20
        ),
    )(*vmem_in, *late, *right, high_weight, proj_weight, shares, *rings)


def results_kernel(*refs):
    hidden, high, proj, qkv, out, up, down, conv, small, chars = refs[:10]
    (
        to_hidden,
        to_table,
        to_conv,
        to_conv_bias,
        to_high,
        to_high_bias,
        to_proj,
        to_gain,
        to_shift,
        to_qkv,
        to_out,
        to_up,
        to_down,
    ) = refs[10:]
    to_hidden[0] = hidden[...]
    to_high[0] = high[...]
    for source, target in ((proj, to_proj), (qkv, to_qkv), (out, to_out), (up, to_up), (down, to_down)):
        target[...] = source[...]
    to_gain[...] = small[0:3, :]
    to_shift[...] = small[3:6, :]
    for line in range(0, 2 * FILTERS, D):
        used = min(D, 2 * FILTERS - line)
        to_high_bias[:, line : line + used] = small[6 + line // D : 7 + line // D, 0:used]
    to_table[...] = chars[:, 0:CHARS]
    for block in range(16):
        to_conv_bias[:, block * 128 : (block + 1) * 128] = chars[block : block + 1, 384:512]
    me = lax.axis_index("dp") * 4 + lax.axis_index("ctx")
    filters = me * 16 + lax.broadcasted_iota(jnp.int32, (16, BIAS_ROW), 0)
    widths = jnp.ones((16, BIAS_ROW), jnp.int32)
    for bound in (1, 2, 4, 8, 16, 32):
        widths = widths + (filters >= FILTERS // 64 * bound).astype(jnp.int32)
    taps = lax.broadcasted_iota(jnp.int32, (16, BIAS_ROW), 1) // CHAR_DIM
    to_conv[...] = jnp.where(taps < widths, conv[:, 0:BIAS_ROW], 0.0)


def results(*arrays):
    shapes = [
        ((1, WORDS, D), BF16),
        ((CHAR_DIM, CHARS), F32),
        ((16, BIAS_ROW), F32),
        ((1, FILTERS), F32),
        ((1, 16, 2 * FILTERS), F32),
        ((1, 2 * FILTERS), F32),
        ((16, D), F32),
        ((3, D), F32),
        ((3, D), F32),
        ((6, 3 * D), F32),
        ((6, D), F32),
        ((6, FF), F32),
        ((24, D), F32),
    ]
    whole = pl.BlockSpec(memory_space=pltpu.VMEM)
    return pl.pallas_call(
        results_kernel,
        out_shape=tuple(jax.ShapeDtypeStruct(*shape) for shape in shapes),
        in_specs=[whole] * len(arrays),
        out_specs=tuple(whole for _ in shapes),
    )(*arrays)


def body(
    char_ids,
    word_lengths,
    word_home,
    seq_lengths,
    char_table,
    conv_weight,
    conv_bias,
    highway_weight,
    highway_bias,
    proj_weight,
    norm_gain,
    norm_shift,
    qkv_weight,
    out_weight,
    up_weight,
    down_weight,
    cotangent,
):
    act, chars, final_rows, embedded, pooled, unfolded, conv_w, mixed = embed_words(
        char_ids.T,
        word_lengths[None, :],
        word_home[None, :],
        char_table.T,
        conv_weight,
        conv_bias,
        highway_weight,
        highway_bias,
        proj_weight,
    )
    (
        out_hidden,
        first_norm,
        context,
        grad_joint,
        grad_attn,
        grad_embedded,
        middle,
        grad_up,
        norms,
        grad_down_weight,
        ring_y,
        ring_z,
        shares,
        turned,
        conv_back,
    ) = encode(
        embedded,
        act,
        seq_lengths[None, :],
        norm_gain,
        norm_shift,
        cotangent.reshape(WORDS, D),
        (qkv_weight, out_weight, up_weight, down_weight),
        (unfolded, conv_w, pooled),
    )
    high, proj, qkv, out, grad_up_weight, conv, small, char_sums = late_sums(
        (
            act,
            final_rows,
            first_norm,
            context,
            middle,
            chars,
            norms,
        ),
        (mixed, pooled, turned, conv_back),
        (grad_embedded, grad_joint, grad_attn, grad_up),
        highway_weight,
        proj_weight,
        shares,
        (ring_y, ring_z),
    )
    outs = list(
        results(
            out_hidden,
            high,
            proj,
            qkv,
            out,
            grad_up_weight,
            grad_down_weight,
            conv,
            small,
            char_sums,
        )
    )
    outs[1], outs[2] = outs[1].T, outs[2].T
    outs[3] = outs[3].reshape(-1)
    return tuple(outs)


def solution(mesh):
    placed = (
        P(("dp", "ctx"), None),
        P(("dp", "ctx")),
        P(("dp", "ctx")),
        P("dp"),
        P(),
        P(),
        P(),
        P(),
        P(),
        P(),
        P(),
        P(),
        P(),
        P(),
        P(),
        P(),
        P("dp", "ctx", None),
    )
    return jax.shard_map(
        body,
        mesh=mesh,
        in_specs=placed,
        out_specs=(
            P("dp", "ctx", None),
            P(),
            P(None, ("dp", "ctx")),
            P(),
            P(None, ("dp", "ctx"), None),
            P(),
            P(("dp", "ctx"), None),
            P(),
            P(),
            P(("dp", "ctx"), None),
            P(("dp", "ctx"), None),
            P(("dp", "ctx"), None),
            P(("dp", "ctx"), None),
        ),
        check_vma=False,
    )
```
